32 devices in a mesh: tm: 8 (over z, y), chan: 4 (over x, core).
Axes of the slice: x: 2, y: 2, z: 4, core: 2. Of those that a mesh axis runs over, the one named last changes fastest.
Arguments:
- series: bfloat16 [2048, 512], P('tm', 'chan'), may hold values from -6 to 6
- proj_weight: bfloat16 [512, 3, 512], P(None, None, 'chan'), may hold values from -0.25 to 0.25
- proj_bias: float32 [3, 512], P(None, 'chan'), may hold values from -6 to 6
- short_taps: float32 [3, 3, 512], P(None, None, 'chan'), may hold values from -6 to 6
- short_bias: float32 [3, 512], P(None, 'chan'), may hold values from -6 to 6
- spectrum: float32 [2, 8, 2, 256, 512], P(None, 'tm', None, None, 'chan'), may hold values from -6 to 6
- skip_gain: float32 [512], P('chan'), may hold values from -6 to 6
- out_weight: bfloat16 [512, 512], replicated, may hold values from -0.25 to 0.25
- out_bias: float32 [512], P('chan'), may hold values from -6 to 6
Outputs:
- mixed_out: bfloat16 [2048, 512], P('tm', 'chan')
The draws below stay inside these ranges and needn't reach their ends.
All inputs are finite; a program needn't handle non-finite values.
Results may differ from the reference program's by a relative error of at most 0.009.
Values may be sent and summed in bfloat16 or wider, within the bound.
A program may use at most 64 MiB of HBM per device.

```python
import jax
import jax.numpy as jnp
from jax import lax

D = 512
TM_DEV = 256
KS = 3
L = 2048
FFT = 4096
N_TM = 8


def block_scale(rng, shape, pieces, smallest, high):
    gain, own = 1.0, jax.random.fold_in(rng, 6)
    for position, parts in pieces:
        heights = jnp.exp(jax.random.uniform(jax.random.fold_in(own, position), (parts,), jnp.float32, smallest / len(pieces), high / len(pieces)))
        gain = gain * jnp.repeat(heights, shape[position] // parts).reshape([-1 if axis == position else 1 for axis in range(len(shape))])
    return gain


def noise(key, dims, scale, bound, pieces=(), held_as=jnp.bfloat16):
    array = jax.random.normal(key, dims, jnp.float32) * scale
    if len(pieces) > 0:
        array = block_scale(key, dims, pieces, -0.22, 0.18) * array
    return jnp.clip(array, min=-bound, max=bound).astype(held_as)


def setup_inputs(seed: int = 0) -> dict:
    key_of = jax.random.split(jax.random.key(seed), 10)
    series = noise(key_of[0], (L, D), 1.0, 6.0, ((0, 8), (1, 4)))
    proj_weight = noise(key_of[1], (D, 3, D), D ** -0.5, 0.25, ((2, 4),))
    proj_bias = noise(key_of[2], (3, D), 1.0, 6.0, ((1, 4),), jnp.float32)
    short_taps = noise(key_of[3], (KS, 3, D), 0.6, 6.0, ((2, 4),), jnp.float32)
    short_bias = noise(key_of[4], (3, D), 0.5, 6.0, ((1, 4),), jnp.float32)
    spectrum = noise(key_of[5], (2, N_TM, 2, TM_DEV, D), 1.2, 6.0, ((1, 8), (4, 4)), jnp.float32)
    skip_gain = noise(key_of[6], (D,), 1.0, 6.0, ((0, 4),), jnp.float32)
    out_weight = noise(key_of[7], (D, D), D ** -0.5, 0.25)
    out_bias = noise(key_of[8], (D,), 1.0, 6.0, ((0, 4),), jnp.float32)
    return dict(series=series, proj_weight=proj_weight, proj_bias=proj_bias, short_taps=short_taps, short_bias=short_bias, spectrum=spectrum, skip_gain=skip_gain, out_weight=out_weight, out_bias=out_bias)


def reverse_bits(values, digits):
    result = jnp.zeros_like(values)
    for bit_level in range(digits):
        result = result | (((values >> bit_level) & 1) << (digits - 1 - bit_level))
    return result


def reference(series, proj_weight, proj_bias, short_taps, short_bias, spectrum, skip_gain, out_weight, out_bias):
    length = series.shape[0]
    projected = jnp.dot(series, proj_weight.reshape(D, 3 * D), preferred_element_type=jnp.float32).reshape(length, 3, D)
    projected = lax.optimization_barrier((projected + proj_bias).astype(jnp.bfloat16)).astype(jnp.float32)
    padded = jnp.pad(projected, ((KS - 1, 0), (0, 0), (0, 0)))
    streams = short_bias + short_taps[0] * padded[KS - 1:]
    for offset in range(1, KS):
        streams = streams + short_taps[offset] * padded[KS - 1 - offset:KS - 1 - offset + length]
    streams = lax.optimization_barrier(streams.astype(jnp.bfloat16)).astype(jnp.float32)
    gate_out = streams[:, 0]
    mixed_in = lax.optimization_barrier((streams[:, 1] * streams[:, 2]).astype(jnp.bfloat16)).astype(jnp.float32)
    tm_count = N_TM
    digits = tm_count.bit_length() - 1
    spectral_rows = jnp.arange(2 * tm_count, dtype=jnp.int32)
    owner_row = reverse_bits(spectral_rows // 2, digits)
    parity = spectral_rows % 2
    ordered = spectrum[:, owner_row, parity]
    natural = ordered.transpose(0, 2, 1, 3).reshape(2, FFT, D)
    groups = D // 64
    signal_blocks = mixed_in.reshape(length, groups, 64).transpose(1, 0, 2)
    filter_blocks = natural.reshape(2, FFT, groups, 64).transpose(2, 0, 1, 3)

    def convolve(operands):
        signal, response = operands
        padded_sig = jnp.concatenate([signal, jnp.zeros_like(signal)], 0)
        spectral = jnp.fft.fft(padded_sig, axis=0)
        product = (response[0] + 1j * response[1]) * spectral
        return jnp.real(jnp.fft.ifft(product, axis=0))[:length]

    convolved = lax.map(convolve, (signal_blocks, filter_blocks)).transpose(1, 0, 2).reshape(length, D)
    gated_rows = ((convolved + skip_gain * mixed_in) * gate_out).astype(jnp.bfloat16)
    mixed_out = jnp.dot(gated_rows, out_weight, preferred_element_type=jnp.float32) + out_bias
    return mixed_out.astype(jnp.bfloat16)
```

```python
import functools
import math

import jax
import jax.numpy as jnp
import numpy as np
from jax import lax
from jax.experimental import pallas as pl
from jax.experimental.pallas import tpu as pltpu
from jax.sharding import PartitionSpec as P

MESH = pl.DeviceIdType.MESH


def from_behind(array, axis, by):
    length = lax.axis_size(axis)
    pairs = [(i, i + by) for i in range(length) if 0 <= i + by < length]
    return lax.ppermute(array, axis, pairs)


def partner_2(block, axis, bit):
    count = lax.axis_size(axis)
    route = []
    for low in range(count):
        high = low | 1 << bit
        if high != low and high < count:
            route += [(low, high), (high, low)]
    return lax.ppermute(block, axis, route)


def reverse_bits(values, digits):
    result = jnp.zeros_like(values)
    for bit_level in range(digits):
        result = result | (values >> bit_level & 1) << digits - 1 - bit_level
    return result


def turning(numer, denom):
    angle = numer.astype(jnp.float32) * (-2.0 * math.pi / denom)
    return (jnp.cos(angle), jnp.sin(angle))


def complex_times(stacked, real_part, imag_part):
    return jnp.stack(
        [
            stacked[0] * real_part - stacked[1] * imag_part,
            stacked[0] * imag_part + stacked[1] * real_part,
        ]
    )


def dft_rows(signals, period, inverse):
    indices = jnp.arange(period, dtype=jnp.int32)
    cosine, sine_part = turning(indices[:, None] * indices[None, :] % period, period)
    if inverse:
        sine_part = -sine_part
    stacked = jnp.concatenate([cosine, sine_part], 0)
    result = jnp.einsum("bt,retc->rebc", stacked, signals, precision=lax.Precision.HIGHEST)
    real_out = result[0, :, :period] - result[1, :, period:]
    imag_out = result[1, :, :period] + result[0, :, period:]
    return jnp.stack([real_out, imag_out])


def shards(
    series,
    proj_weight,
    proj_bias,
    short_taps,
    short_bias,
    spectrum,
    skip_gain,
    out_weight,
    out_bias,
):
    steps_dev = series.shape[0]
    model_width = proj_weight.shape[0]
    channels = proj_weight.shape[2]
    flat_weight = proj_weight.reshape(model_width, 3 * channels)
    weight_rows = flat_weight
    projected = jnp.dot(
        lax.all_gather(series, "chan", axis=1, tiled=True),
        weight_rows,
        preferred_element_type=jnp.float32,
    )
    projected = (projected.reshape(steps_dev, 3, channels) + proj_bias).astype(jnp.bfloat16)
    taps_count = short_taps.shape[0]
    earlier = from_behind(projected[steps_dev - taps_count + 1 :], "tm", 1)
    extended = jnp.concatenate([earlier, projected], 0).astype(jnp.float32)
    streams = short_bias + short_taps[0] * extended[taps_count - 1 :]
    for offset in range(1, taps_count):
        streams = (
            streams
            + short_taps[offset]
            * extended[taps_count - 1 - offset : taps_count - 1 - offset + steps_dev]
        )
    streams = lax.optimization_barrier(streams.astype(jnp.bfloat16)).astype(jnp.float32)
    gate_out = streams[:, 0]
    mixed_in = lax.optimization_barrier((streams[:, 1] * streams[:, 2]).astype(jnp.bfloat16))
    signal = mixed_in.astype(jnp.float32)
    tm_count = lax.axis_size("tm")
    digits = tm_count.bit_length() - 1
    own_index = lax.axis_index("tm")
    period = 2 * tm_count * steps_dev
    positions = jnp.arange(steps_dev, dtype=jnp.int32)
    own_rows = 2 * reverse_bits(own_index, digits) + jnp.arange(2, dtype=jnp.int32)
    twist_cos, twist_sin = turning(own_rows[:, None] * positions[None, :] % period, period)
    twist_cos, twist_sin = (twist_cos[:, :, None], twist_sin[:, :, None])
    half_cos, half_sin = turning(own_index, 2 * tm_count)
    zero_field = jnp.zeros_like(signal)
    current = jnp.stack(
        [jnp.stack([signal, signal * half_cos]), jnp.stack([zero_field, signal * half_sin])]
    )
    for bit_level in reversed(range(digits)):
        partner = partner_2(current, "tm", bit_level)
        half_span = 1 << bit_level
        rot_cos, rot_sin = turning(own_index % half_span, 2 * half_span)
        upper_half = own_index >> bit_level & 1 == 1
        current = jnp.where(
            upper_half, complex_times(partner - current, rot_cos, rot_sin), current + partner
        )
    twisted = complex_times(current, twist_cos, twist_sin)
    spectral = dft_rows(twisted, steps_dev, False)
    response = spectrum.reshape(2, 2, steps_dev, channels)
    product = complex_times(spectral, response[0], response[1])
    returned = dft_rows(product, steps_dev, True)
    current = complex_times(returned, twist_cos, -twist_sin)
    for bit_level in range(digits):
        partner = partner_2(current, "tm", bit_level)
        half_span = 1 << bit_level
        rot_cos, rot_sin = turning(own_index % half_span, 2 * half_span)
        rot_sin = -rot_sin
        upper_half = own_index >> bit_level & 1 == 1
        current = jnp.where(
            upper_half,
            partner - complex_times(current, rot_cos, rot_sin),
            current + complex_times(partner, rot_cos, rot_sin),
        )
    convolved = current[0, 0] + half_cos * current[0, 1] + half_sin * current[1, 1]
    convolved = convolved * (1.0 / period)
    gated_rows = ((convolved + skip_gain * signal) * gate_out).astype(jnp.bfloat16)
    column_start = lax.axis_index("chan") * channels
    weight_rows = lax.dynamic_slice_in_dim(out_weight, column_start, channels, 0)
    partial_value = jnp.dot(gated_rows, weight_rows, preferred_element_type=jnp.float32)
    mixed_out = lax.psum_scatter(partial_value, "chan", scatter_dimension=1, tiled=True)
    return (mixed_out + out_bias).astype(jnp.bfloat16)


def make_tables(tm_count, steps):
    count, period = 2 * tm_count, 2 * tm_count * steps
    rows = np.arange(steps)
    angle = 2.0 * np.pi * (rows[:, None] * rows[None, :] % steps) / steps
    dft = np.stack([np.cos(angle), np.sin(angle)]).astype(jnp.bfloat16)
    angle = 2.0 * np.pi * (np.arange(count)[:, None] * rows[None, :] % period) / period
    twist = np.stack([np.cos(angle), np.sin(angle)]).astype(np.float32)
    return dft, twist


def flip(value, digits):
    result = 0
    for bit_level in range(digits):
        result |= (value >> bit_level & 1) << digits - 1 - bit_level
    return result


def weighted(blocks, weights):
    total = None
    for block, weight in zip(blocks, weights):
        if abs(weight) < 1e-12:
            continue
        if abs(weight - 1.0) < 1e-12:
            term = block
        elif abs(weight + 1.0) < 1e-12:
            term = -block
        else:
            term = block * float(weight)
        total = term if total is None else total + term
    return total


def kernel(
    tm_count,
    chan_count,
    series,
    weight,
    proj_bias,
    taps,
    short_bias,
    spectrum,
    skip_gain,
    out_weight,
    out_bias,
    dft,
    twist,
    out,
    rows_in,
    weight_v,
    proj_bias_v,
    taps_v,
    short_bias_v,
    spectrum_v,
    skip_v,
    out_weight_v,
    out_bias_v,
    dft_v,
    twist_v,
    projected,
    spec_out,
    spec_in,
    mixed_out,
    mixed_in,
    wave,
    conv_out,
    conv_in,
    gated,
    local_sem,
    rows_send,
    rows_recv,
    halo_send,
    halo_recv,
    spec_send,
    spec_recv,
    mix_send,
    mix_recv,
    conv_send,
    conv_recv,
    gate_send,
    gate_recv,
):
    steps, channels = series.shape
    halo = rows_in.shape[0] - steps
    share = channels // tm_count
    digits = tm_count.bit_length() - 1
    slots = 2 * tm_count
    own_t, own_c = lax.axis_index("tm"), lax.axis_index("chan")
    columns = lambda c: pl.ds(pl.multiple_of(c * channels, channels), channels)
    tm_peer = lambda by: lax.rem(own_t + by, tm_count)
    chan_peer = lambda by: lax.rem(own_c + by, chan_count)

    barrier = pltpu.get_barrier_semaphore()
    greet = lambda where: pl.semaphore_signal(barrier, inc=1, device_id=where, device_id_type=MESH)
    for by in range(1, chan_count):
        greet({"chan": chan_peer(by)})
    for by in range(1, tm_count):
        greet({"tm": tm_peer(by)})
    for by in range(1, chan_count):
        greet({"tm": tm_peer(1), "chan": chan_peer(by)})
        greet({"tm": tm_peer(tm_count - 1), "chan": chan_peer(by)})

    pairs = [
        (spectrum.at[:, 0], spectrum_v),
        (series, rows_in.at[pl.ds(halo, steps), columns(own_c)]),
        (weight, weight_v),
        (proj_bias, proj_bias_v),
        (taps, taps_v),
        (short_bias, short_bias_v),
        (dft, dft_v),
        (twist, twist_v),
        (skip_gain, skip_v),
        (out_weight.at[:, columns(own_c)], out_weight_v),
        (out_bias, out_bias_v),
    ]
    local = [pltpu.make_async_copy(a, b, local_sem.at[i]) for i, (a, b) in enumerate(pairs)]
    for copy in local:
        copy.start()
    pl.semaphore_wait(barrier, chan_count - 1 + tm_count - 1 + 2 * (chan_count - 1))

    def remote(src, dst, send, recv, where):
        return pltpu.make_async_remote_copy(
            src_ref=src, dst_ref=dst, send_sem=send, recv_sem=recv, device_id=where, device_id_type=MESH
        )

    def rows_copy(by, owner):
        return remote(
            series,
            rows_in.at[pl.ds(halo, steps), columns(owner)],
            rows_send.at[by],
            rows_recv.at[by],
            {"chan": chan_peer(by)},
        )

    def halo_copy(by, owner):
        return remote(
            series.at[pl.ds(steps - halo, halo)],
            rows_in.at[pl.ds(0, halo), columns(owner)],
            halo_send.at[by],
            halo_recv.at[by],
            {"tm": tm_peer(1), "chan": chan_peer(by)},
        )

    for by in range(1, chan_count):
        rows_copy(by, own_c).start()

    @pl.when(own_t < tm_count - 1)
    def _():
        for by in range(chan_count):
            halo_copy(by, own_c).start()

    @pl.when(own_t == 0)
    def _():
        rows_in[pl.ds(0, halo), :] = jnp.zeros((halo, rows_in.shape[1]), rows_in.dtype)

    local[0].wait()
    for part in range(2):
        for parity in range(2):
            block = spectrum_v[part, parity].T * (1.0 / (slots * steps))
            spec_out[:, part, parity] = block.astype(jnp.bfloat16).reshape(tm_count, share, steps)

    def to_peer(src, dst, send, recv, by):
        return remote(src.at[tm_peer(by)], dst.at[own_t], send.at[by], recv.at[by], {"tm": tm_peer(by)})

    def spread(src, dst, send, recv):
        for by in range(1, tm_count):
            to_peer(src, dst, send, recv, by).start()
        dst[own_t] = src[own_t]

    def collect(src, dst, send, recv):
        for by in range(1, tm_count):
            copy = remote(
                src.at[0], dst.at[tm_peer(tm_count - by)], send.at[by], recv.at[by], {"tm": tm_peer(by)}
            )
            copy.wait_recv()

    spread(spec_out, spec_in, spec_send, spec_recv)

    for copy in local[1:]:
        copy.wait()
    for by in range(1, chan_count):
        rows_copy(by, chan_peer(chan_count - by)).wait_recv()

    @pl.when(own_t > 0)
    def _():
        for by in range(chan_count):
            halo_copy(by, chan_peer(chan_count - by)).wait_recv()

    streams = []
    for j in (1, 2, 0):
        lanes = pl.ds(j * channels, channels)
        value = jnp.dot(rows_in[...], weight_v[:, lanes], preferred_element_type=jnp.float32)
        value = (value + proj_bias_v[j : j + 1]).astype(jnp.bfloat16).astype(jnp.float32)
        projected[j] = value

        @pl.when(own_t == 0)
        def _():
            projected[j, pl.ds(0, halo)] = jnp.zeros((halo, channels), jnp.float32)

        stream = short_bias_v[j : j + 1] + taps_v[0, j : j + 1] * projected[j, pl.ds(halo, steps)]
        for k in range(1, taps.shape[0]):
            stream = stream + taps_v[k, j : j + 1] * projected[j, pl.ds(halo - k, steps)]
        stream = stream.astype(jnp.bfloat16).astype(jnp.float32)
        if j == 2:
            signal = (streams[0] * stream).astype(jnp.bfloat16).astype(jnp.float32)
            mixed_out[...] = signal.T.astype(jnp.bfloat16).reshape(tm_count, share, steps)
            spread(mixed_out, mixed_in, mix_send, mix_recv)
        streams.append(stream)
    gate = streams[2]
    projected[0, pl.ds(0, steps)] = gate
    projected[1, pl.ds(0, steps)] = signal

    collect(mixed_out, mixed_in, mix_send, mix_recv)
    blocks = [mixed_in[b].astype(jnp.float32) for b in range(tm_count)]
    turns = 2.0 * np.pi * np.arange(slots) / slots
    cosine = lambda r, b: math.cos(turns[r * b % slots])
    sine = lambda r, b: math.sin(turns[r * b % slots])
    slot_of = {2 * flip(s // 2, digits) + s % 2: s for s in range(slots)}

    for r in range(tm_count + 1):
        real = weighted(blocks, [cosine(r, b) for b in range(tm_count)])
        imag = weighted(blocks, [-sine(r, b) for b in range(tm_count)])
        for to, sign in ((r, 1.0), (slots - r, -1.0)):
            if to == slots or (sign < 0 and to == r):
                continue
            cos_row, sin_row = twist_v[0, to : to + 1], twist_v[1, to : to + 1]
            if imag is None:
                turned = (real * cos_row, -(real * sin_row))
            else:
                turned = (
                    real * cos_row + sign * (imag * sin_row),
                    sign * (imag * cos_row) - real * sin_row,
                )
            for part in range(2):
                wave[part, slot_of[to]] = turned[part].astype(jnp.bfloat16)

    def within():
        rows = wave[...].reshape(2 * slots * share, steps)
        first = jnp.dot(rows, dft_v[0], preferred_element_type=jnp.float32)
        second = jnp.dot(rows, dft_v[1], preferred_element_type=jnp.float32)
        half = slots * share
        return first[:half], first[half:], second[:half], second[half:]

    real_cos, imag_cos, real_sin, imag_sin = within()
    real, imag = real_cos + imag_sin, imag_cos - real_sin
    collect(spec_out, spec_in, spec_send, spec_recv)
    filter_real = spec_in[:, 0].reshape(slots * share, steps).astype(jnp.float32)
    filter_imag = spec_in[:, 1].reshape(slots * share, steps).astype(jnp.float32)
    shape = (slots, share, steps)
    wave[0] = (real * filter_real - imag * filter_imag).astype(jnp.bfloat16).reshape(shape)
    wave[1] = (real * filter_imag + imag * filter_real).astype(jnp.bfloat16).reshape(shape)
    real_cos, imag_cos, real_sin, imag_sin = within()
    real, imag = (real_cos - imag_sin).reshape(shape), (real_sin + imag_cos).reshape(shape)

    evens, odds = [], []
    for r in range(tm_count + 1):
        even = odd = None
        for to, sign in ((r, 1.0), (slots - r, -1.0)):
            if to == slots or (sign < 0 and to == r):
                continue
            s = slot_of[to]
            cos_row, sin_row = twist_v[0, to : to + 1], twist_v[1, to : to + 1]
            turned = real[s] * cos_row - imag[s] * sin_row
            even = turned if even is None else even + turned
            turned = real[s] * sin_row + imag[s] * cos_row
            odd = turned if odd is None else odd - turned
        evens.append(even)
        odds.append(odd)
    for b in range(tm_count):
        weights = [cosine(r, b) for r in range(tm_count + 1)] + [-sine(r, b) for r in range(tm_count + 1)]
        conv_out[b] = weighted(evens + odds, weights).astype(jnp.bfloat16)
    spread(conv_out, conv_in, conv_send, conv_recv)
    collect(conv_out, conv_in, conv_send, conv_recv)

    convolved = conv_in[...].reshape(channels, steps).astype(jnp.float32).T
    value = (convolved + skip_v[...] * projected[1, pl.ds(0, steps)]) * projected[0, pl.ds(0, steps)]
    gated[:, columns(own_c)] = value.astype(jnp.bfloat16)

    def gate_copy(by, owner):
        return remote(
            gated.at[:, columns(owner)],
            gated.at[:, columns(owner)],
            gate_send.at[by],
            gate_recv.at[by],
            {"chan": chan_peer(by)},
        )

    for by in range(1, chan_count):
        gate_copy(by, own_c).start()
    for by in range(1, chan_count):
        gate_copy(by, chan_peer(chan_count - by)).wait_recv()
    value = jnp.dot(gated[...], out_weight_v[...], preferred_element_type=jnp.float32)
    out[...] = (value + out_bias_v[...]).astype(out.dtype)

    for by in range(1, chan_count):
        rows_copy(by, own_c).wait_send()
        gate_copy(by, own_c).wait_send()

    @pl.when(own_t < tm_count - 1)
    def _():
        for by in range(chan_count):
            halo_copy(by, own_c).wait_send()

    for by in range(1, tm_count):
        to_peer(spec_out, spec_in, spec_send, spec_recv, by).wait_send()
        to_peer(mixed_out, mixed_in, mix_send, mix_recv, by).wait_send()
        to_peer(conv_out, conv_in, conv_send, conv_recv, by).wait_send()


def fused(
    series,
    proj_weight,
    proj_bias,
    short_taps,
    short_bias,
    spectrum,
    skip_gain,
    out_weight,
    out_bias,
):
    steps, channels = series.shape
    width = proj_weight.shape[0]
    tm_count, chan_count = lax.axis_size("tm"), lax.axis_size("chan")
    dft, twist = make_tables(tm_count, steps)
    share, slots, halo = channels // tm_count, 2 * tm_count, 16
    spread_shape = (tm_count, share, steps)
    vmem, dma = pltpu.VMEM, pltpu.SemaphoreType.DMA
    operands = [
        series,
        proj_weight.reshape(width, 3 * channels),
        proj_bias,
        short_taps,
        short_bias,
        spectrum,
        skip_gain.reshape(1, channels),
        out_weight,
        out_bias.reshape(1, channels),
        jnp.asarray(dft),
        jnp.asarray(twist),
    ]
    tm_sems = [dma((tm_count,)), dma((tm_count,))]
    chan_sems = [dma((chan_count,)), dma((chan_count,))]
    return pl.pallas_call(
        functools.partial(kernel, tm_count, chan_count),
        out_shape=jax.ShapeDtypeStruct((steps, channels), jnp.bfloat16),
        in_specs=[pl.BlockSpec(memory_space=pl.ANY)] * len(operands),
        out_specs=pl.BlockSpec(memory_space=pltpu.VMEM),
        scratch_shapes=[
            vmem((halo + steps, width), jnp.bfloat16),
            vmem((width, 3 * channels), jnp.bfloat16),
            vmem(proj_bias.shape, jnp.float32),
            vmem(short_taps.shape, jnp.float32),
            vmem(short_bias.shape, jnp.float32),
            vmem((2, 2, steps, channels), jnp.float32),
            vmem((1, channels), jnp.float32),
            vmem((width, channels), jnp.bfloat16),
            vmem((1, channels), jnp.float32),
            vmem(dft.shape, jnp.bfloat16),
            vmem(twist.shape, jnp.float32),
            vmem((3, halo + steps, channels), jnp.float32),
            vmem((tm_count, 2, 2, share, steps), jnp.bfloat16),
            vmem((tm_count, 2, 2, share, steps), jnp.bfloat16),
            vmem(spread_shape, jnp.bfloat16),
            vmem(spread_shape, jnp.bfloat16),
            vmem((2, slots, share, steps), jnp.bfloat16),
            vmem(spread_shape, jnp.bfloat16),
            vmem(spread_shape, jnp.bfloat16),
            vmem((steps, width), jnp.bfloat16),
            dma((len(operands),)),
            *chan_sems,
            *chan_sems,
            *tm_sems,
            *tm_sems,
            *tm_sems,
            *chan_sems,
        ],
        compiler_params=pltpu.CompilerParams(
            collective_id=0, has_side_effects=True, vmem_limit_bytes=32 * 1024 * 1024
        ),
    )(*operands)


def solution(mesh):
    sizes = mesh.shape

    def program(*arrays):
        share = arrays[0].shape[1] // sizes["chan"] // sizes["tm"]
        wide = share > 0 and share % 16 == 0 and sizes["tm"] >= 4
        return jax.shard_map(
            fused if wide else shards,
            mesh=mesh,
            in_specs=(
                P("tm", "chan"),
                P(None, None, "chan"),
                P(None, "chan"),
                P(None, None, "chan"),
                P(None, "chan"),
                P(None, "tm", None, None, "chan"),
                P("chan"),
                P(),
                P("chan"),
            ),
            out_specs=P("tm", "chan"),
            check_vma=False,
        )(*arrays)

    return program
```

```python
import functools
import math

import jax
import jax.numpy as jnp
import numpy as np
from jax import lax
from jax.experimental import pallas as pl
from jax.experimental.pallas import tpu as pltpu
from jax.sharding import PartitionSpec as P

MESH = pl.DeviceIdType.MESH


def from_behind(array, axis, by):
    length = lax.axis_size(axis)
    pairs = [(i, i + by) for i in range(length) if 0 <= i + by < length]
    return lax.ppermute(array, axis, pairs)


def partner_2(block, axis, bit):
    count = lax.axis_size(axis)
    route = []
    for low in range(count):
        high = low | 1 << bit
        if high != low and high < count:
            route += [(low, high), (high, low)]
    return lax.ppermute(block, axis, route)


def reverse_bits(values, digits):
    result = jnp.zeros_like(values)
    for bit_level in range(digits):
        result = result | (values >> bit_level & 1) << digits - 1 - bit_level
    return result


def turning(numer, denom):
    angle = numer.astype(jnp.float32) * (-2.0 * math.pi / denom)
    return (jnp.cos(angle), jnp.sin(angle))


def complex_times(stacked, real_part, imag_part):
    return jnp.stack(
        [
            stacked[0] * real_part - stacked[1] * imag_part,
            stacked[0] * imag_part + stacked[1] * real_part,
        ]
    )


def dft_rows(signals, period, inverse):
    indices = jnp.arange(period, dtype=jnp.int32)
    cosine, sine_part = turning(indices[:, None] * indices[None, :] % period, period)
    if inverse:
        sine_part = -sine_part
    stacked = jnp.concatenate([cosine, sine_part], 0)
    result = jnp.einsum("bt,retc->rebc", stacked, signals, precision=lax.Precision.HIGHEST)
    real_out = result[0, :, :period] - result[1, :, period:]
    imag_out = result[1, :, :period] + result[0, :, period:]
    return jnp.stack([real_out, imag_out])


def shards(
    series,
    proj_weight,
    proj_bias,
    short_taps,
    short_bias,
    spectrum,
    skip_gain,
    out_weight,
    out_bias,
):
    steps_dev = series.shape[0]
    model_width = proj_weight.shape[0]
    channels = proj_weight.shape[2]
    flat_weight = proj_weight.reshape(model_width, 3 * channels)
    weight_rows = flat_weight
    projected = jnp.dot(
        lax.all_gather(series, "chan", axis=1, tiled=True),
        weight_rows,
        preferred_element_type=jnp.float32,
    )
    projected = (projected.reshape(steps_dev, 3, channels) + proj_bias).astype(jnp.bfloat16)
    taps_count = short_taps.shape[0]
    earlier = from_behind(projected[steps_dev - taps_count + 1 :], "tm", 1)
    extended = jnp.concatenate([earlier, projected], 0).astype(jnp.float32)
    streams = short_bias + short_taps[0] * extended[taps_count - 1 :]
    for offset in range(1, taps_count):
        streams = (
            streams
            + short_taps[offset]
            * extended[taps_count - 1 - offset : taps_count - 1 - offset + steps_dev]
        )
    streams = lax.optimization_barrier(streams.astype(jnp.bfloat16)).astype(jnp.float32)
    gate_out = streams[:, 0]
    mixed_in = lax.optimization_barrier((streams[:, 1] * streams[:, 2]).astype(jnp.bfloat16))
    signal = mixed_in.astype(jnp.float32)
    tm_count = lax.axis_size("tm")
    digits = tm_count.bit_length() - 1
    own_index = lax.axis_index("tm")
    period = 2 * tm_count * steps_dev
    positions = jnp.arange(steps_dev, dtype=jnp.int32)
    own_rows = 2 * reverse_bits(own_index, digits) + jnp.arange(2, dtype=jnp.int32)
    twist_cos, twist_sin = turning(own_rows[:, None] * positions[None, :] % period, period)
    twist_cos, twist_sin = (twist_cos[:, :, None], twist_sin[:, :, None])
    half_cos, half_sin = turning(own_index, 2 * tm_count)
    zero_field = jnp.zeros_like(signal)
    current = jnp.stack(
        [jnp.stack([signal, signal * half_cos]), jnp.stack([zero_field, signal * half_sin])]
    )
    for bit_level in reversed(range(digits)):
        partner = partner_2(current, "tm", bit_level)
        half_span = 1 << bit_level
        rot_cos, rot_sin = turning(own_index % half_span, 2 * half_span)
        upper_half = own_index >> bit_level & 1 == 1
        current = jnp.where(
            upper_half, complex_times(partner - current, rot_cos, rot_sin), current + partner
        )
    twisted = complex_times(current, twist_cos, twist_sin)
    spectral = dft_rows(twisted, steps_dev, False)
    response = spectrum.reshape(2, 2, steps_dev, channels)
    product = complex_times(spectral, response[0], response[1])
    returned = dft_rows(product, steps_dev, True)
    current = complex_times(returned, twist_cos, -twist_sin)
    for bit_level in range(digits):
        partner = partner_2(current, "tm", bit_level)
        half_span = 1 << bit_level
        rot_cos, rot_sin = turning(own_index % half_span, 2 * half_span)
        rot_sin = -rot_sin
        upper_half = own_index >> bit_level & 1 == 1
        current = jnp.where(
            upper_half,
            partner - complex_times(current, rot_cos, rot_sin),
            current + complex_times(partner, rot_cos, rot_sin),
        )
    convolved = current[0, 0] + half_cos * current[0, 1] + half_sin * current[1, 1]
    convolved = convolved * (1.0 / period)
    gated_rows = ((convolved + skip_gain * signal) * gate_out).astype(jnp.bfloat16)
    column_start = lax.axis_index("chan") * channels
    weight_rows = lax.dynamic_slice_in_dim(out_weight, column_start, channels, 0)
    partial_value = jnp.dot(gated_rows, weight_rows, preferred_element_type=jnp.float32)
    mixed_out = lax.psum_scatter(partial_value, "chan", scatter_dimension=1, tiled=True)
    return (mixed_out + out_bias).astype(jnp.bfloat16)


def make_tables(tm_count, steps):
    count, period = 2 * tm_count, 2 * tm_count * steps
    rows = np.arange(steps)
    angle = 2.0 * np.pi * (rows[:, None] * rows[None, :] % steps) / steps
    dft = np.stack([np.cos(angle), np.sin(angle)]).astype(jnp.bfloat16)
    angle = 2.0 * np.pi * (np.arange(count)[:, None] * rows[None, :] % period) / period
    twist = np.stack([np.cos(angle), np.sin(angle)]).astype(np.float32)
    return dft, twist


def flip(value, digits):
    result = 0
    for bit_level in range(digits):
        result |= (value >> bit_level & 1) << digits - 1 - bit_level
    return result


def weighted(blocks, weights):
    total = None
    for block, weight in zip(blocks, weights):
        if abs(weight) < 1e-12:
            continue
        if abs(weight - 1.0) < 1e-12:
            term = block
        elif abs(weight + 1.0) < 1e-12:
            term = -block
        else:
            term = block * float(weight)
        total = term if total is None else total + term
    return total


def kernel(
    tm_count,
    chan_count,
    series,
    weight,
    proj_bias,
    taps,
    short_bias,
    spectrum,
    skip_gain,
    out_weight,
    out_bias,
    dft,
    twist,
    out,
    rows_in,
    weight_v,
    proj_bias_v,
    taps_v,
    short_bias_v,
    spectrum_v,
    skip_v,
    out_weight_v,
    out_weight_t,
    out_bias_v,
    dft_v,
    twist_v,
    projected,
    spec_out,
    spec_in,
    mixed_out,
    mixed_in,
    wave,
    conv_out,
    conv_in,
    gate_t,
    direct_t,
    gated,
    local_sem,
    rows_send,
    rows_recv,
    halo_send,
    halo_recv,
    spec_send,
    spec_recv,
    mix_send,
    mix_recv,
    conv_send,
    conv_recv,
    gate_send,
    gate_recv,
):
    steps, channels = series.shape
    halo = rows_in.shape[0] - steps
    share = channels // tm_count
    digits = tm_count.bit_length() - 1
    slots = 2 * tm_count
    own_t, own_c = lax.axis_index("tm"), lax.axis_index("chan")
    columns = lambda c: pl.ds(pl.multiple_of(c * channels, channels), channels)
    tm_peer = lambda by: lax.rem(own_t + by, tm_count)
    chan_peer = lambda by: lax.rem(own_c + by, chan_count)

    barrier = pltpu.get_barrier_semaphore()
    greet = lambda where: pl.semaphore_signal(barrier, inc=1, device_id=where, device_id_type=MESH)
    for by in range(1, chan_count):
        greet({"chan": chan_peer(by)})
    for by in range(1, tm_count):
        greet({"tm": tm_peer(by)})
    for by in range(1, chan_count):
        greet({"tm": tm_peer(1), "chan": chan_peer(by)})
        greet({"tm": tm_peer(tm_count - 1), "chan": chan_peer(by)})

    pairs = [
        (series, rows_in.at[pl.ds(halo, steps), columns(own_c)]),
        (spectrum.at[:, 0], spectrum_v),
        (weight, weight_v),
        (proj_bias, proj_bias_v),
        (taps, taps_v),
        (short_bias, short_bias_v),
        (dft, dft_v),
        (twist, twist_v),
        (skip_gain, skip_v),
        (out_weight.at[:, columns(own_c)], out_weight_v),
        (out_bias, out_bias_v),
    ]
    local = [pltpu.make_async_copy(a, b, local_sem.at[i]) for i, (a, b) in enumerate(pairs)]
    for copy in local:
        copy.start()
    own_rows = rows_in.at[pl.ds(halo, steps), columns(own_c)]
    local[0].wait()
    pl.semaphore_wait(barrier, chan_count - 1 + tm_count - 1 + 2 * (chan_count - 1))

    def remote(src, dst, send, recv, where):
        return pltpu.make_async_remote_copy(
            src_ref=src, dst_ref=dst, send_sem=send, recv_sem=recv, device_id=where, device_id_type=MESH
        )

    def rows_copy(by, owner):
        return remote(
            own_rows,
            rows_in.at[pl.ds(halo, steps), columns(owner)],
            rows_send.at[by],
            rows_recv.at[by],
            {"chan": chan_peer(by)},
        )

    def halo_copy(by, owner):
        return remote(
            rows_in.at[pl.ds(steps, halo), columns(own_c)],
            rows_in.at[pl.ds(0, halo), columns(owner)],
            halo_send.at[by],
            halo_recv.at[by],
            {"tm": tm_peer(1), "chan": chan_peer(by)},
        )

    for by in range(1, chan_count):
        rows_copy(by, own_c).start()

    @pl.when(own_t < tm_count - 1)
    def _():
        for by in range(chan_count):
            halo_copy(by, own_c).start()

    @pl.when(own_t == 0)
    def _():
        rows_in[pl.ds(0, halo), :] = jnp.zeros((halo, rows_in.shape[1]), rows_in.dtype)

    local[1].wait()
    residue = 2 * sum((own_t >> i & 1) << digits - 1 - i for i in range(digits))
    down = lax.broadcasted_iota(jnp.int32, (steps, steps), 0)
    across = lax.broadcasted_iota(jnp.int32, (steps, steps), 1)
    for parity in range(2):
        wanted = jnp.where(residue + parity > tm_count, steps - 1 - down, down)
        order = jnp.where(wanted == across, 1.0 / (slots * steps), 0.0).astype(jnp.bfloat16)
        for part in range(2):
            block = spectrum_v[part, parity].astype(jnp.bfloat16)
            block = jnp.dot(order, block, preferred_element_type=jnp.float32).T
            spec_out[:, part, parity] = block.astype(jnp.bfloat16).reshape(tm_count, share, steps)

    def to_peer(src, dst, send, recv, by):
        return remote(src.at[tm_peer(by)], dst.at[own_t], send.at[by], recv.at[by], {"tm": tm_peer(by)})

    def spread(src, dst, send, recv):
        for by in range(1, tm_count):
            to_peer(src, dst, send, recv, by).start()
        dst[own_t] = src[own_t]

    def collect(src, dst, send, recv):
        for by in range(1, tm_count):
            copy = remote(
                src.at[0], dst.at[tm_peer(tm_count - by)], send.at[by], recv.at[by], {"tm": tm_peer(by)}
            )
            copy.wait_recv()

    spread(spec_out, spec_in, spec_send, spec_recv)

    for copy in local[2:]:
        copy.wait()
    for by in range(1, chan_count):
        rows_copy(by, chan_peer(chan_count - by)).wait_recv()

    @pl.when(own_t > 0)
    def _():
        for by in range(chan_count):
            halo_copy(by, chan_peer(chan_count - by)).wait_recv()

    streams = []
    for j in (1, 2, 0):
        value = jnp.dot(rows_in[...], weight_v[j], preferred_element_type=jnp.float32)
        value = (value + proj_bias_v[j : j + 1]).astype(jnp.bfloat16).astype(jnp.float32)
        projected[j] = value

        @pl.when(own_t == 0)
        def _():
            projected[j, pl.ds(0, halo)] = jnp.zeros((halo, channels), jnp.float32)

        stream = short_bias_v[j : j + 1] + taps_v[0, j : j + 1] * projected[j, pl.ds(halo, steps)]
        for k in range(1, taps.shape[0]):
            stream = stream + taps_v[k, j : j + 1] * projected[j, pl.ds(halo - k, steps)]
        stream = stream.astype(jnp.bfloat16).astype(jnp.float32)
        if j == 2:
            signal = (streams[0] * stream).astype(jnp.bfloat16).astype(jnp.float32)
            mixed_out[...] = signal.T.astype(jnp.bfloat16).reshape(tm_count, share, steps)
            spread(mixed_out, mixed_in, mix_send, mix_recv)
        streams.append(stream)
    gate_t[...] = streams[2].T.reshape(tm_count, share, steps)
    direct_t[...] = (skip_v[...] * signal).T.reshape(tm_count, share, steps)
    for c in range(chan_count):
        out_weight_t[c] = out_weight_v[pl.ds(c * channels, channels)].astype(jnp.float32).T.astype(jnp.bfloat16)

    collect(mixed_out, mixed_in, mix_send, mix_recv)
    blocks = [mixed_in[b].astype(jnp.float32) for b in range(tm_count)]
    turns = 2.0 * np.pi * np.arange(slots) / slots
    cosine = lambda r, b: math.cos(turns[r * b % slots])
    sine = lambda r, b: math.sin(turns[r * b % slots])
    kept = tm_count + 1

    for r in range(kept):
        real = weighted(blocks, [cosine(r, b) for b in range(tm_count)])
        imag = weighted(blocks, [-sine(r, b) for b in range(tm_count)])
        cos_row, sin_row = twist_v[0, r : r + 1], twist_v[1, r : r + 1]
        if imag is None:
            turned = (real * cos_row, -(real * sin_row))
        else:
            turned = (real * cos_row + imag * sin_row, imag * cos_row - real * sin_row)
        for part in range(2):
            wave[part, r] = turned[part].astype(jnp.bfloat16)

    def within():
        rows = wave[...].reshape(2 * kept * share, steps)
        first = jnp.dot(rows, dft_v[0], preferred_element_type=jnp.float32)
        second = jnp.dot(rows, dft_v[1], preferred_element_type=jnp.float32)
        half = kept * share
        return [a.reshape(kept, share, steps) for a in (first[:half], first[half:], second[:half], second[half:])]

    real_cos, imag_cos, real_sin, imag_sin = within()
    real, imag = real_cos + imag_sin, imag_cos - real_sin
    collect(spec_out, spec_in, spec_send, spec_recv)

    def filter_of(part, r):
        return spec_in[flip(r // 2, digits), part, r % 2].astype(jnp.float32)

    for r in range(kept):
        filter_real, filter_imag = filter_of(0, r), filter_of(1, r)
        if 0 < r < tm_count:
            filter_real = filter_real + filter_of(0, slots - r)
            filter_imag = filter_imag - filter_of(1, slots - r)
        wave[0, r] = (real[r] * filter_real - imag[r] * filter_imag).astype(jnp.bfloat16)
        wave[1, r] = (real[r] * filter_imag + imag[r] * filter_real).astype(jnp.bfloat16)
    real_cos, imag_cos, real_sin, imag_sin = within()
    real, imag = real_cos - imag_sin, real_sin + imag_cos

    terms = []
    for r in range(kept):
        cos_row, sin_row = twist_v[0, r : r + 1], twist_v[1, r : r + 1]
        terms.append(real[r] * cos_row - imag[r] * sin_row)
    for r in range(kept):
        cos_row, sin_row = twist_v[0, r : r + 1], twist_v[1, r : r + 1]
        terms.append(real[r] * sin_row + imag[r] * cos_row)
    for b in range(tm_count):
        weights = [cosine(r, b) for r in range(kept)] + [-sine(r, b) for r in range(kept)]
        conv_out[b] = weighted(terms, weights).astype(jnp.bfloat16)
    spread(conv_out, conv_in, conv_send, conv_recv)

    def gate_copy(by, owner, shift):
        block = gated.at[owner, tm_peer(tm_count - shift)]
        return remote(block, block, gate_send.at[by, shift], gate_recv.at[by, shift], {"chan": chan_peer(by)})

    nearest = sorted(range(tm_count), key=lambda by: min(by, tm_count - by))
    for shift in nearest:
        source = tm_peer(tm_count - shift)
        if shift:
            remote(
                conv_out.at[0], conv_in.at[source], conv_send.at[shift], conv_recv.at[shift], {"tm": tm_peer(shift)}
            ).wait_recv()
        value = (conv_in[source].astype(jnp.float32) + direct_t[source]) * gate_t[source]
        gated[own_c, source] = value.astype(jnp.bfloat16)
        for by in range(1, chan_count):
            gate_copy(by, own_c, shift).start()

    total = None
    for by in range(chan_count):
        owner = chan_peer(chan_count - by)
        if by:
            for shift in nearest:
                gate_copy(by, owner, shift).wait_recv()
        rows = gated[owner].reshape(channels, steps)
        term = jnp.dot(out_weight_t[owner], rows, preferred_element_type=jnp.float32)
        total = term if total is None else total + term
    out[...] = (total.T + out_bias_v[...]).astype(out.dtype)

    for by in range(1, chan_count):
        rows_copy(by, own_c).wait_send()
        for shift in nearest:
            gate_copy(by, own_c, shift).wait_send()

    @pl.when(own_t < tm_count - 1)
    def _():
        for by in range(chan_count):
            halo_copy(by, own_c).wait_send()

    for by in range(1, tm_count):
        to_peer(spec_out, spec_in, spec_send, spec_recv, by).wait_send()
        to_peer(mixed_out, mixed_in, mix_send, mix_recv, by).wait_send()
        to_peer(conv_out, conv_in, conv_send, conv_recv, by).wait_send()


def fused(
    series,
    proj_weight,
    proj_bias,
    short_taps,
    short_bias,
    spectrum,
    skip_gain,
    out_weight,
    out_bias,
):
    steps, channels = series.shape
    width = proj_weight.shape[0]
    tm_count, chan_count = lax.axis_size("tm"), lax.axis_size("chan")
    dft, twist = make_tables(tm_count, steps)
    share, slots, halo = channels // tm_count, 2 * tm_count, 16
    spread_shape = (tm_count, share, steps)
    vmem, dma = pltpu.VMEM, pltpu.SemaphoreType.DMA
    operands = [
        series,
        proj_weight.transpose(1, 0, 2),
        proj_bias,
        short_taps,
        short_bias,
        spectrum,
        skip_gain.reshape(1, channels),
        out_weight,
        out_bias.reshape(1, channels),
        jnp.asarray(dft),
        jnp.asarray(twist),
    ]
    tm_sems = [dma((tm_count,)), dma((tm_count,))]
    chan_sems = [dma((chan_count,)), dma((chan_count,))]
    return pl.pallas_call(
        functools.partial(kernel, tm_count, chan_count),
        out_shape=jax.ShapeDtypeStruct((steps, channels), jnp.bfloat16),
        in_specs=[pl.BlockSpec(memory_space=pl.ANY)] * len(operands),
        out_specs=pl.BlockSpec(memory_space=pltpu.VMEM),
        scratch_shapes=[
            vmem((halo + steps, width), jnp.bfloat16),
            vmem((3, width, channels), jnp.bfloat16),
            vmem(proj_bias.shape, jnp.float32),
            vmem(short_taps.shape, jnp.float32),
            vmem(short_bias.shape, jnp.float32),
            vmem((2, 2, steps, channels), jnp.float32),
            vmem((1, channels), jnp.float32),
            vmem((width, channels), jnp.bfloat16),
            vmem((chan_count, channels, channels), jnp.bfloat16),
            vmem((1, channels), jnp.float32),
            vmem(dft.shape, jnp.bfloat16),
            vmem(twist.shape, jnp.float32),
            vmem((3, halo + steps, channels), jnp.float32),
            vmem((tm_count, 2, 2, share, steps), jnp.bfloat16),
            vmem((tm_count, 2, 2, share, steps), jnp.bfloat16),
            vmem(spread_shape, jnp.bfloat16),
            vmem(spread_shape, jnp.bfloat16),
            vmem((2, tm_count + 1, share, steps), jnp.bfloat16),
            vmem(spread_shape, jnp.bfloat16),
            vmem(spread_shape, jnp.bfloat16),
            vmem(spread_shape, jnp.float32),
            vmem(spread_shape, jnp.float32),
            vmem((chan_count, *spread_shape), jnp.bfloat16),
            dma((len(operands),)),
            *chan_sems,
            *chan_sems,
            *tm_sems,
            *tm_sems,
            *tm_sems,
            dma((chan_count, tm_count)),
            dma((chan_count, tm_count)),
        ],
        compiler_params=pltpu.CompilerParams(
            collective_id=0, has_side_effects=True, vmem_limit_bytes=60 * 1024 * 1024
        ),
    )(*operands)


def solution(mesh):
    sizes = mesh.shape

    def program(*arrays):
        share = arrays[0].shape[1] // sizes["chan"] // sizes["tm"]
        wide = share > 0 and share % 16 == 0 and sizes["tm"] >= 4
        return jax.shard_map(
            fused if wide else shards,
            mesh=mesh,
            in_specs=(
                P("tm", "chan"),
                P(None, None, "chan"),
                P(None, "chan"),
                P(None, None, "chan"),
                P(None, "chan"),
                P(None, "tm", None, None, "chan"),
                P("chan"),
                P(),
                P("chan"),
            ),
            out_specs=P("tm", "chan"),
            check_vma=False,
        )(*arrays)

    return program
```

```python
import functools
import math

import jax
import jax.numpy as jnp
import numpy as np
from jax import lax
from jax.experimental import pallas as pl
from jax.experimental.pallas import tpu as pltpu
from jax.sharding import PartitionSpec as P

MESH = pl.DeviceIdType.MESH


def from_behind(array, axis, by):
    length = lax.axis_size(axis)
    pairs = [(i, i + by) for i in range(length) if 0 <= i + by < length]
    return lax.ppermute(array, axis, pairs)


def partner_2(block, axis, bit):
    count = lax.axis_size(axis)
    route = []
    for low in range(count):
        high = low | 1 << bit
        if high != low and high < count:
            route += [(low, high), (high, low)]
    return lax.ppermute(block, axis, route)


def reverse_bits(values, digits):
    result = jnp.zeros_like(values)
    for bit_level in range(digits):
        result = result | (values >> bit_level & 1) << digits - 1 - bit_level
    return result


def turning(numer, denom):
    angle = numer.astype(jnp.float32) * (-2.0 * math.pi / denom)
    return (jnp.cos(angle), jnp.sin(angle))


def complex_times(stacked, real_part, imag_part):
    return jnp.stack(
        [
            stacked[0] * real_part - stacked[1] * imag_part,
            stacked[0] * imag_part + stacked[1] * real_part,
        ]
    )


def dft_rows(signals, period, inverse):
    indices = jnp.arange(period, dtype=jnp.int32)
    cosine, sine_part = turning(indices[:, None] * indices[None, :] % period, period)
    if inverse:
        sine_part = -sine_part
    stacked = jnp.concatenate([cosine, sine_part], 0)
    result = jnp.einsum("bt,retc->rebc", stacked, signals, precision=lax.Precision.HIGHEST)
    real_out = result[0, :, :period] - result[1, :, period:]
    imag_out = result[1, :, :period] + result[0, :, period:]
    return jnp.stack([real_out, imag_out])


def shards(
    series,
    proj_weight,
    proj_bias,
    short_taps,
    short_bias,
    spectrum,
    skip_gain,
    out_weight,
    out_bias,
):
    steps_dev = series.shape[0]
    model_width = proj_weight.shape[0]
    channels = proj_weight.shape[2]
    flat_weight = proj_weight.reshape(model_width, 3 * channels)
    weight_rows = flat_weight
    projected = jnp.dot(
        lax.all_gather(series, "chan", axis=1, tiled=True),
        weight_rows,
        preferred_element_type=jnp.float32,
    )
    projected = (projected.reshape(steps_dev, 3, channels) + proj_bias).astype(jnp.bfloat16)
    taps_count = short_taps.shape[0]
    earlier = from_behind(projected[steps_dev - taps_count + 1 :], "tm", 1)
    extended = jnp.concatenate([earlier, projected], 0).astype(jnp.float32)
    streams = short_bias + short_taps[0] * extended[taps_count - 1 :]
    for offset in range(1, taps_count):
        streams = (
            streams
            + short_taps[offset]
            * extended[taps_count - 1 - offset : taps_count - 1 - offset + steps_dev]
        )
    streams = lax.optimization_barrier(streams.astype(jnp.bfloat16)).astype(jnp.float32)
    gate_out = streams[:, 0]
    mixed_in = lax.optimization_barrier((streams[:, 1] * streams[:, 2]).astype(jnp.bfloat16))
    signal = mixed_in.astype(jnp.float32)
    tm_count = lax.axis_size("tm")
    digits = tm_count.bit_length() - 1
    own_index = lax.axis_index("tm")
    period = 2 * tm_count * steps_dev
    positions = jnp.arange(steps_dev, dtype=jnp.int32)
    own_rows = 2 * reverse_bits(own_index, digits) + jnp.arange(2, dtype=jnp.int32)
    twist_cos, twist_sin = turning(own_rows[:, None] * positions[None, :] % period, period)
    twist_cos, twist_sin = (twist_cos[:, :, None], twist_sin[:, :, None])
    half_cos, half_sin = turning(own_index, 2 * tm_count)
    zero_field = jnp.zeros_like(signal)
    current = jnp.stack(
        [jnp.stack([signal, signal * half_cos]), jnp.stack([zero_field, signal * half_sin])]
    )
    for bit_level in reversed(range(digits)):
        partner = partner_2(current, "tm", bit_level)
        half_span = 1 << bit_level
        rot_cos, rot_sin = turning(own_index % half_span, 2 * half_span)
        upper_half = own_index >> bit_level & 1 == 1
        current = jnp.where(
            upper_half, complex_times(partner - current, rot_cos, rot_sin), current + partner
        )
    twisted = complex_times(current, twist_cos, twist_sin)
    spectral = dft_rows(twisted, steps_dev, False)
    response = spectrum.reshape(2, 2, steps_dev, channels)
    product = complex_times(spectral, response[0], response[1])
    returned = dft_rows(product, steps_dev, True)
    current = complex_times(returned, twist_cos, -twist_sin)
    for bit_level in range(digits):
        partner = partner_2(current, "tm", bit_level)
        half_span = 1 << bit_level
        rot_cos, rot_sin = turning(own_index % half_span, 2 * half_span)
        rot_sin = -rot_sin
        upper_half = own_index >> bit_level & 1 == 1
        current = jnp.where(
            upper_half,
            partner - complex_times(current, rot_cos, rot_sin),
            current + complex_times(partner, rot_cos, rot_sin),
        )
    convolved = current[0, 0] + half_cos * current[0, 1] + half_sin * current[1, 1]
    convolved = convolved * (1.0 / period)
    gated_rows = ((convolved + skip_gain * signal) * gate_out).astype(jnp.bfloat16)
    column_start = lax.axis_index("chan") * channels
    weight_rows = lax.dynamic_slice_in_dim(out_weight, column_start, channels, 0)
    partial_value = jnp.dot(gated_rows, weight_rows, preferred_element_type=jnp.float32)
    mixed_out = lax.psum_scatter(partial_value, "chan", scatter_dimension=1, tiled=True)
    return (mixed_out + out_bias).astype(jnp.bfloat16)


def make_tables(tm_count, steps):
    count, period = 2 * tm_count, 2 * tm_count * steps
    rows = np.arange(steps)
    angle = 2.0 * np.pi * (rows[:, None] * rows[None, :] % steps) / steps
    dft = np.stack([np.cos(angle), np.sin(angle)]).astype(jnp.bfloat16)
    angle = 2.0 * np.pi * (np.arange(count)[:, None] * rows[None, :] % period) / period
    twist = np.stack([np.cos(angle), np.sin(angle)]).astype(np.float32)
    return dft, twist


def flip(value, digits):
    result = 0
    for bit_level in range(digits):
        result |= (value >> bit_level & 1) << digits - 1 - bit_level
    return result


def across_bits(index, by):
    result, bit = index, 1
    while bit <= by:
        if by & bit:
            result = result + bit * (1 - 2 * lax.rem(lax.div(index, bit), 2))
        bit *= 2
    return result


def weighted(blocks, weights):
    total = None
    for block, weight in zip(blocks, weights):
        if abs(weight) < 1e-12:
            continue
        if abs(weight - 1.0) < 1e-12:
            term = block
        elif abs(weight + 1.0) < 1e-12:
            term = -block
        else:
            term = block * float(weight)
        total = term if total is None else total + term
    return total


def kernel(
    tm_count,
    chan_count,
    series,
    weight,
    proj_bias,
    taps,
    short_bias,
    spectrum,
    skip_gain,
    out_weight,
    out_bias,
    dft,
    twist,
    out,
    rows_in,
    weight_v,
    proj_bias_v,
    taps_v,
    short_bias_v,
    spectrum_v,
    skip_v,
    out_weight_v,
    out_weight_t,
    out_bias_v,
    dft_v,
    twist_v,
    projected,
    spec_out,
    spec_in,
    mixed_out,
    mixed_in,
    wave,
    conv_out,
    conv_in,
    gate_t,
    direct_t,
    gated,
    local_sem,
    rows_send,
    rows_recv,
    halo_send,
    halo_recv,
    spec_send,
    spec_recv,
    mix_send,
    mix_recv,
    conv_send,
    conv_recv,
    gate_send,
    gate_recv,
):
    steps, channels = series.shape
    halo = rows_in.shape[0] - steps
    share = channels // tm_count
    digits = tm_count.bit_length() - 1
    slots = 2 * tm_count
    own_t, own_c = lax.axis_index("tm"), lax.axis_index("chan")
    columns = lambda c: pl.ds(pl.multiple_of(c * channels, channels), channels)
    next_t, last_t = lax.rem(own_t + 1, tm_count), lax.rem(own_t + tm_count - 1, tm_count)
    tm_peer = lambda by: across_bits(own_t, by)
    chan_peer = lambda by: across_bits(own_c, by)
    far_first = list(range(tm_count // 2, tm_count)) + list(range(1, tm_count // 2))

    barrier = pltpu.get_barrier_semaphore()
    greet = lambda where: pl.semaphore_signal(barrier, inc=1, device_id=where, device_id_type=MESH)
    for by in range(1, chan_count):
        greet({"chan": chan_peer(by)})
    for by in range(1, tm_count):
        greet({"tm": tm_peer(by)})
    for by in range(1, chan_count):
        greet({"tm": next_t, "chan": chan_peer(by)})
        greet({"tm": last_t, "chan": chan_peer(by)})

    pairs = [
        (series, rows_in.at[pl.ds(halo, steps), columns(own_c)]),
        (spectrum.at[:, 0], spectrum_v),
        (weight, weight_v),
        (proj_bias, proj_bias_v),
        (taps, taps_v),
        (short_bias, short_bias_v),
        (dft, dft_v),
        (twist, twist_v),
        (skip_gain, skip_v),
        (out_weight.at[:, columns(own_c)], out_weight_v),
        (out_bias, out_bias_v),
    ]
    local = [pltpu.make_async_copy(a, b, local_sem.at[i]) for i, (a, b) in enumerate(pairs)]
    for copy in local:
        copy.start()
    own_rows = rows_in.at[pl.ds(halo, steps), columns(own_c)]

    def remote(src, dst, send, recv, where):
        return pltpu.make_async_remote_copy(
            src_ref=src, dst_ref=dst, send_sem=send, recv_sem=recv, device_id=where, device_id_type=MESH
        )

    local[1].wait()
    residue = 2 * sum((own_t >> i & 1) << digits - 1 - i for i in range(digits))
    down = lax.broadcasted_iota(jnp.int32, (steps, steps), 0)
    across = lax.broadcasted_iota(jnp.int32, (steps, steps), 1)
    for parity in range(2):
        wanted = jnp.where(residue + parity > tm_count, steps - 1 - down, down)
        order = jnp.where(wanted == across, 1.0 / (slots * steps), 0.0).astype(jnp.bfloat16)
        for part in range(2):
            block = spectrum_v[part, parity].astype(jnp.bfloat16)
            block = jnp.dot(order, block, preferred_element_type=jnp.float32).T
            spec_out[:, part, parity] = block.astype(jnp.bfloat16).reshape(tm_count, share, steps)

    local[0].wait()
    pl.semaphore_wait(barrier, chan_count - 1 + tm_count - 1 + 2 * (chan_count - 1))

    def rows_copy(by, owner):
        return remote(
            own_rows,
            rows_in.at[pl.ds(halo, steps), columns(owner)],
            rows_send.at[0],
            rows_recv.at[0],
            {"chan": chan_peer(by)},
        )

    def halo_copy(by, owner):
        return remote(
            rows_in.at[pl.ds(steps, halo), columns(own_c)],
            rows_in.at[pl.ds(0, halo), columns(owner)],
            halo_send.at[0],
            halo_recv.at[0],
            {"tm": next_t, "chan": chan_peer(by)},
        )

    for by in range(1, chan_count):
        rows_copy(by, own_c).start()

    @pl.when(own_t < tm_count - 1)
    def _():
        for by in range(chan_count):
            halo_copy(by, own_c).start()

    @pl.when(own_t == 0)
    def _():
        rows_in[pl.ds(0, halo), :] = jnp.zeros((halo, rows_in.shape[1]), rows_in.dtype)

    def bytes_of(ref, sem):
        pltpu.make_async_copy(ref, ref, sem).wait()

    def spread(src, dst, send, recv):
        for by in far_first:
            remote(src.at[tm_peer(by)], dst.at[own_t], send.at[0], recv.at[0], {"tm": tm_peer(by)}).start()
        dst[own_t] = src[own_t]

    def collect(dst, recv):
        bytes_of(dst.at[pl.ds(0, tm_count - 1)], recv.at[0])

    spread(spec_out, spec_in, spec_send, spec_recv)

    for copy in local[2:]:
        copy.wait()
    others = pl.ds(0, (chan_count - 1) * channels)
    bytes_of(rows_in.at[pl.ds(halo, steps), others], rows_recv.at[0])

    @pl.when(own_t > 0)
    def _():
        bytes_of(rows_in.at[pl.ds(0, halo)], halo_recv.at[0])

    streams = []
    for j in (1, 2, 0):
        value = jnp.dot(rows_in[...], weight_v[j], preferred_element_type=jnp.float32)
        value = (value + proj_bias_v[j : j + 1]).astype(jnp.bfloat16).astype(jnp.float32)
        projected[j] = value

        @pl.when(own_t == 0)
        def _():
            projected[j, pl.ds(0, halo)] = jnp.zeros((halo, channels), jnp.float32)

        stream = short_bias_v[j : j + 1] + taps_v[0, j : j + 1] * projected[j, pl.ds(halo, steps)]
        for k in range(1, taps.shape[0]):
            stream = stream + taps_v[k, j : j + 1] * projected[j, pl.ds(halo - k, steps)]
        stream = stream.astype(jnp.bfloat16).astype(jnp.float32)
        if j == 2:
            signal = (streams[0] * stream).astype(jnp.bfloat16).astype(jnp.float32)
            mixed_out[...] = signal.T.astype(jnp.bfloat16).reshape(tm_count, share, steps)
            spread(mixed_out, mixed_in, mix_send, mix_recv)
        streams.append(stream)
    gate_t[...] = streams[2].T.reshape(tm_count, share, steps)
    direct_t[...] = (skip_v[...] * signal).T.reshape(tm_count, share, steps)
    for c in range(chan_count):
        blocks = [
            out_weight_v[pl.ds(pl.multiple_of(c * channels + tm_peer(by) * share, share), share)]
            for by in range(tm_count)
        ]
        turned = jnp.concatenate(blocks, 0).astype(jnp.float32).T.astype(jnp.bfloat16)
        out_weight_t[0, c] = turned[:, : channels // 2]
        out_weight_t[1, c] = turned[:, channels // 2 :]

    collect(mixed_in, mix_recv)
    blocks = [mixed_in[b].astype(jnp.float32) for b in range(tm_count)]
    turns = 2.0 * np.pi * np.arange(slots) / slots
    cosine = lambda r, b: math.cos(turns[r * b % slots])
    sine = lambda r, b: math.sin(turns[r * b % slots])
    kept = tm_count + 1

    for r in range(kept):
        real = weighted(blocks, [cosine(r, b) for b in range(tm_count)])
        imag = weighted(blocks, [-sine(r, b) for b in range(tm_count)])
        cos_row, sin_row = twist_v[0, r : r + 1], twist_v[1, r : r + 1]
        if imag is None:
            turned = (real * cos_row, -(real * sin_row))
        else:
            turned = (real * cos_row + imag * sin_row, imag * cos_row - real * sin_row)
        for part in range(2):
            wave[part, r] = turned[part].astype(jnp.bfloat16)

    def within():
        rows = wave[...].reshape(2 * kept * share, steps)
        first = jnp.dot(rows, dft_v[0], preferred_element_type=jnp.float32)
        second = jnp.dot(rows, dft_v[1], preferred_element_type=jnp.float32)
        half = kept * share
        return [a.reshape(kept, share, steps) for a in (first[:half], first[half:], second[:half], second[half:])]

    real_cos, imag_cos, real_sin, imag_sin = within()
    real, imag = real_cos + imag_sin, imag_cos - real_sin
    collect(spec_in, spec_recv)

    def filter_of(part, r):
        return spec_in[flip(r // 2, digits), part, r % 2].astype(jnp.float32)

    for r in range(kept):
        filter_real, filter_imag = filter_of(0, r), filter_of(1, r)
        if 0 < r < tm_count:
            filter_real = filter_real + filter_of(0, slots - r)
            filter_imag = filter_imag - filter_of(1, slots - r)
        wave[0, r] = (real[r] * filter_real - imag[r] * filter_imag).astype(jnp.bfloat16)
        wave[1, r] = (real[r] * filter_imag + imag[r] * filter_real).astype(jnp.bfloat16)
    real_cos, imag_cos, real_sin, imag_sin = within()
    real, imag = real_cos - imag_sin, real_sin + imag_cos

    terms = []
    for r in range(kept):
        cos_row, sin_row = twist_v[0, r : r + 1], twist_v[1, r : r + 1]
        terms.append(real[r] * cos_row - imag[r] * sin_row)
    for r in range(kept):
        cos_row, sin_row = twist_v[0, r : r + 1], twist_v[1, r : r + 1]
        terms.append(real[r] * sin_row + imag[r] * cos_row)
    for b in range(tm_count):
        weights = [cosine(r, b) for r in range(kept)] + [-sine(r, b) for r in range(kept)]
        conv_out[b] = weighted(terms, weights).astype(jnp.bfloat16)
    near = tm_count // 2
    for by in far_first:
        half = by // near
        remote(
            conv_out.at[tm_peer(by)], conv_in.at[by], conv_send.at[0], conv_recv.at[half], {"tm": tm_peer(by)}
        ).start()

    bytes_of(rows_in.at[pl.ds(halo, steps), others], rows_send.at[0])

    @pl.when(own_t < tm_count - 1)
    def _():
        bytes_of(rows_in.at[pl.ds(0, halo)], halo_send.at[0])

    bytes_of(spec_in.at[pl.ds(0, tm_count - 1)], spec_send.at[0])
    bytes_of(mixed_in.at[pl.ds(0, tm_count - 1)], mix_send.at[0])

    for half in range(2):
        if half == 0:
            bytes_of(conv_in.at[pl.ds(0, near - 1)], conv_recv.at[0])
        else:
            bytes_of(conv_in.at[pl.ds(0, near)], conv_recv.at[1])
        for by in range(half * near, (half + 1) * near):
            source = tm_peer(by)
            arrived = conv_in[by] if by else conv_out[source]
            value = (arrived.astype(jnp.float32) + direct_t[source]) * gate_t[source]
            gated[half, own_c, pl.ds(by % near * share, share)] = value.astype(jnp.bfloat16)
        for by in range(chan_count - 1, 0, -1):
            block = gated.at[half, own_c]
            remote(block, block, gate_send.at[half], gate_recv.at[half], {"chan": chan_peer(by)}).start()

    total = None
    for half in range(2):
        bytes_of(gated.at[half, pl.ds(0, chan_count - 1)], gate_recv.at[half])
        for c in range(chan_count):
            term = jnp.dot(out_weight_t[half, c], gated[half, c], preferred_element_type=jnp.float32)
            total = term if total is None else total + term
    out[...] = (total.T + out_bias_v[...]).astype(out.dtype)

    bytes_of(conv_in.at[pl.ds(0, tm_count - 1)], conv_send.at[0])
    for half in range(2):
        bytes_of(gated.at[half, pl.ds(0, chan_count - 1)], gate_send.at[half])


def fused(
    series,
    proj_weight,
    proj_bias,
    short_taps,
    short_bias,
    spectrum,
    skip_gain,
    out_weight,
    out_bias,
):
    steps, channels = series.shape
    width = proj_weight.shape[0]
    tm_count, chan_count = lax.axis_size("tm"), lax.axis_size("chan")
    dft, twist = make_tables(tm_count, steps)
    share, slots, halo = channels // tm_count, 2 * tm_count, 16
    spread_shape = (tm_count, share, steps)
    vmem, dma = pltpu.VMEM, pltpu.SemaphoreType.DMA
    operands = [
        series,
        proj_weight.transpose(1, 0, 2),
        proj_bias,
        short_taps,
        short_bias,
        spectrum,
        skip_gain.reshape(1, channels),
        out_weight,
        out_bias.reshape(1, channels),
        jnp.asarray(dft),
        jnp.asarray(twist),
    ]
    return pl.pallas_call(
        functools.partial(kernel, tm_count, chan_count),
        out_shape=jax.ShapeDtypeStruct((steps, channels), jnp.bfloat16),
        in_specs=[pl.BlockSpec(memory_space=pl.ANY)] * len(operands),
        out_specs=pl.BlockSpec(memory_space=pltpu.VMEM),
        scratch_shapes=[
            vmem((halo + steps, width), jnp.bfloat16),
            vmem((3, width, channels), jnp.bfloat16),
            vmem(proj_bias.shape, jnp.float32),
            vmem(short_taps.shape, jnp.float32),
            vmem(short_bias.shape, jnp.float32),
            vmem((2, 2, steps, channels), jnp.float32),
            vmem((1, channels), jnp.float32),
            vmem((width, channels), jnp.bfloat16),
            vmem((2, chan_count, channels, channels // 2), jnp.bfloat16),
            vmem((1, channels), jnp.float32),
            vmem(dft.shape, jnp.bfloat16),
            vmem(twist.shape, jnp.float32),
            vmem((3, halo + steps, channels), jnp.float32),
            vmem((tm_count, 2, 2, share, steps), jnp.bfloat16),
            vmem((tm_count, 2, 2, share, steps), jnp.bfloat16),
            vmem(spread_shape, jnp.bfloat16),
            vmem(spread_shape, jnp.bfloat16),
            vmem((2, tm_count + 1, share, steps), jnp.bfloat16),
            vmem(spread_shape, jnp.bfloat16),
            vmem(spread_shape, jnp.bfloat16),
            vmem(spread_shape, jnp.float32),
            vmem(spread_shape, jnp.float32),
            vmem((2, chan_count, channels // 2, steps), jnp.bfloat16),
            dma((len(operands),)),
            *[dma((2,))] * 12,
        ],
        compiler_params=pltpu.CompilerParams(
            collective_id=0, has_side_effects=True, vmem_limit_bytes=60 * 1024 * 1024
        ),
    )(*operands)


def solution(mesh):
    sizes = mesh.shape

    def program(*arrays):
        share = arrays[0].shape[1] // sizes["chan"] // sizes["tm"]
        wide = share > 0 and share % 16 == 0 and sizes["tm"] >= 4
        wide = wide and all(size & size - 1 == 0 for size in sizes.values())
        return jax.shard_map(
            fused if wide else shards,
            mesh=mesh,
            in_specs=(
                P("tm", "chan"),
                P(None, None, "chan"),
                P(None, "chan"),
                P(None, None, "chan"),
                P(None, "chan"),
                P(None, "tm", None, None, "chan"),
                P("chan"),
                P(),
                P("chan"),
            ),
            out_specs=P("tm", "chan"),
            check_vma=False,
        )(*arrays)

    return program
```

```python
import functools
import math

import jax
import jax.numpy as jnp
import numpy as np
from jax import lax
from jax.experimental import pallas as pl
from jax.experimental.pallas import tpu as pltpu
from jax.sharding import PartitionSpec as P

MESH = pl.DeviceIdType.MESH


def from_behind(array, axis, by):
    length = lax.axis_size(axis)
    pairs = [(i, i + by) for i in range(length) if 0 <= i + by < length]
    return lax.ppermute(array, axis, pairs)


def partner_2(block, axis, bit):
    count = lax.axis_size(axis)
    route = []
    for low in range(count):
        high = low | 1 << bit
        if high != low and high < count:
            route += [(low, high), (high, low)]
    return lax.ppermute(block, axis, route)


def reverse_bits(values, digits):
    result = jnp.zeros_like(values)
    for bit_level in range(digits):
        result = result | (values >> bit_level & 1) << digits - 1 - bit_level
    return result


def turning(numer, denom):
    angle = numer.astype(jnp.float32) * (-2.0 * math.pi / denom)
    return (jnp.cos(angle), jnp.sin(angle))


def complex_times(stacked, real_part, imag_part):
    return jnp.stack(
        [
            stacked[0] * real_part - stacked[1] * imag_part,
            stacked[0] * imag_part + stacked[1] * real_part,
        ]
    )


def dft_rows(signals, period, inverse):
    indices = jnp.arange(period, dtype=jnp.int32)
    cosine, sine_part = turning(indices[:, None] * indices[None, :] % period, period)
    if inverse:
        sine_part = -sine_part
    stacked = jnp.concatenate([cosine, sine_part], 0)
    result = jnp.einsum("bt,retc->rebc", stacked, signals, precision=lax.Precision.HIGHEST)
    real_out = result[0, :, :period] - result[1, :, period:]
    imag_out = result[1, :, :period] + result[0, :, period:]
    return jnp.stack([real_out, imag_out])


def shards(
    series,
    proj_weight,
    proj_bias,
    short_taps,
    short_bias,
    spectrum,
    skip_gain,
    out_weight,
    out_bias,
):
    steps_dev = series.shape[0]
    model_width = proj_weight.shape[0]
    channels = proj_weight.shape[2]
    flat_weight = proj_weight.reshape(model_width, 3 * channels)
    weight_rows = flat_weight
    projected = jnp.dot(
        lax.all_gather(series, "chan", axis=1, tiled=True),
        weight_rows,
        preferred_element_type=jnp.float32,
    )
    projected = (projected.reshape(steps_dev, 3, channels) + proj_bias).astype(jnp.bfloat16)
    taps_count = short_taps.shape[0]
    earlier = from_behind(projected[steps_dev - taps_count + 1 :], "tm", 1)
    extended = jnp.concatenate([earlier, projected], 0).astype(jnp.float32)
    streams = short_bias + short_taps[0] * extended[taps_count - 1 :]
    for offset in range(1, taps_count):
        streams = (
            streams
            + short_taps[offset]
            * extended[taps_count - 1 - offset : taps_count - 1 - offset + steps_dev]
        )
    streams = lax.optimization_barrier(streams.astype(jnp.bfloat16)).astype(jnp.float32)
    gate_out = streams[:, 0]
    mixed_in = lax.optimization_barrier((streams[:, 1] * streams[:, 2]).astype(jnp.bfloat16))
    signal = mixed_in.astype(jnp.float32)
    tm_count = lax.axis_size("tm")
    digits = tm_count.bit_length() - 1
    own_index = lax.axis_index("tm")
    period = 2 * tm_count * steps_dev
    positions = jnp.arange(steps_dev, dtype=jnp.int32)
    own_rows = 2 * reverse_bits(own_index, digits) + jnp.arange(2, dtype=jnp.int32)
    twist_cos, twist_sin = turning(own_rows[:, None] * positions[None, :] % period, period)
    twist_cos, twist_sin = (twist_cos[:, :, None], twist_sin[:, :, None])
    half_cos, half_sin = turning(own_index, 2 * tm_count)
    zero_field = jnp.zeros_like(signal)
    current = jnp.stack(
        [jnp.stack([signal, signal * half_cos]), jnp.stack([zero_field, signal * half_sin])]
    )
    for bit_level in reversed(range(digits)):
        partner = partner_2(current, "tm", bit_level)
        half_span = 1 << bit_level
        rot_cos, rot_sin = turning(own_index % half_span, 2 * half_span)
        upper_half = own_index >> bit_level & 1 == 1
        current = jnp.where(
            upper_half, complex_times(partner - current, rot_cos, rot_sin), current + partner
        )
    twisted = complex_times(current, twist_cos, twist_sin)
    spectral = dft_rows(twisted, steps_dev, False)
    response = spectrum.reshape(2, 2, steps_dev, channels)
    product = complex_times(spectral, response[0], response[1])
    returned = dft_rows(product, steps_dev, True)
    current = complex_times(returned, twist_cos, -twist_sin)
    for bit_level in range(digits):
        partner = partner_2(current, "tm", bit_level)
        half_span = 1 << bit_level
        rot_cos, rot_sin = turning(own_index % half_span, 2 * half_span)
        rot_sin = -rot_sin
        upper_half = own_index >> bit_level & 1 == 1
        current = jnp.where(
            upper_half,
            partner - complex_times(current, rot_cos, rot_sin),
            current + complex_times(partner, rot_cos, rot_sin),
        )
    convolved = current[0, 0] + half_cos * current[0, 1] + half_sin * current[1, 1]
    convolved = convolved * (1.0 / period)
    gated_rows = ((convolved + skip_gain * signal) * gate_out).astype(jnp.bfloat16)
    column_start = lax.axis_index("chan") * channels
    weight_rows = lax.dynamic_slice_in_dim(out_weight, column_start, channels, 0)
    partial_value = jnp.dot(gated_rows, weight_rows, preferred_element_type=jnp.float32)
    mixed_out = lax.psum_scatter(partial_value, "chan", scatter_dimension=1, tiled=True)
    return (mixed_out + out_bias).astype(jnp.bfloat16)


def make_tables(tm_count, steps):
    count, period = 2 * tm_count, 2 * tm_count * steps
    rows = np.arange(steps)
    angle = 2.0 * np.pi * (rows[:, None] * rows[None, :] % steps) / steps
    dft = np.stack([np.cos(angle), np.sin(angle)]).astype(jnp.bfloat16)
    angle = 2.0 * np.pi * (np.arange(count)[:, None] * rows[None, :] % period) / period
    twist = np.stack([np.cos(angle), np.sin(angle)]).astype(np.float32)
    return dft, twist


def flip(value, digits):
    result = 0
    for bit_level in range(digits):
        result |= (value >> bit_level & 1) << digits - 1 - bit_level
    return result


def across_bits(index, by):
    result, bit = index, 1
    while bit <= by:
        if by & bit:
            result = result + bit * (1 - 2 * lax.rem(lax.div(index, bit), 2))
        bit *= 2
    return result


def weighted(blocks, weights):
    total = None
    for block, weight in zip(blocks, weights):
        if abs(weight) < 1e-12:
            continue
        if abs(weight - 1.0) < 1e-12:
            term = block
        elif abs(weight + 1.0) < 1e-12:
            term = -block
        else:
            term = block * float(weight)
        total = term if total is None else total + term
    return total


def kernel(
    tm_count,
    chan_count,
    series,
    weight,
    proj_bias,
    taps,
    short_bias,
    spectrum,
    skip_gain,
    out_weight,
    out_bias,
    dft,
    twist,
    out,
    rows_in,
    weight_v,
    proj_bias_v,
    taps_v,
    short_bias_v,
    spectrum_v,
    skip_v,
    out_weight_v,
    out_weight_t,
    out_bias_v,
    dft_v,
    twist_v,
    projected,
    spec_out,
    spec_in,
    mixed_out,
    mixed_in,
    wave,
    conv_out,
    conv_in,
    gate_t,
    direct_t,
    gated,
    local_sem,
    rows_send,
    rows_recv,
    halo_send,
    halo_recv,
    spec_send,
    spec_recv,
    mix_send,
    mix_recv,
    conv_send,
    conv_recv,
    gate_send,
    gate_recv,
):
    steps, channels = series.shape
    halo = rows_in.shape[0] - steps
    share = channels // tm_count
    digits = tm_count.bit_length() - 1
    slots = 2 * tm_count
    own_t, own_c = lax.axis_index("tm"), lax.axis_index("chan")
    columns = lambda c: pl.ds(pl.multiple_of(c * channels, channels), channels)
    next_t, last_t = lax.rem(own_t + 1, tm_count), lax.rem(own_t + tm_count - 1, tm_count)
    tm_peer = lambda by: across_bits(own_t, by)
    chan_peer = lambda by: across_bits(own_c, by)
    far_first = list(range(tm_count // 2, tm_count)) + list(range(1, tm_count // 2))

    barrier = pltpu.get_barrier_semaphore()
    greet = lambda where: pl.semaphore_signal(barrier, inc=1, device_id=where, device_id_type=MESH)
    for by in range(1, chan_count):
        greet({"chan": chan_peer(by)})
    for by in range(1, tm_count):
        greet({"tm": tm_peer(by)})
    for by in range(1, chan_count):
        greet({"tm": next_t, "chan": chan_peer(by)})
        greet({"tm": last_t, "chan": chan_peer(by)})

    pairs = [
        (series, rows_in.at[pl.ds(halo, steps), columns(own_c)]),
        (spectrum.at[:, 0], spectrum_v),
        *[(weight.at[j], weight_v.at[:, pl.ds(j * channels, channels)]) for j in range(3)],
        (proj_bias, proj_bias_v),
        (taps, taps_v),
        (short_bias, short_bias_v),
        (dft, dft_v),
        (twist, twist_v),
        (skip_gain, skip_v),
        (out_weight.at[:, columns(own_c)], out_weight_v),
        (out_bias, out_bias_v),
    ]
    local = [pltpu.make_async_copy(a, b, local_sem.at[i]) for i, (a, b) in enumerate(pairs)]
    for copy in local:
        copy.start()
    own_rows = rows_in.at[pl.ds(halo, steps), columns(own_c)]

    def remote(src, dst, send, recv, where):
        return pltpu.make_async_remote_copy(
            src_ref=src, dst_ref=dst, send_sem=send, recv_sem=recv, device_id=where, device_id_type=MESH
        )

    residue = 2 * sum((own_t >> i & 1) << digits - 1 - i for i in range(digits))
    down = lax.broadcasted_iota(jnp.int32, (steps, steps), 0)
    across = lax.broadcasted_iota(jnp.int32, (steps, steps), 1)

    def turn_spectrum(parity):
        wanted = jnp.where(residue + parity > tm_count, steps - 1 - down, down)
        order = jnp.where(wanted == across, 1.0 / (slots * steps), 0.0).astype(jnp.bfloat16)
        for part in range(2):
            block = spectrum_v[part, parity].astype(jnp.bfloat16)
            block = jnp.dot(order, block, preferred_element_type=jnp.float32).T
            spec_out[parity, :, part] = block.astype(jnp.bfloat16).reshape(tm_count, share, steps)

    local[1].wait()
    turn_spectrum(0)
    local[0].wait()
    pl.semaphore_wait(barrier, chan_count - 1 + tm_count - 1 + 2 * (chan_count - 1))

    core_c, x_c, far_c = chan_peer(1), chan_peer(2), chan_peer(3)
    part_rows = steps // 2

    def rows_copy(owner, first, count, recv, to):
        block = rows_in.at[pl.ds(halo + first, count), columns(owner)]
        return remote(block, block, rows_send.at[0], rows_recv.at[recv], {"chan": to})

    def halo_copy(by, owner):
        return remote(
            rows_in.at[pl.ds(steps, halo), columns(own_c)],
            rows_in.at[pl.ds(0, halo), columns(owner)],
            halo_send.at[0],
            halo_recv.at[0],
            {"tm": next_t, "chan": chan_peer(by)},
        )

    for i in range(2):
        rows_copy(own_c, i * part_rows, part_rows, i, x_c).start()
    rows_copy(own_c, 0, steps, 2, core_c).start()

    @pl.when(own_t < tm_count - 1)
    def _():
        for by in range(chan_count):
            halo_copy(by, own_c).start()

    @pl.when(own_t == 0)
    def _():
        rows_in[pl.ds(0, halo), :] = jnp.zeros((halo, rows_in.shape[1]), rows_in.dtype)

    def bytes_of(ref, sem):
        pltpu.make_async_copy(ref, ref, sem).wait()

    def spread(src, dst, send, recv):
        for by in far_first:
            remote(src.at[tm_peer(by)], dst.at[own_t], send, recv, {"tm": tm_peer(by)}).start()
        dst[own_t] = src[own_t]

    def collect(dst, recv):
        bytes_of(dst.at[pl.ds(0, tm_count - 1)], recv)

    spread(spec_out.at[0], spec_in.at[0], spec_send.at[0], spec_recv.at[0])
    turn_spectrum(1)
    spread(spec_out.at[1], spec_in.at[1], spec_send.at[1], spec_recv.at[1])

    for i in range(2):
        bytes_of(rows_in.at[pl.ds(halo, part_rows), columns(x_c)], rows_recv.at[i])
        rows_copy(x_c, i * part_rows, part_rows, 3, core_c).start()
    for copy in local[2:]:
        copy.wait()
    others = pl.ds(0, (chan_count - 1) * channels)

    @pl.when(own_t > 0)
    def _():
        bytes_of(rows_in.at[pl.ds(0, halo)], halo_recv.at[0])

    bytes_of(rows_in.at[pl.ds(halo, steps), columns(core_c)], rows_recv.at[2])

    def of_chip(chip):
        inputs = pl.ds(pl.multiple_of(chip * 2 * channels, 2 * channels), 2 * channels)
        return jnp.dot(rows_in[:, inputs], weight_v[inputs, :], preferred_element_type=jnp.float32)

    own_chip = lax.div(own_c, 2)
    near_sum = of_chip(own_chip)
    bytes_of(rows_in.at[pl.ds(halo, steps), columns(far_c)], rows_recv.at[3])
    sums = near_sum + of_chip(1 - own_chip)

    streams = []
    for j in (1, 2, 0):
        value = sums[:, j * channels : (j + 1) * channels]
        value = (value + proj_bias_v[j : j + 1]).astype(jnp.bfloat16).astype(jnp.float32)
        projected[j] = value

        @pl.when(own_t == 0)
        def _():
            projected[j, pl.ds(0, halo)] = jnp.zeros((halo, channels), jnp.float32)

        stream = short_bias_v[j : j + 1] + taps_v[0, j : j + 1] * projected[j, pl.ds(halo, steps)]
        for k in range(1, taps.shape[0]):
            stream = stream + taps_v[k, j : j + 1] * projected[j, pl.ds(halo - k, steps)]
        stream = stream.astype(jnp.bfloat16).astype(jnp.float32)
        if j == 2:
            signal = (streams[0] * stream).astype(jnp.bfloat16).astype(jnp.float32)
            mixed_out[...] = signal.T.astype(jnp.bfloat16).reshape(tm_count, share, steps)
            spread(mixed_out, mixed_in, mix_send.at[0], mix_recv.at[0])
        streams.append(stream)
    gate_t[...] = streams[2].T.reshape(tm_count, share, steps)
    direct_t[...] = (skip_v[...] * signal).T.reshape(tm_count, share, steps)
    near = tm_count // 2
    for half in range(2):
        blocks = [
            out_weight_v[pl.ds(pl.multiple_of(c * channels + tm_peer(half * near + by) * share, share), share)]
            for c in range(chan_count)
            for by in range(near)
        ]
        out_weight_t[half] = jnp.concatenate(blocks, 0).astype(jnp.float32).T.astype(jnp.bfloat16)

    collect(mixed_in, mix_recv.at[0])
    blocks = [mixed_in[b].astype(jnp.float32) for b in range(tm_count)]
    turns = 2.0 * np.pi * np.arange(slots) / slots
    cosine = lambda r, b: math.cos(turns[r * b % slots])
    sine = lambda r, b: math.sin(turns[r * b % slots])
    kept = tm_count + 1

    for r in range(kept):
        real = weighted(blocks, [cosine(r, b) for b in range(tm_count)])
        imag = weighted(blocks, [-sine(r, b) for b in range(tm_count)])
        cos_row, sin_row = twist_v[0, r : r + 1], twist_v[1, r : r + 1]
        if imag is None:
            turned = (real * cos_row, -(real * sin_row))
        else:
            turned = (real * cos_row + imag * sin_row, imag * cos_row - real * sin_row)
        for part in range(2):
            wave[part, r] = turned[part].astype(jnp.bfloat16)

    def within():
        rows = wave[...].reshape(2 * kept * share, steps)
        first = jnp.dot(rows, dft_v[0], preferred_element_type=jnp.float32)
        second = jnp.dot(rows, dft_v[1], preferred_element_type=jnp.float32)
        half = kept * share
        return [a.reshape(kept, share, steps) for a in (first[:half], first[half:], second[:half], second[half:])]

    real_cos, imag_cos, real_sin, imag_sin = within()
    real, imag = real_cos + imag_sin, imag_cos - real_sin
    for parity in range(2):
        collect(spec_in.at[parity], spec_recv.at[parity])

    def filter_of(part, r):
        return spec_in[r % 2, flip(r // 2, digits), part].astype(jnp.float32)

    for r in range(kept):
        filter_real, filter_imag = filter_of(0, r), filter_of(1, r)
        if 0 < r < tm_count:
            filter_real = filter_real + filter_of(0, slots - r)
            filter_imag = filter_imag - filter_of(1, slots - r)
        wave[0, r] = (real[r] * filter_real - imag[r] * filter_imag).astype(jnp.bfloat16)
        wave[1, r] = (real[r] * filter_imag + imag[r] * filter_real).astype(jnp.bfloat16)
    real_cos, imag_cos, real_sin, imag_sin = within()
    real, imag = real_cos - imag_sin, real_sin + imag_cos

    terms = []
    for r in range(kept):
        cos_row, sin_row = twist_v[0, r : r + 1], twist_v[1, r : r + 1]
        terms.append(real[r] * cos_row - imag[r] * sin_row)
    for r in range(kept):
        cos_row, sin_row = twist_v[0, r : r + 1], twist_v[1, r : r + 1]
        terms.append(real[r] * sin_row + imag[r] * cos_row)
    for b in range(tm_count):
        weights = [cosine(r, b) for r in range(kept)] + [-sine(r, b) for r in range(kept)]
        conv_out[b] = weighted(terms, weights).astype(jnp.bfloat16)
    for by in far_first:
        half = by // near
        remote(
            conv_out.at[tm_peer(by)], conv_in.at[by], conv_send.at[0], conv_recv.at[half], {"tm": tm_peer(by)}
        ).start()

    bytes_of(rows_in.at[pl.ds(halo, steps), others], rows_send.at[0])

    @pl.when(own_t < tm_count - 1)
    def _():
        bytes_of(rows_in.at[pl.ds(0, halo)], halo_send.at[0])

    for parity in range(2):
        collect(spec_in.at[parity], spec_send.at[parity])
    bytes_of(mixed_in.at[pl.ds(0, tm_count - 1)], mix_send.at[0])

    def gate_copy(half, owner, recv, to):
        block = gated.at[half, owner]
        return remote(block, block, gate_send.at[half], gate_recv.at[half, recv], {"chan": to})

    for half in range(2):
        if half == 0:
            bytes_of(conv_in.at[pl.ds(0, near - 1)], conv_recv.at[0])
        else:
            bytes_of(conv_in.at[pl.ds(0, near)], conv_recv.at[1])
        for by in range(half * near, (half + 1) * near):
            source = tm_peer(by)
            arrived = conv_in[by] if by else conv_out[source]
            value = (arrived.astype(jnp.float32) + direct_t[source]) * gate_t[source]
            gated[half, own_c, pl.ds(by % near * share, share)] = value.astype(jnp.bfloat16)
        gate_copy(half, own_c, 0, x_c).start()
        gate_copy(half, own_c, 1, core_c).start()
    for half in range(2):
        bytes_of(gated.at[half, x_c], gate_recv.at[half, 0])
        gate_copy(half, x_c, 2, core_c).start()

    total = None
    for half in range(2):
        bytes_of(gated.at[half, core_c], gate_recv.at[half, 1])
        bytes_of(gated.at[half, far_c], gate_recv.at[half, 2])
        rows = gated[half].reshape(chan_count * channels // 2, steps)
        term = jnp.dot(out_weight_t[half], rows, preferred_element_type=jnp.float32)
        total = term if total is None else total + term
    out[...] = (total.T + out_bias_v[...]).astype(out.dtype)

    bytes_of(conv_in.at[pl.ds(0, tm_count - 1)], conv_send.at[0])
    for half in range(2):
        bytes_of(gated.at[half, pl.ds(0, chan_count - 1)], gate_send.at[half])


def fused(
    series,
    proj_weight,
    proj_bias,
    short_taps,
    short_bias,
    spectrum,
    skip_gain,
    out_weight,
    out_bias,
):
    steps, channels = series.shape
    width = proj_weight.shape[0]
    tm_count, chan_count = lax.axis_size("tm"), lax.axis_size("chan")
    dft, twist = make_tables(tm_count, steps)
    share, slots, halo = channels // tm_count, 2 * tm_count, 16
    spread_shape = (tm_count, share, steps)
    vmem, dma = pltpu.VMEM, pltpu.SemaphoreType.DMA
    operands = [
        series,
        proj_weight.transpose(1, 0, 2),
        proj_bias,
        short_taps,
        short_bias,
        spectrum,
        skip_gain.reshape(1, channels),
        out_weight,
        out_bias.reshape(1, channels),
        jnp.asarray(dft),
        jnp.asarray(twist),
    ]
    return pl.pallas_call(
        functools.partial(kernel, tm_count, chan_count),
        out_shape=jax.ShapeDtypeStruct((steps, channels), jnp.bfloat16),
        in_specs=[pl.BlockSpec(memory_space=pl.ANY)] * len(operands),
        out_specs=pl.BlockSpec(memory_space=pltpu.VMEM),
        scratch_shapes=[
            vmem((halo + steps, width), jnp.bfloat16),
            vmem((width, 3 * channels), jnp.bfloat16),
            vmem(proj_bias.shape, jnp.float32),
            vmem(short_taps.shape, jnp.float32),
            vmem(short_bias.shape, jnp.float32),
            vmem((2, 2, steps, channels), jnp.float32),
            vmem((1, channels), jnp.float32),
            vmem((width, channels), jnp.bfloat16),
            vmem((2, channels, width // 2), jnp.bfloat16),
            vmem((1, channels), jnp.float32),
            vmem(dft.shape, jnp.bfloat16),
            vmem(twist.shape, jnp.float32),
            vmem((3, halo + steps, channels), jnp.float32),
            vmem((2, tm_count, 2, share, steps), jnp.bfloat16),
            vmem((2, tm_count, 2, share, steps), jnp.bfloat16),
            vmem(spread_shape, jnp.bfloat16),
            vmem(spread_shape, jnp.bfloat16),
            vmem((2, tm_count + 1, share, steps), jnp.bfloat16),
            vmem(spread_shape, jnp.bfloat16),
            vmem(spread_shape, jnp.bfloat16),
            vmem(spread_shape, jnp.float32),
            vmem(spread_shape, jnp.float32),
            vmem((2, chan_count, channels // 2, steps), jnp.bfloat16),
            dma((len(operands) + 2,)),
            dma((1,)),
            dma((4,)),
            *[dma((2,))] * 9,
            dma((2, 3)),
        ],
        compiler_params=pltpu.CompilerParams(
            collective_id=0, has_side_effects=True, vmem_limit_bytes=32 * 1024 * 1024
        ),
    )(*[pltpu.with_memory_space_constraint(operand, pltpu.HBM) for operand in operands])


def solution(mesh):
    sizes = mesh.shape

    def program(*arrays):
        share = arrays[0].shape[1] // sizes["chan"] // sizes["tm"]
        wide = share > 0 and share % 16 == 0 and sizes["tm"] >= 4 and sizes["chan"] == 4
        wide = wide and sizes["tm"] & sizes["tm"] - 1 == 0
        return jax.shard_map(
            fused if wide else shards,
            mesh=mesh,
            in_specs=(
                P("tm", "chan"),
                P(None, None, "chan"),
                P(None, "chan"),
                P(None, None, "chan"),
                P(None, "chan"),
                P(None, "tm", None, None, "chan"),
                P("chan"),
                P(),
                P("chan"),
            ),
            out_specs=P("tm", "chan"),
            check_vma=False,
        )(*arrays)

    return program
```

```python
import functools
import math

import jax
import jax.numpy as jnp
import numpy as np
from jax import lax
from jax.experimental import pallas as pl
from jax.experimental.pallas import tpu as pltpu
from jax.sharding import PartitionSpec as P

MESH = pl.DeviceIdType.MESH


def from_behind(array, axis, by):
    length = lax.axis_size(axis)
    pairs = [(i, i + by) for i in range(length) if 0 <= i + by < length]
    return lax.ppermute(array, axis, pairs)


def partner_2(block, axis, bit):
    count = lax.axis_size(axis)
    route = []
    for low in range(count):
        high = low | 1 << bit
        if high != low and high < count:
            route += [(low, high), (high, low)]
    return lax.ppermute(block, axis, route)


def reverse_bits(values, digits):
    result = jnp.zeros_like(values)
    for bit_level in range(digits):
        result = result | (values >> bit_level & 1) << digits - 1 - bit_level
    return result


def turning(numer, denom):
    angle = numer.astype(jnp.float32) * (-2.0 * math.pi / denom)
    return (jnp.cos(angle), jnp.sin(angle))


def complex_times(stacked, real_part, imag_part):
    return jnp.stack(
        [
            stacked[0] * real_part - stacked[1] * imag_part,
            stacked[0] * imag_part + stacked[1] * real_part,
        ]
    )


def dft_rows(signals, period, inverse):
    indices = jnp.arange(period, dtype=jnp.int32)
    cosine, sine_part = turning(indices[:, None] * indices[None, :] % period, period)
    if inverse:
        sine_part = -sine_part
    stacked = jnp.concatenate([cosine, sine_part], 0)
    result = jnp.einsum("bt,retc->rebc", stacked, signals, precision=lax.Precision.HIGHEST)
    real_out = result[0, :, :period] - result[1, :, period:]
    imag_out = result[1, :, :period] + result[0, :, period:]
    return jnp.stack([real_out, imag_out])


def shards(
    series,
    proj_weight,
    proj_bias,
    short_taps,
    short_bias,
    spectrum,
    skip_gain,
    out_weight,
    out_bias,
):
    steps_dev = series.shape[0]
    model_width = proj_weight.shape[0]
    channels = proj_weight.shape[2]
    flat_weight = proj_weight.reshape(model_width, 3 * channels)
    weight_rows = flat_weight
    projected = jnp.dot(
        lax.all_gather(series, "chan", axis=1, tiled=True),
        weight_rows,
        preferred_element_type=jnp.float32,
    )
    projected = (projected.reshape(steps_dev, 3, channels) + proj_bias).astype(jnp.bfloat16)
    taps_count = short_taps.shape[0]
    earlier = from_behind(projected[steps_dev - taps_count + 1 :], "tm", 1)
    extended = jnp.concatenate([earlier, projected], 0).astype(jnp.float32)
    streams = short_bias + short_taps[0] * extended[taps_count - 1 :]
    for offset in range(1, taps_count):
        streams = (
            streams
            + short_taps[offset]
            * extended[taps_count - 1 - offset : taps_count - 1 - offset + steps_dev]
        )
    streams = lax.optimization_barrier(streams.astype(jnp.bfloat16)).astype(jnp.float32)
    gate_out = streams[:, 0]
    mixed_in = lax.optimization_barrier((streams[:, 1] * streams[:, 2]).astype(jnp.bfloat16))
    signal = mixed_in.astype(jnp.float32)
    tm_count = lax.axis_size("tm")
    digits = tm_count.bit_length() - 1
    own_index = lax.axis_index("tm")
    period = 2 * tm_count * steps_dev
    positions = jnp.arange(steps_dev, dtype=jnp.int32)
    own_rows = 2 * reverse_bits(own_index, digits) + jnp.arange(2, dtype=jnp.int32)
    twist_cos, twist_sin = turning(own_rows[:, None] * positions[None, :] % period, period)
    twist_cos, twist_sin = (twist_cos[:, :, None], twist_sin[:, :, None])
    half_cos, half_sin = turning(own_index, 2 * tm_count)
    zero_field = jnp.zeros_like(signal)
    current = jnp.stack(
        [jnp.stack([signal, signal * half_cos]), jnp.stack([zero_field, signal * half_sin])]
    )
    for bit_level in reversed(range(digits)):
        partner = partner_2(current, "tm", bit_level)
        half_span = 1 << bit_level
        rot_cos, rot_sin = turning(own_index % half_span, 2 * half_span)
        upper_half = own_index >> bit_level & 1 == 1
        current = jnp.where(
            upper_half, complex_times(partner - current, rot_cos, rot_sin), current + partner
        )
    twisted = complex_times(current, twist_cos, twist_sin)
    spectral = dft_rows(twisted, steps_dev, False)
    response = spectrum.reshape(2, 2, steps_dev, channels)
    product = complex_times(spectral, response[0], response[1])
    returned = dft_rows(product, steps_dev, True)
    current = complex_times(returned, twist_cos, -twist_sin)
    for bit_level in range(digits):
        partner = partner_2(current, "tm", bit_level)
        half_span = 1 << bit_level
        rot_cos, rot_sin = turning(own_index % half_span, 2 * half_span)
        rot_sin = -rot_sin
        upper_half = own_index >> bit_level & 1 == 1
        current = jnp.where(
            upper_half,
            partner - complex_times(current, rot_cos, rot_sin),
            current + complex_times(partner, rot_cos, rot_sin),
        )
    convolved = current[0, 0] + half_cos * current[0, 1] + half_sin * current[1, 1]
    convolved = convolved * (1.0 / period)
    gated_rows = ((convolved + skip_gain * signal) * gate_out).astype(jnp.bfloat16)
    column_start = lax.axis_index("chan") * channels
    weight_rows = lax.dynamic_slice_in_dim(out_weight, column_start, channels, 0)
    partial_value = jnp.dot(gated_rows, weight_rows, preferred_element_type=jnp.float32)
    mixed_out = lax.psum_scatter(partial_value, "chan", scatter_dimension=1, tiled=True)
    return (mixed_out + out_bias).astype(jnp.bfloat16)


def make_tables(tm_count, steps):
    count, period = 2 * tm_count, 2 * tm_count * steps
    rows = np.arange(steps)
    angle = 2.0 * np.pi * (rows[:, None] * rows[None, :] % steps) / steps
    dft = np.stack([np.cos(angle), np.sin(angle)]).astype(jnp.bfloat16)
    angle = 2.0 * np.pi * (np.arange(count)[:, None] * rows[None, :] % period) / period
    twist = np.stack([np.cos(angle), np.sin(angle)]).astype(np.float32)
    return dft, twist


def flip(value, digits):
    result = 0
    for bit_level in range(digits):
        result |= (value >> bit_level & 1) << digits - 1 - bit_level
    return result


def across_bits(index, by):
    result, bit = index, 1
    while bit <= by:
        if by & bit:
            result = result + bit * (1 - 2 * lax.rem(lax.div(index, bit), 2))
        bit *= 2
    return result


def weighted(blocks, weights):
    total = None
    for block, weight in zip(blocks, weights):
        if abs(weight) < 1e-12:
            continue
        if abs(weight - 1.0) < 1e-12:
            term = block
        elif abs(weight + 1.0) < 1e-12:
            term = -block
        else:
            term = block * float(weight)
        total = term if total is None else total + term
    return total


def kernel(
    tm_count,
    chan_count,
    series,
    weight,
    proj_bias,
    taps,
    short_bias,
    spectrum,
    skip_gain,
    out_weight,
    out_bias,
    dft,
    twist,
    out,
    rows_in,
    weight_v,
    proj_bias_v,
    taps_v,
    short_bias_v,
    spectrum_v,
    skip_v,
    out_weight_v,
    out_weight_t,
    out_bias_v,
    dft_v,
    twist_v,
    projected,
    spec_out,
    spec_in,
    mixed_out,
    mixed_in,
    wave,
    conv_out,
    conv_in,
    gate_t,
    direct_t,
    gated,
    local_sem,
    rows_send,
    rows_recv,
    halo_send,
    halo_recv,
    spec_send,
    spec_recv,
    mix_send,
    mix_recv,
    conv_send,
    conv_recv,
    gate_send,
    gate_recv,
):
    steps, channels = series.shape
    halo = rows_in.shape[0] - steps
    share = channels // tm_count
    digits = tm_count.bit_length() - 1
    slots = 2 * tm_count
    own_t, own_c = lax.axis_index("tm"), lax.axis_index("chan")
    columns = lambda c: pl.ds(pl.multiple_of(c * channels, channels), channels)
    next_t, last_t = lax.rem(own_t + 1, tm_count), lax.rem(own_t + tm_count - 1, tm_count)
    tm_peer = lambda by: across_bits(own_t, by)
    chan_peer = lambda by: across_bits(own_c, by)
    far_first = list(range(tm_count // 2, tm_count)) + list(range(1, tm_count // 2))

    barrier = pltpu.get_barrier_semaphore()
    greet = lambda where: pl.semaphore_signal(barrier, inc=1, device_id=where, device_id_type=MESH)
    for by in range(1, chan_count):
        greet({"chan": chan_peer(by)})
    for by in range(1, tm_count):
        greet({"tm": tm_peer(by)})
    for by in range(1, chan_count):
        greet({"tm": next_t, "chan": chan_peer(by)})
        greet({"tm": last_t, "chan": chan_peer(by)})

    pairs = [
        (series, rows_in.at[pl.ds(halo, steps), columns(own_c)]),
        (spectrum.at[:, 0], spectrum_v),
        *[(weight.at[j], weight_v.at[:, pl.ds((j + 2) % 3 * channels, channels)]) for j in range(3)],
        (proj_bias, proj_bias_v),
        (taps, taps_v),
        (short_bias, short_bias_v),
        (dft, dft_v),
        (twist, twist_v),
        (skip_gain, skip_v),
        (out_weight.at[:, columns(own_c)], out_weight_v),
        (out_bias, out_bias_v),
    ]
    local = [pltpu.make_async_copy(a, b, local_sem.at[i]) for i, (a, b) in enumerate(pairs)]
    for copy in local:
        copy.start()

    def remote(src, dst, send, recv, where):
        return pltpu.make_async_remote_copy(
            src_ref=src, dst_ref=dst, send_sem=send, recv_sem=recv, device_id=where, device_id_type=MESH
        )

    residue = 2 * sum((own_t >> i & 1) << digits - 1 - i for i in range(digits))
    down = lax.broadcasted_iota(jnp.int32, (steps, steps), 0)
    across = lax.broadcasted_iota(jnp.int32, (steps, steps), 1)

    def turn_spectrum(parity):
        wanted = jnp.where(residue + parity > tm_count, steps - 1 - down, down)
        order = jnp.where(wanted == across, 1.0 / (slots * steps), 0.0).astype(jnp.bfloat16)
        for part in range(2):
            block = spectrum_v[part, parity].astype(jnp.bfloat16)
            block = jnp.dot(order, block, preferred_element_type=jnp.float32).T
            spec_out[parity, :, part] = block.astype(jnp.bfloat16).reshape(tm_count, share, steps)

    early = own_t < tm_count // 2

    @pl.when(early)
    def _():
        local[1].wait()
        turn_spectrum(0)
        turn_spectrum(1)

    pl.semaphore_wait(barrier, chan_count - 1 + tm_count - 1 + 2 * (chan_count - 1))

    core_c, x_c, far_c = chan_peer(1), chan_peer(2), chan_peer(3)
    part_rows = steps // 2

    def rows_copy(owner, first, count, recv, to):
        block = rows_in.at[pl.ds(halo + first, count), columns(owner)]
        source = series.at[pl.ds(first, count)] if owner is own_c else block
        return remote(source, block, rows_send.at[0], rows_recv.at[recv], {"chan": to})

    def halo_copy(by, owner):
        return remote(
            series.at[pl.ds(steps - halo, halo)],
            rows_in.at[pl.ds(0, halo), columns(owner)],
            halo_send.at[0],
            halo_recv.at[0],
            {"tm": next_t, "chan": chan_peer(by)},
        )

    for i in range(2):
        rows_copy(own_c, i * part_rows, part_rows, i, x_c).start()
    rows_copy(own_c, 0, steps, 2, core_c).start()

    @pl.when(own_t < tm_count - 1)
    def _():
        for by in range(chan_count):
            halo_copy(by, own_c).start()

    @pl.when(own_t == 0)
    def _():
        rows_in[pl.ds(0, halo), :] = jnp.zeros((halo, rows_in.shape[1]), rows_in.dtype)

    def bytes_of(ref, sem):
        pltpu.make_async_copy(ref, ref, sem).wait()

    def spread(src, dst, send, recv):
        for by in far_first:
            remote(src.at[tm_peer(by)], dst.at[own_t], send, recv, {"tm": tm_peer(by)}).start()
        dst[own_t] = src[own_t]

    def collect(dst, recv):
        bytes_of(dst.at[pl.ds(0, tm_count - 1)], recv)

    def spread_spectrum(parity):
        spread(spec_out.at[parity], spec_in.at[parity], spec_send.at[parity], spec_recv.at[parity])

    @pl.when(early)
    def _():
        spread_spectrum(0)
        spread_spectrum(1)

    @pl.when(jnp.logical_not(early))
    def _():
        local[1].wait()
        for parity in range(2):
            turn_spectrum(parity)
            spread_spectrum(parity)


    for i in range(2):
        bytes_of(rows_in.at[pl.ds(halo, part_rows), columns(x_c)], rows_recv.at[i])
        rows_copy(x_c, i * part_rows, part_rows, 3, core_c).start()
    local[0].wait()
    for copy in local[2:]:
        copy.wait()
    others = pl.ds(0, (chan_count - 1) * channels)

    @pl.when(own_t > 0)
    def _():
        bytes_of(rows_in.at[pl.ds(0, halo)], halo_recv.at[0])

    bytes_of(rows_in.at[pl.ds(halo, steps), columns(core_c)], rows_recv.at[2])

    def of_chip(chip):
        inputs = pl.ds(pl.multiple_of(chip * 2 * channels, 2 * channels), 2 * channels)
        return jnp.dot(
            rows_in[:, inputs], weight_v[inputs, pl.ds(0, 2 * channels)], preferred_element_type=jnp.float32
        )

    own_chip = lax.div(own_c, 2)
    near_sum = of_chip(own_chip)
    bytes_of(rows_in.at[pl.ds(halo, steps), columns(far_c)], rows_recv.at[3])
    sums = near_sum + of_chip(1 - own_chip)

    streams = []
    for j in (1, 2, 0):
        if j:
            value = sums[:, (j - 1) * channels : j * channels]
        else:
            value = jnp.dot(
                rows_in[...], weight_v[:, pl.ds(2 * channels, channels)], preferred_element_type=jnp.float32
            )
        value = (value + proj_bias_v[j : j + 1]).astype(jnp.bfloat16).astype(jnp.float32)
        projected[j] = value

        @pl.when(own_t == 0)
        def _():
            projected[j, pl.ds(0, halo)] = jnp.zeros((halo, channels), jnp.float32)

        stream = short_bias_v[j : j + 1] + taps_v[0, j : j + 1] * projected[j, pl.ds(halo, steps)]
        for k in range(1, taps.shape[0]):
            stream = stream + taps_v[k, j : j + 1] * projected[j, pl.ds(halo - k, steps)]
        stream = stream.astype(jnp.bfloat16).astype(jnp.float32)
        if j == 2:
            signal = (streams[0] * stream).astype(jnp.bfloat16).astype(jnp.float32)
            mixed_out[...] = signal.T.astype(jnp.bfloat16).reshape(tm_count, share, steps)
            spread(mixed_out, mixed_in, mix_send.at[0], mix_recv.at[0])
        streams.append(stream)
    gate_t[...] = streams[2].T.reshape(tm_count, share, steps)
    direct_t[...] = (skip_v[...] * signal).T.reshape(tm_count, share, steps)
    near = tm_count // 2
    for half in range(2):
        blocks = [
            out_weight_v[pl.ds(pl.multiple_of(c * channels + tm_peer(half * near + by) * share, share), share)]
            for c in range(chan_count)
            for by in range(near)
        ]
        out_weight_t[half] = jnp.concatenate(blocks, 0).astype(jnp.float32).T.astype(jnp.bfloat16)

    collect(mixed_in, mix_recv.at[0])
    blocks = [mixed_in[b].astype(jnp.float32) for b in range(tm_count)]
    turns = 2.0 * np.pi * np.arange(slots) / slots
    cosine = lambda r, b: math.cos(turns[r * b % slots])
    sine = lambda r, b: math.sin(turns[r * b % slots])
    kept = tm_count + 1

    for r in range(kept):
        real = weighted(blocks, [cosine(r, b) for b in range(tm_count)])
        imag = weighted(blocks, [-sine(r, b) for b in range(tm_count)])
        cos_row, sin_row = twist_v[0, r : r + 1], twist_v[1, r : r + 1]
        if imag is None:
            turned = (real * cos_row, -(real * sin_row))
        else:
            turned = (real * cos_row + imag * sin_row, imag * cos_row - real * sin_row)
        for part in range(2):
            wave[part, r] = turned[part].astype(jnp.bfloat16)

    def within():
        rows = wave[...].reshape(2 * kept * share, steps)
        first = jnp.dot(rows, dft_v[0], preferred_element_type=jnp.float32)
        second = jnp.dot(rows, dft_v[1], preferred_element_type=jnp.float32)
        half = kept * share
        return [a.reshape(kept, share, steps) for a in (first[:half], first[half:], second[:half], second[half:])]

    real_cos, imag_cos, real_sin, imag_sin = within()
    real, imag = real_cos + imag_sin, imag_cos - real_sin
    for parity in range(2):
        collect(spec_in.at[parity], spec_recv.at[parity])

    def filter_of(part, r):
        return spec_in[r % 2, flip(r // 2, digits), part].astype(jnp.float32)

    for r in range(kept):
        filter_real, filter_imag = filter_of(0, r), filter_of(1, r)
        if 0 < r < tm_count:
            filter_real = filter_real + filter_of(0, slots - r)
            filter_imag = filter_imag - filter_of(1, slots - r)
        wave[0, r] = (real[r] * filter_real - imag[r] * filter_imag).astype(jnp.bfloat16)
        wave[1, r] = (real[r] * filter_imag + imag[r] * filter_real).astype(jnp.bfloat16)
    real_cos, imag_cos, real_sin, imag_sin = within()
    real, imag = real_cos - imag_sin, real_sin + imag_cos

    terms = []
    for r in range(kept):
        cos_row, sin_row = twist_v[0, r : r + 1], twist_v[1, r : r + 1]
        terms.append(real[r] * cos_row - imag[r] * sin_row)
    for r in range(kept):
        cos_row, sin_row = twist_v[0, r : r + 1], twist_v[1, r : r + 1]
        terms.append(real[r] * sin_row + imag[r] * cos_row)
    for b in range(tm_count):
        weights = [cosine(r, b) for r in range(kept)] + [-sine(r, b) for r in range(kept)]
        conv_out[b] = weighted(terms, weights).astype(jnp.bfloat16)
    for by in far_first:
        half = by // near
        remote(
            conv_out.at[tm_peer(by)], conv_in.at[by], conv_send.at[0], conv_recv.at[half], {"tm": tm_peer(by)}
        ).start()

    bytes_of(rows_in.at[pl.ds(halo, steps), others], rows_send.at[0])

    @pl.when(own_t < tm_count - 1)
    def _():
        bytes_of(rows_in.at[pl.ds(0, halo)], halo_send.at[0])

    for parity in range(2):
        collect(spec_in.at[parity], spec_send.at[parity])
    bytes_of(mixed_in.at[pl.ds(0, tm_count - 1)], mix_send.at[0])

    def gate_copy(half, owner, recv, to):
        block = gated.at[half, owner]
        return remote(block, block, gate_send.at[half], gate_recv.at[half, recv], {"chan": to})

    for half in range(2):
        if half == 0:
            bytes_of(conv_in.at[pl.ds(0, near - 1)], conv_recv.at[0])
        else:
            bytes_of(conv_in.at[pl.ds(0, near)], conv_recv.at[1])
        for by in range(half * near, (half + 1) * near):
            source = tm_peer(by)
            arrived = conv_in[by] if by else conv_out[source]
            value = (arrived.astype(jnp.float32) + direct_t[source]) * gate_t[source]
            gated[half, own_c, pl.ds(by % near * share, share)] = value.astype(jnp.bfloat16)
        gate_copy(half, own_c, 0, x_c).start()
        gate_copy(half, own_c, 1, core_c).start()
    for half in range(2):
        bytes_of(gated.at[half, x_c], gate_recv.at[half, 0])
        gate_copy(half, x_c, 2, core_c).start()

    total = None
    for half in range(2):
        bytes_of(gated.at[half, core_c], gate_recv.at[half, 1])
        bytes_of(gated.at[half, far_c], gate_recv.at[half, 2])
        rows = gated[half].reshape(chan_count * channels // 2, steps)
        term = jnp.dot(out_weight_t[half], rows, preferred_element_type=jnp.float32)
        total = term if total is None else total + term
    out[...] = (total.T + out_bias_v[...]).astype(out.dtype)

    bytes_of(conv_in.at[pl.ds(0, tm_count - 1)], conv_send.at[0])
    for half in range(2):
        bytes_of(gated.at[half, pl.ds(0, chan_count - 1)], gate_send.at[half])


def fused(
    series,
    proj_weight,
    proj_bias,
    short_taps,
    short_bias,
    spectrum,
    skip_gain,
    out_weight,
    out_bias,
):
    steps, channels = series.shape
    width = proj_weight.shape[0]
    tm_count, chan_count = lax.axis_size("tm"), lax.axis_size("chan")
    dft, twist = make_tables(tm_count, steps)
    share, slots, halo = channels // tm_count, 2 * tm_count, 16
    spread_shape = (tm_count, share, steps)
    vmem, dma = pltpu.VMEM, pltpu.SemaphoreType.DMA
    operands = [
        series,
        proj_weight.transpose(1, 0, 2),
        proj_bias,
        short_taps,
        short_bias,
        spectrum,
        skip_gain.reshape(1, channels),
        out_weight,
        out_bias.reshape(1, channels),
        jnp.asarray(dft),
        jnp.asarray(twist),
    ]
    return pl.pallas_call(
        functools.partial(kernel, tm_count, chan_count),
        out_shape=jax.ShapeDtypeStruct((steps, channels), jnp.bfloat16),
        in_specs=[pl.BlockSpec(memory_space=pl.ANY)] * len(operands),
        out_specs=pl.BlockSpec(memory_space=pltpu.VMEM),
        scratch_shapes=[
            vmem((halo + steps, width), jnp.bfloat16),
            vmem((width, 3 * channels), jnp.bfloat16),
            vmem(proj_bias.shape, jnp.float32),
            vmem(short_taps.shape, jnp.float32),
            vmem(short_bias.shape, jnp.float32),
            vmem((2, 2, steps, channels), jnp.float32),
            vmem((1, channels), jnp.float32),
            vmem((width, channels), jnp.bfloat16),
            vmem((2, channels, width // 2), jnp.bfloat16),
            vmem((1, channels), jnp.float32),
            vmem(dft.shape, jnp.bfloat16),
            vmem(twist.shape, jnp.float32),
            vmem((3, halo + steps, channels), jnp.float32),
            vmem((2, tm_count, 2, share, steps), jnp.bfloat16),
            vmem((2, tm_count, 2, share, steps), jnp.bfloat16),
            vmem(spread_shape, jnp.bfloat16),
            vmem(spread_shape, jnp.bfloat16),
            vmem((2, tm_count + 1, share, steps), jnp.bfloat16),
            vmem(spread_shape, jnp.bfloat16),
            vmem(spread_shape, jnp.bfloat16),
            vmem(spread_shape, jnp.float32),
            vmem(spread_shape, jnp.float32),
            vmem((2, chan_count, channels // 2, steps), jnp.bfloat16),
            dma((len(operands) + 2,)),
            dma((1,)),
            dma((4,)),
            *[dma((2,))] * 9,
            dma((2, 3)),
        ],
        compiler_params=pltpu.CompilerParams(
            collective_id=0, has_side_effects=True, vmem_limit_bytes=32 * 1024 * 1024
        ),
    )(*[pltpu.with_memory_space_constraint(operand, pltpu.HBM) for operand in operands])


def solution(mesh):
    sizes = mesh.shape

    def program(*arrays):
        share = arrays[0].shape[1] // sizes["chan"] // sizes["tm"]
        wide = share > 0 and share % 16 == 0 and sizes["tm"] >= 4 and sizes["chan"] == 4
        wide = wide and sizes["tm"] & sizes["tm"] - 1 == 0
        return jax.shard_map(
            fused if wide else shards,
            mesh=mesh,
            in_specs=(
                P("tm", "chan"),
                P(None, None, "chan"),
                P(None, "chan"),
                P(None, None, "chan"),
                P(None, "chan"),
                P(None, "tm", None, None, "chan"),
                P("chan"),
                P(),
                P("chan"),
            ),
            out_specs=P("tm", "chan"),
            check_vma=False,
        )(*arrays)

    return program
```

```python
import functools
import math

import jax
import jax.numpy as jnp
import numpy as np
from jax import lax
from jax.experimental import pallas as pl
from jax.experimental.pallas import tpu as pltpu
from jax.sharding import PartitionSpec as P

MESH = pl.DeviceIdType.MESH


def from_behind(array, axis, by):
    length = lax.axis_size(axis)
    pairs = [(i, i + by) for i in range(length) if 0 <= i + by < length]
    return lax.ppermute(array, axis, pairs)


def partner_2(block, axis, bit):
    count = lax.axis_size(axis)
    route = []
    for low in range(count):
        high = low | 1 << bit
        if high != low and high < count:
            route += [(low, high), (high, low)]
    return lax.ppermute(block, axis, route)


def reverse_bits(values, digits):
    result = jnp.zeros_like(values)
    for bit_level in range(digits):
        result = result | (values >> bit_level & 1) << digits - 1 - bit_level
    return result


def turning(numer, denom):
    angle = numer.astype(jnp.float32) * (-2.0 * math.pi / denom)
    return (jnp.cos(angle), jnp.sin(angle))


def complex_times(stacked, real_part, imag_part):
    return jnp.stack(
        [
            stacked[0] * real_part - stacked[1] * imag_part,
            stacked[0] * imag_part + stacked[1] * real_part,
        ]
    )


def dft_rows(signals, period, inverse):
    indices = jnp.arange(period, dtype=jnp.int32)
    cosine, sine_part = turning(indices[:, None] * indices[None, :] % period, period)
    if inverse:
        sine_part = -sine_part
    stacked = jnp.concatenate([cosine, sine_part], 0)
    result = jnp.einsum("bt,retc->rebc", stacked, signals, precision=lax.Precision.HIGHEST)
    real_out = result[0, :, :period] - result[1, :, period:]
    imag_out = result[1, :, :period] + result[0, :, period:]
    return jnp.stack([real_out, imag_out])


def shards(
    series,
    proj_weight,
    proj_bias,
    short_taps,
    short_bias,
    spectrum,
    skip_gain,
    out_weight,
    out_bias,
):
    steps_dev = series.shape[0]
    model_width = proj_weight.shape[0]
    channels = proj_weight.shape[2]
    flat_weight = proj_weight.reshape(model_width, 3 * channels)
    weight_rows = flat_weight
    projected = jnp.dot(
        lax.all_gather(series, "chan", axis=1, tiled=True),
        weight_rows,
        preferred_element_type=jnp.float32,
    )
    projected = (projected.reshape(steps_dev, 3, channels) + proj_bias).astype(jnp.bfloat16)
    taps_count = short_taps.shape[0]
    earlier = from_behind(projected[steps_dev - taps_count + 1 :], "tm", 1)
    extended = jnp.concatenate([earlier, projected], 0).astype(jnp.float32)
    streams = short_bias + short_taps[0] * extended[taps_count - 1 :]
    for offset in range(1, taps_count):
        streams = (
            streams
            + short_taps[offset]
            * extended[taps_count - 1 - offset : taps_count - 1 - offset + steps_dev]
        )
    streams = lax.optimization_barrier(streams.astype(jnp.bfloat16)).astype(jnp.float32)
    gate_out = streams[:, 0]
    mixed_in = lax.optimization_barrier((streams[:, 1] * streams[:, 2]).astype(jnp.bfloat16))
    signal = mixed_in.astype(jnp.float32)
    tm_count = lax.axis_size("tm")
    digits = tm_count.bit_length() - 1
    own_index = lax.axis_index("tm")
    period = 2 * tm_count * steps_dev
    positions = jnp.arange(steps_dev, dtype=jnp.int32)
    own_rows = 2 * reverse_bits(own_index, digits) + jnp.arange(2, dtype=jnp.int32)
    twist_cos, twist_sin = turning(own_rows[:, None] * positions[None, :] % period, period)
    twist_cos, twist_sin = (twist_cos[:, :, None], twist_sin[:, :, None])
    half_cos, half_sin = turning(own_index, 2 * tm_count)
    zero_field = jnp.zeros_like(signal)
    current = jnp.stack(
        [jnp.stack([signal, signal * half_cos]), jnp.stack([zero_field, signal * half_sin])]
    )
    for bit_level in reversed(range(digits)):
        partner = partner_2(current, "tm", bit_level)
        half_span = 1 << bit_level
        rot_cos, rot_sin = turning(own_index % half_span, 2 * half_span)
        upper_half = own_index >> bit_level & 1 == 1
        current = jnp.where(
            upper_half, complex_times(partner - current, rot_cos, rot_sin), current + partner
        )
    twisted = complex_times(current, twist_cos, twist_sin)
    spectral = dft_rows(twisted, steps_dev, False)
    response = spectrum.reshape(2, 2, steps_dev, channels)
    product = complex_times(spectral, response[0], response[1])
    returned = dft_rows(product, steps_dev, True)
    current = complex_times(returned, twist_cos, -twist_sin)
    for bit_level in range(digits):
        partner = partner_2(current, "tm", bit_level)
        half_span = 1 << bit_level
        rot_cos, rot_sin = turning(own_index % half_span, 2 * half_span)
        rot_sin = -rot_sin
        upper_half = own_index >> bit_level & 1 == 1
        current = jnp.where(
            upper_half,
            partner - complex_times(current, rot_cos, rot_sin),
            current + complex_times(partner, rot_cos, rot_sin),
        )
    convolved = current[0, 0] + half_cos * current[0, 1] + half_sin * current[1, 1]
    convolved = convolved * (1.0 / period)
    gated_rows = ((convolved + skip_gain * signal) * gate_out).astype(jnp.bfloat16)
    column_start = lax.axis_index("chan") * channels
    weight_rows = lax.dynamic_slice_in_dim(out_weight, column_start, channels, 0)
    partial_value = jnp.dot(gated_rows, weight_rows, preferred_element_type=jnp.float32)
    mixed_out = lax.psum_scatter(partial_value, "chan", scatter_dimension=1, tiled=True)
    return (mixed_out + out_bias).astype(jnp.bfloat16)


def make_tables(tm_count, steps):
    count, period = 2 * tm_count, 2 * tm_count * steps
    rows = np.arange(steps)
    angle = 2.0 * np.pi * (rows[:, None] * rows[None, :] % steps) / steps
    dft = np.stack([np.cos(angle), np.sin(angle)]).astype(jnp.bfloat16)
    angle = 2.0 * np.pi * (np.arange(count)[:, None] * rows[None, :] % period) / period
    twist = np.stack([np.cos(angle), np.sin(angle)]).astype(np.float32)
    return dft, twist


def flip(value, digits):
    result = 0
    for bit_level in range(digits):
        result |= (value >> bit_level & 1) << digits - 1 - bit_level
    return result


def across_bits(index, by):
    result, bit = index, 1
    while bit <= by:
        if by & bit:
            result = result + bit * (1 - 2 * lax.rem(lax.div(index, bit), 2))
        bit *= 2
    return result


def weighted(blocks, weights):
    total = None
    for block, weight in zip(blocks, weights):
        if abs(weight) < 1e-12:
            continue
        if abs(weight - 1.0) < 1e-12:
            term = block
        elif abs(weight + 1.0) < 1e-12:
            term = -block
        else:
            term = block * float(weight)
        total = term if total is None else total + term
    return total


def kernel(
    tm_count,
    chan_count,
    series,
    weight,
    proj_bias,
    taps,
    short_bias,
    spectrum,
    skip_gain,
    out_weight,
    out_bias,
    dft,
    twist,
    out,
    rows_in,
    weight_v,
    proj_bias_v,
    taps_v,
    short_bias_v,
    spectrum_v,
    skip_v,
    out_weight_v,
    out_weight_t,
    out_bias_v,
    dft_v,
    twist_v,
    projected,
    spec_out,
    spec_in,
    odd_out,
    odd_in,
    mixed_out,
    mixed_in,
    wave,
    odd_wave,
    even_sum,
    conv_out,
    conv_in,
    gate_t,
    direct_t,
    gated,
    local_sem,
    rows_send,
    rows_recv,
    halo_send,
    halo_recv,
    spec_send,
    spec_recv,
    mix_send,
    mix_recv,
    conv_send,
    conv_recv,
    gate_send,
    gate_recv,
):
    steps, channels = series.shape
    halo = rows_in.shape[0] - steps
    share = channels // tm_count
    digits = tm_count.bit_length() - 1
    slots = 2 * tm_count
    own_t, own_c = lax.axis_index("tm"), lax.axis_index("chan")
    columns = lambda c: pl.ds(pl.multiple_of(c * channels, channels), channels)
    next_t, last_t = lax.rem(own_t + 1, tm_count), lax.rem(own_t + tm_count - 1, tm_count)
    tm_peer = lambda by: across_bits(own_t, by)
    chan_peer = lambda by: across_bits(own_c, by)
    far_first = list(range(tm_count // 2, tm_count)) + list(range(1, tm_count // 2))

    barrier = pltpu.get_barrier_semaphore()
    greet = lambda where: pl.semaphore_signal(barrier, inc=1, device_id=where, device_id_type=MESH)
    for by in range(1, chan_count):
        greet({"chan": chan_peer(by)})
    for by in range(1, tm_count):
        greet({"tm": tm_peer(by)})
    for by in range(1, chan_count):
        greet({"tm": next_t, "chan": chan_peer(by)})
        greet({"tm": last_t, "chan": chan_peer(by)})

    pairs = [
        (series, rows_in.at[pl.ds(halo, steps), columns(own_c)]),
        (spectrum.at[:, 0], spectrum_v),
        *[(weight.at[j], weight_v.at[:, pl.ds((j + 2) % 3 * channels, channels)]) for j in range(3)],
        (proj_bias, proj_bias_v),
        (taps, taps_v),
        (short_bias, short_bias_v),
        (dft, dft_v),
        (twist, twist_v),
        (skip_gain, skip_v),
        (out_weight.at[:, columns(own_c)], out_weight_v),
        (out_bias, out_bias_v),
    ]
    local = [pltpu.make_async_copy(a, b, local_sem.at[i]) for i, (a, b) in enumerate(pairs)]
    for copy in local:
        copy.start()

    def remote(src, dst, send, recv, where):
        return pltpu.make_async_remote_copy(
            src_ref=src, dst_ref=dst, send_sem=send, recv_sem=recv, device_id=where, device_id_type=MESH
        )

    residue = 2 * sum((own_t >> i & 1) << digits - 1 - i for i in range(digits))
    down = lax.broadcasted_iota(jnp.int32, (steps, steps), 0)
    across = lax.broadcasted_iota(jnp.int32, (steps, steps), 1)

    def turn_spectrum(parity):
        wanted = jnp.where(residue + parity > tm_count, steps - 1 - down, down)
        order = jnp.where(wanted == across, 1.0 / (slots * steps), 0.0).astype(jnp.bfloat16)
        for part in range(2):
            block = spectrum_v[part, parity].astype(jnp.bfloat16)
            block = jnp.dot(order, block, preferred_element_type=jnp.float32).T
            block = block.astype(jnp.bfloat16).reshape(tm_count, share, steps)
            if parity:
                odd_out[part] = block
            else:
                spec_out[0, :, part] = block

    early = own_t < tm_count // 2

    @pl.when(early)
    def _():
        local[1].wait()
        turn_spectrum(0)
        turn_spectrum(1)

    pl.semaphore_wait(barrier, chan_count - 1 + tm_count - 1 + 2 * (chan_count - 1))

    core_c, x_c, far_c = chan_peer(1), chan_peer(2), chan_peer(3)
    part_rows = steps // 2

    def rows_copy(owner, first, count, recv, to):
        block = rows_in.at[pl.ds(halo + first, count), columns(owner)]
        source = series.at[pl.ds(first, count)] if owner is own_c else block
        return remote(source, block, rows_send.at[0], rows_recv.at[recv], {"chan": to})

    def halo_copy(by, owner):
        return remote(
            series.at[pl.ds(steps - halo, halo)],
            rows_in.at[pl.ds(0, halo), columns(owner)],
            halo_send.at[0],
            halo_recv.at[0],
            {"tm": next_t, "chan": chan_peer(by)},
        )

    for i in range(2):
        rows_copy(own_c, i * part_rows, part_rows, i, x_c).start()
    rows_copy(own_c, 0, steps, 2, core_c).start()

    @pl.when(own_t < tm_count - 1)
    def _():
        for by in range(chan_count):
            halo_copy(by, own_c).start()

    @pl.when(own_t == 0)
    def _():
        rows_in[pl.ds(0, halo), :] = jnp.zeros((halo, rows_in.shape[1]), rows_in.dtype)

    def bytes_of(ref, sem):
        pltpu.make_async_copy(ref, ref, sem).wait()

    def spread(src, dst, send, recv):
        for by in far_first:
            remote(src.at[tm_peer(by)], dst.at[own_t], send, recv, {"tm": tm_peer(by)}).start()
        dst[own_t] = src[own_t]

    def collect(dst, recv):
        bytes_of(dst.at[pl.ds(0, tm_count - 1)], recv)

    def spread_spectrum(piece):
        if piece == 0:
            spread(spec_out.at[0], spec_in.at[0], spec_send.at[0], spec_recv.at[0])
        else:
            spread(odd_out.at[piece - 1], odd_in.at[piece - 1], spec_send.at[piece], spec_recv.at[piece])

    @pl.when(early)
    def _():
        spread_spectrum(0)
        spread_spectrum(1)

    @pl.when(jnp.logical_not(early))
    def _():
        local[1].wait()
        for parity in range(2):
            turn_spectrum(parity)
            spread_spectrum(parity)

    for i in range(2):
        bytes_of(rows_in.at[pl.ds(halo, part_rows), columns(x_c)], rows_recv.at[i])
        rows_copy(x_c, i * part_rows, part_rows, 3, core_c).start()
    local[0].wait()
    for copy in local[2:]:
        copy.wait()
    others = pl.ds(0, (chan_count - 1) * channels)

    @pl.when(own_t > 0)
    def _():
        bytes_of(rows_in.at[pl.ds(0, halo)], halo_recv.at[0])

    bytes_of(rows_in.at[pl.ds(halo, steps), columns(core_c)], rows_recv.at[2])

    def of_chip(chip):
        inputs = pl.ds(pl.multiple_of(chip * 2 * channels, 2 * channels), 2 * channels)
        return jnp.dot(
            rows_in[:, inputs], weight_v[inputs, pl.ds(0, 2 * channels)], preferred_element_type=jnp.float32
        )

    own_chip = lax.div(own_c, 2)
    near_sum = of_chip(own_chip)
    bytes_of(rows_in.at[pl.ds(halo, steps), columns(far_c)], rows_recv.at[3])
    sums = near_sum + of_chip(1 - own_chip)

    streams = []
    for j in (1, 2, 0):
        if j:
            value = sums[:, (j - 1) * channels : j * channels]
        else:
            value = jnp.dot(
                rows_in[...], weight_v[:, pl.ds(2 * channels, channels)], preferred_element_type=jnp.float32
            )
        value = (value + proj_bias_v[j : j + 1]).astype(jnp.bfloat16).astype(jnp.float32)
        projected[j] = value

        @pl.when(own_t == 0)
        def _():
            projected[j, pl.ds(0, halo)] = jnp.zeros((halo, channels), jnp.float32)

        stream = short_bias_v[j : j + 1] + taps_v[0, j : j + 1] * projected[j, pl.ds(halo, steps)]
        for k in range(1, taps.shape[0]):
            stream = stream + taps_v[k, j : j + 1] * projected[j, pl.ds(halo - k, steps)]
        stream = stream.astype(jnp.bfloat16).astype(jnp.float32)
        if j == 2:
            signal = (streams[0] * stream).astype(jnp.bfloat16).astype(jnp.float32)
            mixed_out[...] = signal.T.astype(jnp.bfloat16).reshape(tm_count, share, steps)
            spread(mixed_out, mixed_in, mix_send.at[0], mix_recv.at[0])
            spread_spectrum(2)
        streams.append(stream)
    gate_t[...] = streams[2].T.reshape(tm_count, share, steps)
    direct_t[...] = (skip_v[...] * signal).T.reshape(tm_count, share, steps)
    near = tm_count // 2
    for half in range(2):
        blocks = [
            out_weight_v[pl.ds(pl.multiple_of(c * channels + tm_peer(half * near + by) * share, share), share)]
            for c in range(chan_count)
            for by in range(near)
        ]
        out_weight_t[half] = jnp.concatenate(blocks, 0).astype(jnp.float32).T.astype(jnp.bfloat16)

    collect(mixed_in, mix_recv.at[0])
    blocks = [mixed_in[b].astype(jnp.float32) for b in range(tm_count)]
    turns = 2.0 * np.pi * np.arange(slots) / slots
    cosine = lambda r, b: math.cos(turns[r * b % slots])
    sine = lambda r, b: math.sin(turns[r * b % slots])
    kept = tm_count + 1
    waves = (wave, odd_wave)

    for r in range(kept):
        real = weighted(blocks, [cosine(r, b) for b in range(tm_count)])
        imag = weighted(blocks, [-sine(r, b) for b in range(tm_count)])
        cos_row, sin_row = twist_v[0, r : r + 1], twist_v[1, r : r + 1]
        if imag is None:
            turned = (real * cos_row, -(real * sin_row))
        else:
            turned = (real * cos_row + imag * sin_row, imag * cos_row - real * sin_row)
        for part in range(2):
            waves[r % 2][part, r // 2] = turned[part].astype(jnp.bfloat16)

    def within(parity):
        count = waves[parity].shape[1]
        rows = waves[parity][...].reshape(2 * count * share, steps)
        first = jnp.dot(rows, dft_v[0], preferred_element_type=jnp.float32)
        second = jnp.dot(rows, dft_v[1], preferred_element_type=jnp.float32)
        half = count * share
        return [a.reshape(count, share, steps) for a in (first[:half], first[half:], second[:half], second[half:])]

    def filter_of(part, r):
        slot = flip(r // 2, digits)
        return (odd_in[part, slot] if r % 2 else spec_in[0, slot, part]).astype(jnp.float32)

    forward = []
    for parity in range(2):
        real_cos, imag_cos, real_sin, imag_sin = within(parity)
        forward.append((real_cos + imag_sin, imag_cos - real_sin))
    sums = []
    for parity in range(2):
        if parity:
            for part in range(2):
                collect(odd_in.at[part], spec_recv.at[1 + part])
        else:
            collect(spec_in.at[0], spec_recv.at[0])
        real, imag = forward[parity]
        residues = range(parity, kept, 2)
        for i, r in enumerate(residues):
            filter_real, filter_imag = filter_of(0, r), filter_of(1, r)
            if 0 < r < tm_count:
                filter_real = filter_real + filter_of(0, slots - r)
                filter_imag = filter_imag - filter_of(1, slots - r)
            waves[parity][0, i] = (real[i] * filter_real - imag[i] * filter_imag).astype(jnp.bfloat16)
            waves[parity][1, i] = (real[i] * filter_imag + imag[i] * filter_real).astype(jnp.bfloat16)
        real_cos, imag_cos, real_sin, imag_sin = within(parity)
        real, imag = real_cos - imag_sin, real_sin + imag_cos
        terms = []
        for i, r in enumerate(residues):
            cos_row, sin_row = twist_v[0, r : r + 1], twist_v[1, r : r + 1]
            terms.append(real[i] * cos_row - imag[i] * sin_row)
            terms.append(real[i] * sin_row + imag[i] * cos_row)
        for b in range(tm_count):
            total = weighted(terms, [w for r in residues for w in (cosine(r, b), -sine(r, b))])
            if parity:
                conv_out[b] = (even_sum[b] + total).astype(jnp.bfloat16)
            else:
                even_sum[b] = total
    for by in far_first:
        half = by // near
        remote(
            conv_out.at[tm_peer(by)], conv_in.at[by], conv_send.at[0], conv_recv.at[half], {"tm": tm_peer(by)}
        ).start()

    bytes_of(rows_in.at[pl.ds(halo, steps), others], rows_send.at[0])

    @pl.when(own_t < tm_count - 1)
    def _():
        bytes_of(rows_in.at[pl.ds(0, halo)], halo_send.at[0])

    collect(spec_in.at[0], spec_send.at[0])
    for part in range(2):
        collect(odd_in.at[part], spec_send.at[1 + part])
    bytes_of(mixed_in.at[pl.ds(0, tm_count - 1)], mix_send.at[0])

    def gate_copy(half, owner, recv, to):
        block = gated.at[half, owner]
        return remote(block, block, gate_send.at[half], gate_recv.at[half, recv], {"chan": to})

    for half in range(2):
        if half == 0:
            bytes_of(conv_in.at[pl.ds(0, near - 1)], conv_recv.at[0])
        else:
            bytes_of(conv_in.at[pl.ds(0, near)], conv_recv.at[1])
        for by in range(half * near, (half + 1) * near):
            source = tm_peer(by)
            arrived = conv_in[by] if by else conv_out[source]
            value = (arrived.astype(jnp.float32) + direct_t[source]) * gate_t[source]
            gated[half, own_c, pl.ds(by % near * share, share)] = value.astype(jnp.bfloat16)
        gate_copy(half, own_c, 0, x_c).start()
        gate_copy(half, own_c, 1, core_c).start()
    for half in range(2):
        bytes_of(gated.at[half, x_c], gate_recv.at[half, 0])
        gate_copy(half, x_c, 2, core_c).start()

    total = None
    for half in range(2):
        bytes_of(gated.at[half, core_c], gate_recv.at[half, 1])
        bytes_of(gated.at[half, far_c], gate_recv.at[half, 2])
        rows = gated[half].reshape(chan_count * channels // 2, steps)
        term = jnp.dot(out_weight_t[half], rows, preferred_element_type=jnp.float32)
        total = term if total is None else total + term
    out[...] = (total.T + out_bias_v[...]).astype(out.dtype)

    bytes_of(conv_in.at[pl.ds(0, tm_count - 1)], conv_send.at[0])
    for half in range(2):
        bytes_of(gated.at[half, pl.ds(0, chan_count - 1)], gate_send.at[half])


def fused(
    series,
    proj_weight,
    proj_bias,
    short_taps,
    short_bias,
    spectrum,
    skip_gain,
    out_weight,
    out_bias,
):
    steps, channels = series.shape
    width = proj_weight.shape[0]
    tm_count, chan_count = lax.axis_size("tm"), lax.axis_size("chan")
    dft, twist = make_tables(tm_count, steps)
    share, slots, halo = channels // tm_count, 2 * tm_count, 16
    spread_shape = (tm_count, share, steps)
    vmem, dma = pltpu.VMEM, pltpu.SemaphoreType.DMA
    operands = [
        series,
        proj_weight.transpose(1, 0, 2),
        proj_bias,
        short_taps,
        short_bias,
        spectrum,
        skip_gain.reshape(1, channels),
        out_weight,
        out_bias.reshape(1, channels),
        jnp.asarray(dft),
        jnp.asarray(twist),
    ]
    return pl.pallas_call(
        functools.partial(kernel, tm_count, chan_count),
        out_shape=jax.ShapeDtypeStruct((steps, channels), jnp.bfloat16),
        in_specs=[pl.BlockSpec(memory_space=pl.ANY)] * len(operands),
        out_specs=pl.BlockSpec(memory_space=pltpu.VMEM),
        scratch_shapes=[
            vmem((halo + steps, width), jnp.bfloat16),
            vmem((width, 3 * channels), jnp.bfloat16),
            vmem(proj_bias.shape, jnp.float32),
            vmem(short_taps.shape, jnp.float32),
            vmem(short_bias.shape, jnp.float32),
            vmem((2, 2, steps, channels), jnp.float32),
            vmem((1, channels), jnp.float32),
            vmem((width, channels), jnp.bfloat16),
            vmem((2, channels, width // 2), jnp.bfloat16),
            vmem((1, channels), jnp.float32),
            vmem(dft.shape, jnp.bfloat16),
            vmem(twist.shape, jnp.float32),
            vmem((3, halo + steps, channels), jnp.float32),
            vmem((1, tm_count, 2, share, steps), jnp.bfloat16),
            vmem((1, tm_count, 2, share, steps), jnp.bfloat16),
            vmem((2, *spread_shape), jnp.bfloat16),
            vmem((2, *spread_shape), jnp.bfloat16),
            vmem(spread_shape, jnp.bfloat16),
            vmem(spread_shape, jnp.bfloat16),
            vmem((2, tm_count // 2 + 1, share, steps), jnp.bfloat16),
            vmem((2, tm_count // 2, share, steps), jnp.bfloat16),
            vmem(spread_shape, jnp.float32),
            vmem(spread_shape, jnp.bfloat16),
            vmem(spread_shape, jnp.bfloat16),
            vmem(spread_shape, jnp.float32),
            vmem(spread_shape, jnp.float32),
            vmem((2, chan_count, channels // 2, steps), jnp.bfloat16),
            dma((len(operands) + 2,)),
            dma((1,)),
            dma((4,)),
            *[dma((3,))] * 9,
            dma((2, 3)),
        ],
        compiler_params=pltpu.CompilerParams(
            collective_id=0, has_side_effects=True, vmem_limit_bytes=32 * 1024 * 1024
        ),
    )(*[pltpu.with_memory_space_constraint(operand, pltpu.HBM) for operand in operands])


def solution(mesh):
    sizes = mesh.shape

    def program(*arrays):
        share = arrays[0].shape[1] // sizes["chan"] // sizes["tm"]
        wide = share > 0 and share % 16 == 0 and sizes["tm"] >= 4 and sizes["chan"] == 4
        wide = wide and sizes["tm"] & sizes["tm"] - 1 == 0
        return jax.shard_map(
            fused if wide else shards,
            mesh=mesh,
            in_specs=(
                P("tm", "chan"),
                P(None, None, "chan"),
                P(None, "chan"),
                P(None, None, "chan"),
                P(None, "chan"),
                P(None, "tm", None, None, "chan"),
                P("chan"),
                P(),
                P("chan"),
            ),
            out_specs=P("tm", "chan"),
            check_vma=False,
        )(*arrays)

    return program
```

```python
import functools
import math

import jax
import jax.numpy as jnp
import numpy as np
from jax import lax
from jax.experimental import pallas as pl
from jax.experimental.pallas import tpu as pltpu
from jax.sharding import PartitionSpec as P

MESH = pl.DeviceIdType.MESH


def from_behind(array, axis, by):
    length = lax.axis_size(axis)
    pairs = [(i, i + by) for i in range(length) if 0 <= i + by < length]
    return lax.ppermute(array, axis, pairs)


def partner_2(block, axis, bit):
    count = lax.axis_size(axis)
    route = []
    for low in range(count):
        high = low | 1 << bit
        if high != low and high < count:
            route += [(low, high), (high, low)]
    return lax.ppermute(block, axis, route)


def reverse_bits(values, digits):
    result = jnp.zeros_like(values)
    for bit_level in range(digits):
        result = result | (values >> bit_level & 1) << digits - 1 - bit_level
    return result


def turning(numer, denom):
    angle = numer.astype(jnp.float32) * (-2.0 * math.pi / denom)
    return (jnp.cos(angle), jnp.sin(angle))


def complex_times(stacked, real_part, imag_part):
    return jnp.stack(
        [
            stacked[0] * real_part - stacked[1] * imag_part,
            stacked[0] * imag_part + stacked[1] * real_part,
        ]
    )


def dft_rows(signals, period, inverse):
    indices = jnp.arange(period, dtype=jnp.int32)
    cosine, sine_part = turning(indices[:, None] * indices[None, :] % period, period)
    if inverse:
        sine_part = -sine_part
    stacked = jnp.concatenate([cosine, sine_part], 0)
    result = jnp.einsum("bt,retc->rebc", stacked, signals, precision=lax.Precision.HIGHEST)
    real_out = result[0, :, :period] - result[1, :, period:]
    imag_out = result[1, :, :period] + result[0, :, period:]
    return jnp.stack([real_out, imag_out])


def shards(
    series,
    proj_weight,
    proj_bias,
    short_taps,
    short_bias,
    spectrum,
    skip_gain,
    out_weight,
    out_bias,
):
    steps_dev = series.shape[0]
    model_width = proj_weight.shape[0]
    channels = proj_weight.shape[2]
    flat_weight = proj_weight.reshape(model_width, 3 * channels)
    weight_rows = flat_weight
    projected = jnp.dot(
        lax.all_gather(series, "chan", axis=1, tiled=True),
        weight_rows,
        preferred_element_type=jnp.float32,
    )
    projected = (projected.reshape(steps_dev, 3, channels) + proj_bias).astype(jnp.bfloat16)
    taps_count = short_taps.shape[0]
    earlier = from_behind(projected[steps_dev - taps_count + 1 :], "tm", 1)
    extended = jnp.concatenate([earlier, projected], 0).astype(jnp.float32)
    streams = short_bias + short_taps[0] * extended[taps_count - 1 :]
    for offset in range(1, taps_count):
        streams = (
            streams
            + short_taps[offset]
            * extended[taps_count - 1 - offset : taps_count - 1 - offset + steps_dev]
        )
    streams = lax.optimization_barrier(streams.astype(jnp.bfloat16)).astype(jnp.float32)
    gate_out = streams[:, 0]
    mixed_in = lax.optimization_barrier((streams[:, 1] * streams[:, 2]).astype(jnp.bfloat16))
    signal = mixed_in.astype(jnp.float32)
    tm_count = lax.axis_size("tm")
    digits = tm_count.bit_length() - 1
    own_index = lax.axis_index("tm")
    period = 2 * tm_count * steps_dev
    positions = jnp.arange(steps_dev, dtype=jnp.int32)
    own_rows = 2 * reverse_bits(own_index, digits) + jnp.arange(2, dtype=jnp.int32)
    twist_cos, twist_sin = turning(own_rows[:, None] * positions[None, :] % period, period)
    twist_cos, twist_sin = (twist_cos[:, :, None], twist_sin[:, :, None])
    half_cos, half_sin = turning(own_index, 2 * tm_count)
    zero_field = jnp.zeros_like(signal)
    current = jnp.stack(
        [jnp.stack([signal, signal * half_cos]), jnp.stack([zero_field, signal * half_sin])]
    )
    for bit_level in reversed(range(digits)):
        partner = partner_2(current, "tm", bit_level)
        half_span = 1 << bit_level
        rot_cos, rot_sin = turning(own_index % half_span, 2 * half_span)
        upper_half = own_index >> bit_level & 1 == 1
        current = jnp.where(
            upper_half, complex_times(partner - current, rot_cos, rot_sin), current + partner
        )
    twisted = complex_times(current, twist_cos, twist_sin)
    spectral = dft_rows(twisted, steps_dev, False)
    response = spectrum.reshape(2, 2, steps_dev, channels)
    product = complex_times(spectral, response[0], response[1])
    returned = dft_rows(product, steps_dev, True)
    current = complex_times(returned, twist_cos, -twist_sin)
    for bit_level in range(digits):
        partner = partner_2(current, "tm", bit_level)
        half_span = 1 << bit_level
        rot_cos, rot_sin = turning(own_index % half_span, 2 * half_span)
        rot_sin = -rot_sin
        upper_half = own_index >> bit_level & 1 == 1
        current = jnp.where(
            upper_half,
            partner - complex_times(current, rot_cos, rot_sin),
            current + complex_times(partner, rot_cos, rot_sin),
        )
    convolved = current[0, 0] + half_cos * current[0, 1] + half_sin * current[1, 1]
    convolved = convolved * (1.0 / period)
    gated_rows = ((convolved + skip_gain * signal) * gate_out).astype(jnp.bfloat16)
    column_start = lax.axis_index("chan") * channels
    weight_rows = lax.dynamic_slice_in_dim(out_weight, column_start, channels, 0)
    partial_value = jnp.dot(gated_rows, weight_rows, preferred_element_type=jnp.float32)
    mixed_out = lax.psum_scatter(partial_value, "chan", scatter_dimension=1, tiled=True)
    return (mixed_out + out_bias).astype(jnp.bfloat16)


def make_tables(tm_count, steps):
    count, period = 2 * tm_count, 2 * tm_count * steps
    rows = np.arange(steps)
    angle = 2.0 * np.pi * (rows[:, None] * rows[None, :] % steps) / steps
    dft = np.stack([np.cos(angle), np.sin(angle)]).astype(jnp.bfloat16)
    angle = 2.0 * np.pi * (np.arange(count)[:, None] * rows[None, :] % period) / period
    twist = np.stack([np.cos(angle), np.sin(angle)]).astype(np.float32)
    return dft, twist


def flip(value, digits):
    result = 0
    for bit_level in range(digits):
        result |= (value >> bit_level & 1) << digits - 1 - bit_level
    return result


def across_bits(index, by):
    result, bit = index, 1
    while bit <= by:
        if by & bit:
            result = result + bit * (1 - 2 * lax.rem(lax.div(index, bit), 2))
        bit *= 2
    return result


def weighted(blocks, weights):
    total = None
    for block, weight in zip(blocks, weights):
        if abs(weight) < 1e-12:
            continue
        if abs(weight - 1.0) < 1e-12:
            term = block
        elif abs(weight + 1.0) < 1e-12:
            term = -block
        else:
            term = block * float(weight)
        total = term if total is None else total + term
    return total


def kernel(
    tm_count,
    chan_count,
    series,
    weight,
    proj_bias,
    taps,
    short_bias,
    spectrum,
    skip_gain,
    out_weight,
    out_bias,
    dft,
    twist,
    out,
    rows_in,
    weight_v,
    proj_bias_v,
    taps_v,
    short_bias_v,
    spectrum_v,
    skip_v,
    out_weight_v,
    out_weight_t,
    out_bias_v,
    dft_v,
    twist_v,
    projected,
    spec_out,
    spec_in,
    mixed_out,
    mixed_in,
    wave,
    conv_out,
    conv_in,
    gate_t,
    direct_t,
    gated,
    local_sem,
    rows_send,
    rows_recv,
    halo_send,
    halo_recv,
    spec_send,
    spec_recv,
    mix_send,
    mix_recv,
    conv_send,
    conv_recv,
    gate_send,
    gate_recv,
):
    steps, channels = series.shape
    halo = rows_in.shape[0] - steps
    share = channels // tm_count
    digits = tm_count.bit_length() - 1
    slots = 2 * tm_count
    own_t, own_c = lax.axis_index("tm"), lax.axis_index("chan")
    columns = lambda c: pl.ds(pl.multiple_of(c * channels, channels), channels)
    next_t, last_t = lax.rem(own_t + 1, tm_count), lax.rem(own_t + tm_count - 1, tm_count)
    tm_peer = lambda by: across_bits(own_t, by)
    chan_peer = lambda by: across_bits(own_c, by)
    far_first = list(range(tm_count // 2, tm_count)) + list(range(1, tm_count // 2))

    barrier = pltpu.get_barrier_semaphore()
    greet = lambda where: pl.semaphore_signal(barrier, inc=1, device_id=where, device_id_type=MESH)
    for by in range(1, chan_count):
        greet({"chan": chan_peer(by)})
    for by in range(1, tm_count):
        greet({"tm": tm_peer(by)})
    for by in range(1, chan_count):
        greet({"tm": next_t, "chan": chan_peer(by)})
        greet({"tm": last_t, "chan": chan_peer(by)})

    pairs = [
        (series, rows_in.at[pl.ds(halo, steps), columns(own_c)]),
        (spectrum.at[:, 0], spectrum_v),
        *[(weight.at[j], weight_v.at[:, pl.ds((j + 2) % 3 * channels, channels)]) for j in range(3)],
        (proj_bias, proj_bias_v),
        (taps, taps_v),
        (short_bias, short_bias_v),
        (dft, dft_v),
        (twist, twist_v),
        (skip_gain, skip_v),
        (out_weight.at[:, columns(own_c)], out_weight_v),
        (out_bias, out_bias_v),
    ]
    local = [pltpu.make_async_copy(a, b, local_sem.at[i]) for i, (a, b) in enumerate(pairs)]
    for copy in local:
        copy.start()

    def remote(src, dst, send, recv, where):
        return pltpu.make_async_remote_copy(
            src_ref=src, dst_ref=dst, send_sem=send, recv_sem=recv, device_id=where, device_id_type=MESH
        )

    residue = 2 * sum((own_t >> i & 1) << digits - 1 - i for i in range(digits))
    down = lax.broadcasted_iota(jnp.int32, (steps, steps), 0)
    across = lax.broadcasted_iota(jnp.int32, (steps, steps), 1)

    def turn_spectrum(parity):
        wanted = jnp.where(residue + parity > tm_count, steps - 1 - down, down)
        order = jnp.where(wanted == across, 1.0 / (slots * steps), 0.0).astype(jnp.bfloat16)
        for part in range(2):
            block = spectrum_v[part, parity].astype(jnp.bfloat16)
            block = lax.dot_general(
                block, order, (((0,), (0,)), ((), ())), preferred_element_type=jnp.float32
            )
            spec_out[parity, :, part] = block.astype(jnp.bfloat16).reshape(tm_count, share, steps)

    early = own_t < tm_count // 2

    @pl.when(early)
    def _():
        local[1].wait()
        turn_spectrum(0)
        turn_spectrum(1)

    pl.semaphore_wait(barrier, chan_count - 1 + tm_count - 1 + 2 * (chan_count - 1))

    core_c, x_c, far_c = chan_peer(1), chan_peer(2), chan_peer(3)
    part_rows = steps // 2

    def rows_copy(owner, first, count, recv, to):
        block = rows_in.at[pl.ds(halo + first, count), columns(owner)]
        source = series.at[pl.ds(first, count)] if owner is own_c else block
        return remote(source, block, rows_send.at[0], rows_recv.at[recv], {"chan": to})

    def halo_copy(by, owner):
        return remote(
            series.at[pl.ds(steps - halo, halo)],
            rows_in.at[pl.ds(0, halo), columns(owner)],
            halo_send.at[0],
            halo_recv.at[0],
            {"tm": next_t, "chan": chan_peer(by)},
        )

    for i in range(2):
        rows_copy(own_c, i * part_rows, part_rows, i, x_c).start()
    rows_copy(own_c, 0, steps, 2, core_c).start()

    @pl.when(own_t < tm_count - 1)
    def _():
        for by in range(chan_count):
            halo_copy(by, own_c).start()

    @pl.when(own_t == 0)
    def _():
        rows_in[pl.ds(0, halo), :] = jnp.zeros((halo, rows_in.shape[1]), rows_in.dtype)

    def bytes_of(ref, sem):
        pltpu.make_async_copy(ref, ref, sem).wait()

    def spread(src, dst, send, recv):
        for by in far_first:
            remote(src.at[tm_peer(by)], dst.at[own_t], send, recv, {"tm": tm_peer(by)}).start()
        dst[own_t] = src[own_t]

    def collect(dst, recv):
        bytes_of(dst.at[pl.ds(0, tm_count - 1)], recv)

    def relay_rows():
        for i in range(2):
            bytes_of(rows_in.at[pl.ds(halo, part_rows), columns(x_c)], rows_recv.at[i])
            rows_copy(x_c, i * part_rows, part_rows, 3, core_c).start()

    def spread_spectrum(parity):
        spread(spec_out.at[parity], spec_in.at[parity], spec_send.at[parity], spec_recv.at[parity])

    @pl.when(early)
    def _():
        spread_spectrum(0)
        spread_spectrum(1)
        relay_rows()

    @pl.when(jnp.logical_not(early))
    def _():
        local[1].wait()
        turn_spectrum(0)
        spread_spectrum(0)
        relay_rows()
        turn_spectrum(1)
        spread_spectrum(1)

    local[0].wait()
    for copy in local[2:]:
        copy.wait()
    others = pl.ds(0, (chan_count - 1) * channels)

    @pl.when(own_t > 0)
    def _():
        bytes_of(rows_in.at[pl.ds(0, halo)], halo_recv.at[0])

    bytes_of(rows_in.at[pl.ds(halo, steps), columns(core_c)], rows_recv.at[2])

    def of_chip(chip):
        inputs = pl.ds(pl.multiple_of(chip * 2 * channels, 2 * channels), 2 * channels)
        return jnp.dot(
            rows_in[:, inputs], weight_v[inputs, pl.ds(0, 2 * channels)], preferred_element_type=jnp.float32
        )

    own_chip = lax.div(own_c, 2)
    near_sum = of_chip(own_chip)
    bytes_of(rows_in.at[pl.ds(halo, steps), columns(far_c)], rows_recv.at[3])
    sums = near_sum + of_chip(1 - own_chip)

    streams = []
    for j in (1, 2, 0):
        if j:
            value = sums[:, (j - 1) * channels : j * channels]
        else:
            value = jnp.dot(
                rows_in[...], weight_v[:, pl.ds(2 * channels, channels)], preferred_element_type=jnp.float32
            )
        value = (value + proj_bias_v[j : j + 1]).astype(jnp.bfloat16).astype(jnp.float32)
        projected[j] = value

        @pl.when(own_t == 0)
        def _():
            projected[j, pl.ds(0, halo)] = jnp.zeros((halo, channels), jnp.float32)

        stream = short_bias_v[j : j + 1] + taps_v[0, j : j + 1] * projected[j, pl.ds(halo, steps)]
        for k in range(1, taps.shape[0]):
            stream = stream + taps_v[k, j : j + 1] * projected[j, pl.ds(halo - k, steps)]
        stream = stream.astype(jnp.bfloat16).astype(jnp.float32)
        if j == 2:
            signal = (streams[0] * stream).astype(jnp.bfloat16).astype(jnp.float32)
            mixed_out[...] = signal.T.astype(jnp.bfloat16).reshape(tm_count, share, steps)
            spread(mixed_out, mixed_in, mix_send.at[0], mix_recv.at[0])
        streams.append(stream)
    gate_t[...] = streams[2].T.reshape(tm_count, share, steps)
    direct_t[...] = (skip_v[...] * signal).T.reshape(tm_count, share, steps)
    near = tm_count // 2
    for half in range(2):
        blocks = [
            out_weight_v[pl.ds(pl.multiple_of(c * channels + tm_peer(half * near + by) * share, share), share)]
            for c in range(chan_count)
            for by in range(near)
        ]
        out_weight_t[half] = jnp.concatenate(blocks, 0).astype(jnp.float32).T.astype(jnp.bfloat16)

    collect(mixed_in, mix_recv.at[0])
    blocks = [mixed_in[b].astype(jnp.float32) for b in range(tm_count)]
    turns = 2.0 * np.pi * np.arange(slots) / slots
    cosine = lambda r, b: math.cos(turns[r * b % slots])
    sine = lambda r, b: math.sin(turns[r * b % slots])
    kept = tm_count + 1

    for r in range(kept):
        real = weighted(blocks, [cosine(r, b) for b in range(tm_count)])
        imag = weighted(blocks, [-sine(r, b) for b in range(tm_count)])
        cos_row, sin_row = twist_v[0, r : r + 1], twist_v[1, r : r + 1]
        if imag is None:
            turned = (real * cos_row, -(real * sin_row))
        else:
            turned = (real * cos_row + imag * sin_row, imag * cos_row - real * sin_row)
        for part in range(2):
            wave[part, r] = turned[part].astype(jnp.bfloat16)

    def within():
        rows = wave[...].reshape(2 * kept * share, steps)
        first = jnp.dot(rows, dft_v[0], preferred_element_type=jnp.float32)
        second = jnp.dot(rows, dft_v[1], preferred_element_type=jnp.float32)
        half = kept * share
        return [a.reshape(kept, share, steps) for a in (first[:half], first[half:], second[:half], second[half:])]

    real_cos, imag_cos, real_sin, imag_sin = within()
    real, imag = real_cos + imag_sin, imag_cos - real_sin
    for parity in range(2):
        collect(spec_in.at[parity], spec_recv.at[parity])

    def filter_of(part, r):
        return spec_in[r % 2, flip(r // 2, digits), part].astype(jnp.float32)

    for r in range(kept):
        filter_real, filter_imag = filter_of(0, r), filter_of(1, r)
        if 0 < r < tm_count:
            filter_real = filter_real + filter_of(0, slots - r)
            filter_imag = filter_imag - filter_of(1, slots - r)
        wave[0, r] = (real[r] * filter_real - imag[r] * filter_imag).astype(jnp.bfloat16)
        wave[1, r] = (real[r] * filter_imag + imag[r] * filter_real).astype(jnp.bfloat16)
    real_cos, imag_cos, real_sin, imag_sin = within()
    real, imag = real_cos - imag_sin, real_sin + imag_cos

    terms = []
    for r in range(kept):
        cos_row, sin_row = twist_v[0, r : r + 1], twist_v[1, r : r + 1]
        terms.append(real[r] * cos_row - imag[r] * sin_row)
    for r in range(kept):
        cos_row, sin_row = twist_v[0, r : r + 1], twist_v[1, r : r + 1]
        terms.append(real[r] * sin_row + imag[r] * cos_row)
    for b in range(tm_count):
        weights = [cosine(r, b) for r in range(kept)] + [-sine(r, b) for r in range(kept)]
        conv_out[b] = weighted(terms, weights).astype(jnp.bfloat16)
    for by in far_first:
        half = by // near
        remote(
            conv_out.at[tm_peer(by)], conv_in.at[by], conv_send.at[0], conv_recv.at[half], {"tm": tm_peer(by)}
        ).start()

    bytes_of(rows_in.at[pl.ds(halo, steps), others], rows_send.at[0])

    @pl.when(own_t < tm_count - 1)
    def _():
        bytes_of(rows_in.at[pl.ds(0, halo)], halo_send.at[0])

    for parity in range(2):
        collect(spec_in.at[parity], spec_send.at[parity])
    bytes_of(mixed_in.at[pl.ds(0, tm_count - 1)], mix_send.at[0])

    def gate_copy(half, owner, recv, to):
        block = gated.at[half, owner]
        return remote(block, block, gate_send.at[half], gate_recv.at[half, recv], {"chan": to})

    for half in range(2):
        if half == 0:
            bytes_of(conv_in.at[pl.ds(0, near - 1)], conv_recv.at[0])
        else:
            bytes_of(conv_in.at[pl.ds(0, near)], conv_recv.at[1])
        for by in range(half * near, (half + 1) * near):
            source = tm_peer(by)
            arrived = conv_in[by] if by else conv_out[source]
            value = (arrived.astype(jnp.float32) + direct_t[source]) * gate_t[source]
            gated[half, own_c, pl.ds(by % near * share, share)] = value.astype(jnp.bfloat16)
        gate_copy(half, own_c, 0, x_c).start()
        gate_copy(half, own_c, 1, core_c).start()
    for half in range(2):
        bytes_of(gated.at[half, x_c], gate_recv.at[half, 0])
        gate_copy(half, x_c, 2, core_c).start()

    total = None
    for half in range(2):
        bytes_of(gated.at[half, core_c], gate_recv.at[half, 1])
        bytes_of(gated.at[half, far_c], gate_recv.at[half, 2])
        rows = gated[half].reshape(chan_count * channels // 2, steps)
        term = jnp.dot(out_weight_t[half], rows, preferred_element_type=jnp.float32)
        total = term if total is None else total + term
    out[...] = (total.T + out_bias_v[...]).astype(out.dtype)

    bytes_of(conv_in.at[pl.ds(0, tm_count - 1)], conv_send.at[0])
    for half in range(2):
        bytes_of(gated.at[half, pl.ds(0, chan_count - 1)], gate_send.at[half])


def fused(
    series,
    proj_weight,
    proj_bias,
    short_taps,
    short_bias,
    spectrum,
    skip_gain,
    out_weight,
    out_bias,
):
    steps, channels = series.shape
    width = proj_weight.shape[0]
    tm_count, chan_count = lax.axis_size("tm"), lax.axis_size("chan")
    dft, twist = make_tables(tm_count, steps)
    share, slots, halo = channels // tm_count, 2 * tm_count, 16
    spread_shape = (tm_count, share, steps)
    vmem, dma = pltpu.VMEM, pltpu.SemaphoreType.DMA
    operands = [
        series,
        proj_weight.transpose(1, 0, 2),
        proj_bias,
        short_taps,
        short_bias,
        spectrum,
        skip_gain.reshape(1, channels),
        out_weight,
        out_bias.reshape(1, channels),
        jnp.asarray(dft),
        jnp.asarray(twist),
    ]
    return pl.pallas_call(
        functools.partial(kernel, tm_count, chan_count),
        out_shape=jax.ShapeDtypeStruct((steps, channels), jnp.bfloat16),
        in_specs=[pl.BlockSpec(memory_space=pl.ANY)] * len(operands),
        out_specs=pl.BlockSpec(memory_space=pltpu.VMEM),
        scratch_shapes=[
            vmem((halo + steps, width), jnp.bfloat16),
            vmem((width, 3 * channels), jnp.bfloat16),
            vmem(proj_bias.shape, jnp.float32),
            vmem(short_taps.shape, jnp.float32),
            vmem(short_bias.shape, jnp.float32),
            vmem((2, 2, steps, channels), jnp.float32),
            vmem((1, channels), jnp.float32),
            vmem((width, channels), jnp.bfloat16),
            vmem((2, channels, width // 2), jnp.bfloat16),
            vmem((1, channels), jnp.float32),
            vmem(dft.shape, jnp.bfloat16),
            vmem(twist.shape, jnp.float32),
            vmem((3, halo + steps, channels), jnp.float32),
            vmem((2, tm_count, 2, share, steps), jnp.bfloat16),
            vmem((2, tm_count, 2, share, steps), jnp.bfloat16),
            vmem(spread_shape, jnp.bfloat16),
            vmem(spread_shape, jnp.bfloat16),
            vmem((2, tm_count + 1, share, steps), jnp.bfloat16),
            vmem(spread_shape, jnp.bfloat16),
            vmem(spread_shape, jnp.bfloat16),
            vmem(spread_shape, jnp.float32),
            vmem(spread_shape, jnp.float32),
            vmem((2, chan_count, channels // 2, steps), jnp.bfloat16),
            dma((len(operands) + 2,)),
            dma((1,)),
            dma((4,)),
            *[dma((2,))] * 9,
            dma((2, 3)),
        ],
        compiler_params=pltpu.CompilerParams(
            collective_id=0, has_side_effects=True, vmem_limit_bytes=32 * 1024 * 1024
        ),
    )(*[pltpu.with_memory_space_constraint(operand, pltpu.HBM) for operand in operands])


def solution(mesh):
    sizes = mesh.shape

    def program(*arrays):
        share = arrays[0].shape[1] // sizes["chan"] // sizes["tm"]
        wide = share > 0 and share % 16 == 0 and sizes["tm"] >= 4 and sizes["chan"] == 4
        wide = wide and sizes["tm"] & sizes["tm"] - 1 == 0
        return jax.shard_map(
            fused if wide else shards,
            mesh=mesh,
            in_specs=(
                P("tm", "chan"),
                P(None, None, "chan"),
                P(None, "chan"),
                P(None, None, "chan"),
                P(None, "chan"),
                P(None, "tm", None, None, "chan"),
                P("chan"),
                P(),
                P("chan"),
            ),
            out_specs=P("tm", "chan"),
            check_vma=False,
        )(*arrays)

    return program
```

```python
import functools
import math

import jax
import jax.numpy as jnp
import numpy as np
from jax import lax
from jax.experimental import pallas as pl
from jax.experimental.pallas import tpu as pltpu
from jax.sharding import PartitionSpec as P

MESH = pl.DeviceIdType.MESH


def from_behind(array, axis, by):
    length = lax.axis_size(axis)
    pairs = [(i, i + by) for i in range(length) if 0 <= i + by < length]
    return lax.ppermute(array, axis, pairs)


def partner_2(block, axis, bit):
    count = lax.axis_size(axis)
    route = []
    for low in range(count):
        high = low | 1 << bit
        if high != low and high < count:
            route += [(low, high), (high, low)]
    return lax.ppermute(block, axis, route)


def reverse_bits(values, digits):
    result = jnp.zeros_like(values)
    for bit_level in range(digits):
        result = result | (values >> bit_level & 1) << digits - 1 - bit_level
    return result


def turning(numer, denom):
    angle = numer.astype(jnp.float32) * (-2.0 * math.pi / denom)
    return (jnp.cos(angle), jnp.sin(angle))


def complex_times(stacked, real_part, imag_part):
    return jnp.stack(
        [
            stacked[0] * real_part - stacked[1] * imag_part,
            stacked[0] * imag_part + stacked[1] * real_part,
        ]
    )


def dft_rows(signals, period, inverse):
    indices = jnp.arange(period, dtype=jnp.int32)
    cosine, sine_part = turning(indices[:, None] * indices[None, :] % period, period)
    if inverse:
        sine_part = -sine_part
    stacked = jnp.concatenate([cosine, sine_part], 0)
    result = jnp.einsum("bt,retc->rebc", stacked, signals, precision=lax.Precision.HIGHEST)
    real_out = result[0, :, :period] - result[1, :, period:]
    imag_out = result[1, :, :period] + result[0, :, period:]
    return jnp.stack([real_out, imag_out])


def shards(
    series,
    proj_weight,
    proj_bias,
    short_taps,
    short_bias,
    spectrum,
    skip_gain,
    out_weight,
    out_bias,
):
    steps_dev = series.shape[0]
    model_width = proj_weight.shape[0]
    channels = proj_weight.shape[2]
    flat_weight = proj_weight.reshape(model_width, 3 * channels)
    weight_rows = flat_weight
    projected = jnp.dot(
        lax.all_gather(series, "chan", axis=1, tiled=True),
        weight_rows,
        preferred_element_type=jnp.float32,
    )
    projected = (projected.reshape(steps_dev, 3, channels) + proj_bias).astype(jnp.bfloat16)
    taps_count = short_taps.shape[0]
    earlier = from_behind(projected[steps_dev - taps_count + 1 :], "tm", 1)
    extended = jnp.concatenate([earlier, projected], 0).astype(jnp.float32)
    streams = short_bias + short_taps[0] * extended[taps_count - 1 :]
    for offset in range(1, taps_count):
        streams = (
            streams
            + short_taps[offset]
            * extended[taps_count - 1 - offset : taps_count - 1 - offset + steps_dev]
        )
    streams = lax.optimization_barrier(streams.astype(jnp.bfloat16)).astype(jnp.float32)
    gate_out = streams[:, 0]
    mixed_in = lax.optimization_barrier((streams[:, 1] * streams[:, 2]).astype(jnp.bfloat16))
    signal = mixed_in.astype(jnp.float32)
    tm_count = lax.axis_size("tm")
    digits = tm_count.bit_length() - 1
    own_index = lax.axis_index("tm")
    period = 2 * tm_count * steps_dev
    positions = jnp.arange(steps_dev, dtype=jnp.int32)
    own_rows = 2 * reverse_bits(own_index, digits) + jnp.arange(2, dtype=jnp.int32)
    twist_cos, twist_sin = turning(own_rows[:, None] * positions[None, :] % period, period)
    twist_cos, twist_sin = (twist_cos[:, :, None], twist_sin[:, :, None])
    half_cos, half_sin = turning(own_index, 2 * tm_count)
    zero_field = jnp.zeros_like(signal)
    current = jnp.stack(
        [jnp.stack([signal, signal * half_cos]), jnp.stack([zero_field, signal * half_sin])]
    )
    for bit_level in reversed(range(digits)):
        partner = partner_2(current, "tm", bit_level)
        half_span = 1 << bit_level
        rot_cos, rot_sin = turning(own_index % half_span, 2 * half_span)
        upper_half = own_index >> bit_level & 1 == 1
        current = jnp.where(
            upper_half, complex_times(partner - current, rot_cos, rot_sin), current + partner
        )
    twisted = complex_times(current, twist_cos, twist_sin)
    spectral = dft_rows(twisted, steps_dev, False)
    response = spectrum.reshape(2, 2, steps_dev, channels)
    product = complex_times(spectral, response[0], response[1])
    returned = dft_rows(product, steps_dev, True)
    current = complex_times(returned, twist_cos, -twist_sin)
    for bit_level in range(digits):
        partner = partner_2(current, "tm", bit_level)
        half_span = 1 << bit_level
        rot_cos, rot_sin = turning(own_index % half_span, 2 * half_span)
        rot_sin = -rot_sin
        upper_half = own_index >> bit_level & 1 == 1
        current = jnp.where(
            upper_half,
            partner - complex_times(current, rot_cos, rot_sin),
            current + complex_times(partner, rot_cos, rot_sin),
        )
    convolved = current[0, 0] + half_cos * current[0, 1] + half_sin * current[1, 1]
    convolved = convolved * (1.0 / period)
    gated_rows = ((convolved + skip_gain * signal) * gate_out).astype(jnp.bfloat16)
    column_start = lax.axis_index("chan") * channels
    weight_rows = lax.dynamic_slice_in_dim(out_weight, column_start, channels, 0)
    partial_value = jnp.dot(gated_rows, weight_rows, preferred_element_type=jnp.float32)
    mixed_out = lax.psum_scatter(partial_value, "chan", scatter_dimension=1, tiled=True)
    return (mixed_out + out_bias).astype(jnp.bfloat16)


def make_tables(tm_count, steps):
    count, period = 2 * tm_count, 2 * tm_count * steps
    rows = np.arange(steps)
    angle = 2.0 * np.pi * (rows[:, None] * rows[None, :] % steps) / steps
    dft = np.stack([np.cos(angle), np.sin(angle)]).astype(jnp.bfloat16)
    angle = 2.0 * np.pi * (np.arange(count)[:, None] * rows[None, :] % period) / period
    twist = np.stack([np.cos(angle), np.sin(angle)]).astype(np.float32)
    return dft, twist


def flip(value, digits):
    result = 0
    for bit_level in range(digits):
        result |= (value >> bit_level & 1) << digits - 1 - bit_level
    return result


def across_bits(index, by):
    result, bit = index, 1
    while bit <= by:
        if by & bit:
            result = result + bit * (1 - 2 * lax.rem(lax.div(index, bit), 2))
        bit *= 2
    return result


def weighted(blocks, weights):
    total = None
    for block, weight in zip(blocks, weights):
        if abs(weight) < 1e-12:
            continue
        if abs(weight - 1.0) < 1e-12:
            term = block
        elif abs(weight + 1.0) < 1e-12:
            term = -block
        else:
            term = block * float(weight)
        total = term if total is None else total + term
    return total


def kernel(
    tm_count,
    chan_count,
    series,
    weight,
    proj_bias,
    taps,
    short_bias,
    spectrum,
    skip_gain,
    out_weight,
    out_bias,
    dft,
    twist,
    out,
    rows_in,
    weight_v,
    proj_bias_v,
    taps_v,
    short_bias_v,
    spectrum_v,
    skip_v,
    out_weight_v,
    out_weight_t,
    out_bias_v,
    dft_v,
    twist_v,
    projected,
    spec_out,
    spec_in,
    mixed_out,
    mixed_in,
    wave,
    conv_out,
    conv_in,
    gate_t,
    direct_t,
    gated,
    local_sem,
    rows_send,
    rows_recv,
    halo_send,
    halo_recv,
    spec_send,
    spec_recv,
    mix_send,
    mix_recv,
    conv_send,
    conv_recv,
    gate_send,
    gate_recv,
):
    steps, channels = series.shape
    halo = rows_in.shape[0] - steps
    share = channels // tm_count
    digits = tm_count.bit_length() - 1
    slots = 2 * tm_count
    own_t, own_c = lax.axis_index("tm"), lax.axis_index("chan")
    columns = lambda c: pl.ds(pl.multiple_of(c * channels, channels), channels)
    next_t, last_t = lax.rem(own_t + 1, tm_count), lax.rem(own_t + tm_count - 1, tm_count)
    tm_peer = lambda by: across_bits(own_t, by)
    chan_peer = lambda by: across_bits(own_c, by)
    far_first = list(range(tm_count // 2, tm_count)) + list(range(1, tm_count // 2))

    barrier = pltpu.get_barrier_semaphore()
    greet = lambda where: pl.semaphore_signal(barrier, inc=1, device_id=where, device_id_type=MESH)
    for by in range(1, chan_count):
        greet({"chan": chan_peer(by)})
    for by in range(1, tm_count):
        greet({"tm": tm_peer(by)})
    for by in range(1, chan_count):
        greet({"tm": next_t, "chan": chan_peer(by)})
        greet({"tm": last_t, "chan": chan_peer(by)})

    pairs = [
        (series, rows_in.at[pl.ds(halo, steps), columns(own_c)]),
        (spectrum.at[:, 0], spectrum_v),
        *[(weight.at[j], weight_v.at[:, pl.ds((j + 2) % 3 * channels, channels)]) for j in range(3)],
        (proj_bias, proj_bias_v),
        (taps, taps_v),
        (short_bias, short_bias_v),
        (dft, dft_v),
        (twist, twist_v),
        (skip_gain, skip_v),
        (out_weight.at[:, columns(own_c)], out_weight_v),
        (out_bias, out_bias_v),
    ]
    local = [pltpu.make_async_copy(a, b, local_sem.at[i]) for i, (a, b) in enumerate(pairs)]
    local[1].start()

    def remote(src, dst, send, recv, where):
        return pltpu.make_async_remote_copy(
            src_ref=src, dst_ref=dst, send_sem=send, recv_sem=recv, device_id=where, device_id_type=MESH
        )

    residue = 2 * sum((own_t >> i & 1) << digits - 1 - i for i in range(digits))
    down = lax.broadcasted_iota(jnp.int32, (steps, steps), 0)
    across = lax.broadcasted_iota(jnp.int32, (steps, steps), 1)

    def turn_spectrum(parity):
        wanted = jnp.where(residue + parity > tm_count, steps - 1 - down, down)
        order = jnp.where(wanted == across, 1.0 / (slots * steps), 0.0).astype(jnp.bfloat16)
        for part in range(2):
            block = spectrum_v[part, parity].astype(jnp.bfloat16)
            block = lax.dot_general(
                block, order, (((0,), (0,)), ((), ())), preferred_element_type=jnp.float32
            )
            spec_out[parity, :, part] = block.astype(jnp.bfloat16).reshape(tm_count, share, steps)

    early = own_t < tm_count // 2

    @pl.when(early)
    def _():
        local[1].wait()
        turn_spectrum(0)
        turn_spectrum(1)

    pl.semaphore_wait(barrier, chan_count - 1 + tm_count - 1 + 2 * (chan_count - 1))

    core_c, x_c, far_c = chan_peer(1), chan_peer(2), chan_peer(3)
    part_rows = steps // 2

    def rows_copy(owner, first, count, recv, to):
        block = rows_in.at[pl.ds(halo + first, count), columns(owner)]
        source = series.at[pl.ds(first, count)] if owner is own_c else block
        return remote(source, block, rows_send.at[0], rows_recv.at[recv], {"chan": to})

    def halo_copy(by, owner):
        return remote(
            series.at[pl.ds(steps - halo, halo)],
            rows_in.at[pl.ds(0, halo), columns(owner)],
            halo_send.at[0],
            halo_recv.at[0],
            {"tm": next_t, "chan": chan_peer(by)},
        )

    for i in range(2):
        rows_copy(own_c, i * part_rows, part_rows, i, x_c).start()
    rows_copy(own_c, part_rows, part_rows, 3, far_c).start()
    rows_copy(own_c, 0, steps, 2, core_c).start()

    @pl.when(own_t < tm_count - 1)
    def _():
        for by in range(chan_count):
            halo_copy(by, own_c).start()

    @pl.when(own_t == 0)
    def _():
        rows_in[pl.ds(0, halo), :] = jnp.zeros((halo, rows_in.shape[1]), rows_in.dtype)

    def bytes_of(ref, sem):
        pltpu.make_async_copy(ref, ref, sem).wait()

    def spread(src, dst, send, recv):
        for by in far_first:
            remote(src.at[tm_peer(by)], dst.at[own_t], send, recv, {"tm": tm_peer(by)}).start()
        dst[own_t] = src[own_t]

    def collect(dst, recv):
        bytes_of(dst.at[pl.ds(0, tm_count - 1)], recv)

    for copy in local[:1] + local[2:]:
        copy.start()

    def relay_rows():
        bytes_of(rows_in.at[pl.ds(halo, part_rows), columns(x_c)], rows_recv.at[0])
        rows_copy(x_c, 0, part_rows, 4, core_c).start()

    def spread_spectrum(parity):
        spread(spec_out.at[parity], spec_in.at[parity], spec_send.at[parity], spec_recv.at[parity])

    @pl.when(early)
    def _():
        spread_spectrum(0)
        spread_spectrum(1)
        relay_rows()

    @pl.when(jnp.logical_not(early))
    def _():
        local[1].wait()
        turn_spectrum(0)
        spread_spectrum(0)
        relay_rows()
        turn_spectrum(1)
        spread_spectrum(1)

    local[0].wait()
    for copy in local[2:]:
        copy.wait()
    others = pl.ds(0, (chan_count - 1) * channels)

    @pl.when(own_t > 0)
    def _():
        bytes_of(rows_in.at[pl.ds(0, halo)], halo_recv.at[0])

    bytes_of(rows_in.at[pl.ds(halo, steps), columns(core_c)], rows_recv.at[2])

    def of_chip(chip):
        inputs = pl.ds(pl.multiple_of(chip * 2 * channels, 2 * channels), 2 * channels)
        return jnp.dot(
            rows_in[:, inputs], weight_v[inputs, pl.ds(0, 2 * channels)], preferred_element_type=jnp.float32
        )

    own_chip = lax.div(own_c, 2)
    near_sum = of_chip(own_chip)
    bytes_of(rows_in.at[pl.ds(halo, part_rows), columns(x_c)], rows_recv.at[1])
    for i in range(2):
        bytes_of(rows_in.at[pl.ds(halo, part_rows), columns(far_c)], rows_recv.at[3 + i])
    sums = near_sum + of_chip(1 - own_chip)

    streams = []
    for j in (1, 2, 0):
        if j:
            value = sums[:, (j - 1) * channels : j * channels]
        else:
            value = jnp.dot(
                rows_in[...], weight_v[:, pl.ds(2 * channels, channels)], preferred_element_type=jnp.float32
            )
        value = (value + proj_bias_v[j : j + 1]).astype(jnp.bfloat16).astype(jnp.float32)
        projected[j] = value

        @pl.when(own_t == 0)
        def _():
            projected[j, pl.ds(0, halo)] = jnp.zeros((halo, channels), jnp.float32)

        stream = short_bias_v[j : j + 1] + taps_v[0, j : j + 1] * projected[j, pl.ds(halo, steps)]
        for k in range(1, taps.shape[0]):
            stream = stream + taps_v[k, j : j + 1] * projected[j, pl.ds(halo - k, steps)]
        stream = stream.astype(jnp.bfloat16).astype(jnp.float32)
        if j == 2:
            signal = (streams[0] * stream).astype(jnp.bfloat16).astype(jnp.float32)
            mixed_out[...] = signal.T.astype(jnp.bfloat16).reshape(tm_count, share, steps)
            spread(mixed_out, mixed_in, mix_send.at[0], mix_recv.at[0])
        streams.append(stream)
    gate_t[...] = streams[2].T.reshape(tm_count, share, steps)
    direct_t[...] = (skip_v[...] * signal).T.reshape(tm_count, share, steps)
    near = tm_count // 2
    for half in range(2):
        blocks = [
            out_weight_v[pl.ds(pl.multiple_of(c * channels + tm_peer(half * near + by) * share, share), share)]
            for c in range(chan_count)
            for by in range(near)
        ]
        out_weight_t[half] = jnp.concatenate(blocks, 0).astype(jnp.float32).T.astype(jnp.bfloat16)

    collect(mixed_in, mix_recv.at[0])
    blocks = [mixed_in[b].astype(jnp.float32) for b in range(tm_count)]
    turns = 2.0 * np.pi * np.arange(slots) / slots
    cosine = lambda r, b: math.cos(turns[r * b % slots])
    sine = lambda r, b: math.sin(turns[r * b % slots])
    kept = tm_count + 1

    for r in range(kept):
        real = weighted(blocks, [cosine(r, b) for b in range(tm_count)])
        imag = weighted(blocks, [-sine(r, b) for b in range(tm_count)])
        cos_row, sin_row = twist_v[0, r : r + 1], twist_v[1, r : r + 1]
        if imag is None:
            turned = (real * cos_row, -(real * sin_row))
        else:
            turned = (real * cos_row + imag * sin_row, imag * cos_row - real * sin_row)
        for part in range(2):
            wave[part, r] = turned[part].astype(jnp.bfloat16)

    def within():
        rows = wave[...].reshape(2 * kept * share, steps)
        first = jnp.dot(rows, dft_v[0], preferred_element_type=jnp.float32)
        second = jnp.dot(rows, dft_v[1], preferred_element_type=jnp.float32)
        half = kept * share
        return [a.reshape(kept, share, steps) for a in (first[:half], first[half:], second[:half], second[half:])]

    real_cos, imag_cos, real_sin, imag_sin = within()
    real, imag = real_cos + imag_sin, imag_cos - real_sin
    for parity in range(2):
        collect(spec_in.at[parity], spec_recv.at[parity])

    def filter_of(part, r):
        return spec_in[r % 2, flip(r // 2, digits), part].astype(jnp.float32)

    for r in range(kept):
        filter_real, filter_imag = filter_of(0, r), filter_of(1, r)
        if 0 < r < tm_count:
            filter_real = filter_real + filter_of(0, slots - r)
            filter_imag = filter_imag - filter_of(1, slots - r)
        wave[0, r] = (real[r] * filter_real - imag[r] * filter_imag).astype(jnp.bfloat16)
        wave[1, r] = (real[r] * filter_imag + imag[r] * filter_real).astype(jnp.bfloat16)
    real_cos, imag_cos, real_sin, imag_sin = within()
    real, imag = real_cos - imag_sin, real_sin + imag_cos

    terms = []
    for r in range(kept):
        cos_row, sin_row = twist_v[0, r : r + 1], twist_v[1, r : r + 1]
        terms.append(real[r] * cos_row - imag[r] * sin_row)
    for r in range(kept):
        cos_row, sin_row = twist_v[0, r : r + 1], twist_v[1, r : r + 1]
        terms.append(real[r] * sin_row + imag[r] * cos_row)
    for b in range(tm_count):
        weights = [cosine(r, b) for r in range(kept)] + [-sine(r, b) for r in range(kept)]
        conv_out[b] = weighted(terms, weights).astype(jnp.bfloat16)
    for by in far_first:
        half = by // near
        remote(
            conv_out.at[tm_peer(by)], conv_in.at[by], conv_send.at[0], conv_recv.at[half], {"tm": tm_peer(by)}
        ).start()

    bytes_of(rows_in.at[pl.ds(halo, steps), others], rows_send.at[0])

    @pl.when(own_t < tm_count - 1)
    def _():
        bytes_of(rows_in.at[pl.ds(0, halo)], halo_send.at[0])

    for parity in range(2):
        collect(spec_in.at[parity], spec_send.at[parity])
    bytes_of(mixed_in.at[pl.ds(0, tm_count - 1)], mix_send.at[0])

    def gate_copy(half, owner, recv, to):
        block = gated.at[half, owner]
        return remote(block, block, gate_send.at[half], gate_recv.at[half, recv], {"chan": to})

    for half in range(2):
        if half == 0:
            bytes_of(conv_in.at[pl.ds(0, near - 1)], conv_recv.at[0])
        else:
            bytes_of(conv_in.at[pl.ds(0, near)], conv_recv.at[1])
        for by in range(half * near, (half + 1) * near):
            source = tm_peer(by)
            arrived = conv_in[by] if by else conv_out[source]
            value = (arrived.astype(jnp.float32) + direct_t[source]) * gate_t[source]
            gated[half, own_c, pl.ds(by % near * share, share)] = value.astype(jnp.bfloat16)
        gate_copy(half, own_c, 0, x_c).start()
        if half:
            gate_copy(half, own_c, 2, far_c).start()
        gate_copy(half, own_c, 1, core_c).start()

    bytes_of(gated.at[0, x_c], gate_recv.at[0, 0])
    gate_copy(0, x_c, 2, core_c).start()

    total = None
    for half in range(2):
        bytes_of(gated.at[half, core_c], gate_recv.at[half, 1])
        if half:
            bytes_of(gated.at[half, x_c], gate_recv.at[half, 0])
        bytes_of(gated.at[half, far_c], gate_recv.at[half, 2])
        rows = gated[half].reshape(chan_count * channels // 2, steps)
        term = jnp.dot(out_weight_t[half], rows, preferred_element_type=jnp.float32)
        total = term if total is None else total + term
    out[...] = (total.T + out_bias_v[...]).astype(out.dtype)

    bytes_of(conv_in.at[pl.ds(0, tm_count - 1)], conv_send.at[0])
    for half in range(2):
        bytes_of(gated.at[half, pl.ds(0, chan_count - 1)], gate_send.at[half])


def fused(
    series,
    proj_weight,
    proj_bias,
    short_taps,
    short_bias,
    spectrum,
    skip_gain,
    out_weight,
    out_bias,
):
    steps, channels = series.shape
    width = proj_weight.shape[0]
    tm_count, chan_count = lax.axis_size("tm"), lax.axis_size("chan")
    dft, twist = make_tables(tm_count, steps)
    share, slots, halo = channels // tm_count, 2 * tm_count, 16
    spread_shape = (tm_count, share, steps)
    vmem, dma = pltpu.VMEM, pltpu.SemaphoreType.DMA
    operands = [
        series,
        proj_weight.transpose(1, 0, 2),
        proj_bias,
        short_taps,
        short_bias,
        spectrum,
        skip_gain.reshape(1, channels),
        out_weight,
        out_bias.reshape(1, channels),
        jnp.asarray(dft),
        jnp.asarray(twist),
    ]
    return pl.pallas_call(
        functools.partial(kernel, tm_count, chan_count),
        out_shape=jax.ShapeDtypeStruct((steps, channels), jnp.bfloat16),
        in_specs=[pl.BlockSpec(memory_space=pl.ANY)] * len(operands),
        out_specs=pl.BlockSpec(memory_space=pltpu.VMEM),
        scratch_shapes=[
            vmem((halo + steps, width), jnp.bfloat16),
            vmem((width, 3 * channels), jnp.bfloat16),
            vmem(proj_bias.shape, jnp.float32),
            vmem(short_taps.shape, jnp.float32),
            vmem(short_bias.shape, jnp.float32),
            vmem((2, 2, steps, channels), jnp.float32),
            vmem((1, channels), jnp.float32),
            vmem((width, channels), jnp.bfloat16),
            vmem((2, channels, width // 2), jnp.bfloat16),
            vmem((1, channels), jnp.float32),
            vmem(dft.shape, jnp.bfloat16),
            vmem(twist.shape, jnp.float32),
            vmem((3, halo + steps, channels), jnp.float32),
            vmem((2, tm_count, 2, share, steps), jnp.bfloat16),
            vmem((2, tm_count, 2, share, steps), jnp.bfloat16),
            vmem(spread_shape, jnp.bfloat16),
            vmem(spread_shape, jnp.bfloat16),
            vmem((2, tm_count + 1, share, steps), jnp.bfloat16),
            vmem(spread_shape, jnp.bfloat16),
            vmem(spread_shape, jnp.bfloat16),
            vmem(spread_shape, jnp.float32),
            vmem(spread_shape, jnp.float32),
            vmem((2, chan_count, channels // 2, steps), jnp.bfloat16),
            dma((len(operands) + 2,)),
            dma((1,)),
            dma((5,)),
            *[dma((2,))] * 9,
            dma((2, 3)),
        ],
        compiler_params=pltpu.CompilerParams(
            collective_id=0, has_side_effects=True, vmem_limit_bytes=32 * 1024 * 1024
        ),
    )(*[pltpu.with_memory_space_constraint(operand, pltpu.HBM) for operand in operands])


def solution(mesh):
    sizes = mesh.shape

    def program(*arrays):
        share = arrays[0].shape[1] // sizes["chan"] // sizes["tm"]
        wide = share > 0 and share % 16 == 0 and sizes["tm"] >= 4 and sizes["chan"] == 4
        wide = wide and sizes["tm"] & sizes["tm"] - 1 == 0
        return jax.shard_map(
            fused if wide else shards,
            mesh=mesh,
            in_specs=(
                P("tm", "chan"),
                P(None, None, "chan"),
                P(None, "chan"),
                P(None, None, "chan"),
                P(None, "chan"),
                P(None, "tm", None, None, "chan"),
                P("chan"),
                P(),
                P("chan"),
            ),
            out_specs=P("tm", "chan"),
            check_vma=False,
        )(*arrays)

    return program
```

```python
import functools
import math

import jax
import jax.numpy as jnp
import numpy as np
from jax import lax
from jax.experimental import pallas as pl
from jax.experimental.pallas import tpu as pltpu
from jax.sharding import PartitionSpec as P

MESH = pl.DeviceIdType.MESH


def from_behind(array, axis, by):
    length = lax.axis_size(axis)
    pairs = [(i, i + by) for i in range(length) if 0 <= i + by < length]
    return lax.ppermute(array, axis, pairs)


def partner_2(block, axis, bit):
    count = lax.axis_size(axis)
    route = []
    for low in range(count):
        high = low | 1 << bit
        if high != low and high < count:
            route += [(low, high), (high, low)]
    return lax.ppermute(block, axis, route)


def reverse_bits(values, digits):
    result = jnp.zeros_like(values)
    for bit_level in range(digits):
        result = result | (values >> bit_level & 1) << digits - 1 - bit_level
    return result


def turning(numer, denom):
    angle = numer.astype(jnp.float32) * (-2.0 * math.pi / denom)
    return (jnp.cos(angle), jnp.sin(angle))


def complex_times(stacked, real_part, imag_part):
    return jnp.stack(
        [
            stacked[0] * real_part - stacked[1] * imag_part,
            stacked[0] * imag_part + stacked[1] * real_part,
        ]
    )


def dft_rows(signals, period, inverse):
    indices = jnp.arange(period, dtype=jnp.int32)
    cosine, sine_part = turning(indices[:, None] * indices[None, :] % period, period)
    if inverse:
        sine_part = -sine_part
    stacked = jnp.concatenate([cosine, sine_part], 0)
    result = jnp.einsum("bt,retc->rebc", stacked, signals, precision=lax.Precision.HIGHEST)
    real_out = result[0, :, :period] - result[1, :, period:]
    imag_out = result[1, :, :period] + result[0, :, period:]
    return jnp.stack([real_out, imag_out])


def shards(
    series,
    proj_weight,
    proj_bias,
    short_taps,
    short_bias,
    spectrum,
    skip_gain,
    out_weight,
    out_bias,
):
    steps_dev = series.shape[0]
    model_width = proj_weight.shape[0]
    channels = proj_weight.shape[2]
    flat_weight = proj_weight.reshape(model_width, 3 * channels)
    weight_rows = flat_weight
    projected = jnp.dot(
        lax.all_gather(series, "chan", axis=1, tiled=True),
        weight_rows,
        preferred_element_type=jnp.float32,
    )
    projected = (projected.reshape(steps_dev, 3, channels) + proj_bias).astype(jnp.bfloat16)
    taps_count = short_taps.shape[0]
    earlier = from_behind(projected[steps_dev - taps_count + 1 :], "tm", 1)
    extended = jnp.concatenate([earlier, projected], 0).astype(jnp.float32)
    streams = short_bias + short_taps[0] * extended[taps_count - 1 :]
    for offset in range(1, taps_count):
        streams = (
            streams
            + short_taps[offset]
            * extended[taps_count - 1 - offset : taps_count - 1 - offset + steps_dev]
        )
    streams = lax.optimization_barrier(streams.astype(jnp.bfloat16)).astype(jnp.float32)
    gate_out = streams[:, 0]
    mixed_in = lax.optimization_barrier((streams[:, 1] * streams[:, 2]).astype(jnp.bfloat16))
    signal = mixed_in.astype(jnp.float32)
    tm_count = lax.axis_size("tm")
    digits = tm_count.bit_length() - 1
    own_index = lax.axis_index("tm")
    period = 2 * tm_count * steps_dev
    positions = jnp.arange(steps_dev, dtype=jnp.int32)
    own_rows = 2 * reverse_bits(own_index, digits) + jnp.arange(2, dtype=jnp.int32)
    twist_cos, twist_sin = turning(own_rows[:, None] * positions[None, :] % period, period)
    twist_cos, twist_sin = (twist_cos[:, :, None], twist_sin[:, :, None])
    half_cos, half_sin = turning(own_index, 2 * tm_count)
    zero_field = jnp.zeros_like(signal)
    current = jnp.stack(
        [jnp.stack([signal, signal * half_cos]), jnp.stack([zero_field, signal * half_sin])]
    )
    for bit_level in reversed(range(digits)):
        partner = partner_2(current, "tm", bit_level)
        half_span = 1 << bit_level
        rot_cos, rot_sin = turning(own_index % half_span, 2 * half_span)
        upper_half = own_index >> bit_level & 1 == 1
        current = jnp.where(
            upper_half, complex_times(partner - current, rot_cos, rot_sin), current + partner
        )
    twisted = complex_times(current, twist_cos, twist_sin)
    spectral = dft_rows(twisted, steps_dev, False)
    response = spectrum.reshape(2, 2, steps_dev, channels)
    product = complex_times(spectral, response[0], response[1])
    returned = dft_rows(product, steps_dev, True)
    current = complex_times(returned, twist_cos, -twist_sin)
    for bit_level in range(digits):
        partner = partner_2(current, "tm", bit_level)
        half_span = 1 << bit_level
        rot_cos, rot_sin = turning(own_index % half_span, 2 * half_span)
        rot_sin = -rot_sin
        upper_half = own_index >> bit_level & 1 == 1
        current = jnp.where(
            upper_half,
            partner - complex_times(current, rot_cos, rot_sin),
            current + complex_times(partner, rot_cos, rot_sin),
        )
    convolved = current[0, 0] + half_cos * current[0, 1] + half_sin * current[1, 1]
    convolved = convolved * (1.0 / period)
    gated_rows = ((convolved + skip_gain * signal) * gate_out).astype(jnp.bfloat16)
    column_start = lax.axis_index("chan") * channels
    weight_rows = lax.dynamic_slice_in_dim(out_weight, column_start, channels, 0)
    partial_value = jnp.dot(gated_rows, weight_rows, preferred_element_type=jnp.float32)
    mixed_out = lax.psum_scatter(partial_value, "chan", scatter_dimension=1, tiled=True)
    return (mixed_out + out_bias).astype(jnp.bfloat16)


def make_tables(tm_count, steps):
    count, period = 2 * tm_count, 2 * tm_count * steps
    rows = np.arange(steps)
    angle = 2.0 * np.pi * (rows[:, None] * rows[None, :] % steps) / steps
    dft = np.stack([np.cos(angle), np.sin(angle)]).astype(jnp.bfloat16)
    angle = 2.0 * np.pi * (np.arange(count)[:, None] * rows[None, :] % period) / period
    twist = np.stack([np.cos(angle), np.sin(angle)]).astype(np.float32)
    return dft, twist


def flip(value, digits):
    result = 0
    for bit_level in range(digits):
        result |= (value >> bit_level & 1) << digits - 1 - bit_level
    return result


def across_bits(index, by):
    result, bit = index, 1
    while bit <= by:
        if by & bit:
            result = result + bit * (1 - 2 * lax.rem(lax.div(index, bit), 2))
        bit *= 2
    return result


def weighted(blocks, weights):
    total = None
    for block, weight in zip(blocks, weights):
        if abs(weight) < 1e-12:
            continue
        if abs(weight - 1.0) < 1e-12:
            term = block
        elif abs(weight + 1.0) < 1e-12:
            term = -block
        else:
            term = block * float(weight)
        total = term if total is None else total + term
    return total


def kernel(
    tm_count,
    chan_count,
    series,
    weight,
    proj_bias,
    taps,
    short_bias,
    spectrum,
    skip_gain,
    out_weight,
    out_bias,
    dft,
    twist,
    out,
    rows_in,
    weight_v,
    proj_bias_v,
    taps_v,
    short_bias_v,
    spectrum_v,
    skip_v,
    out_weight_v,
    out_weight_t,
    out_bias_v,
    dft_v,
    twist_v,
    projected,
    spec_out,
    spec_in,
    mixed_out,
    mixed_in,
    wave,
    conv_out,
    conv_in,
    gate_t,
    direct_t,
    gated,
    local_sem,
    rows_send,
    rows_recv,
    halo_send,
    halo_recv,
    spec_send,
    spec_recv,
    mix_send,
    mix_recv,
    conv_send,
    conv_recv,
    gate_send,
    gate_recv,
):
    steps, channels = series.shape
    halo = rows_in.shape[0] - steps
    share = channels // tm_count
    digits = tm_count.bit_length() - 1
    slots = 2 * tm_count
    own_t, own_c = lax.axis_index("tm"), lax.axis_index("chan")
    columns = lambda c: pl.ds(pl.multiple_of(c * channels, channels), channels)
    next_t, last_t = lax.rem(own_t + 1, tm_count), lax.rem(own_t + tm_count - 1, tm_count)
    tm_peer = lambda by: across_bits(own_t, by)
    chan_peer = lambda by: across_bits(own_c, by)
    far_first = list(range(tm_count // 2, tm_count)) + list(range(1, tm_count // 2))

    barrier = pltpu.get_barrier_semaphore()
    greet = lambda where: pl.semaphore_signal(barrier, inc=1, device_id=where, device_id_type=MESH)
    for by in range(1, chan_count):
        greet({"chan": chan_peer(by)})
    for by in range(1, tm_count):
        greet({"tm": tm_peer(by)})
    for by in range(1, chan_count):
        greet({"tm": next_t, "chan": chan_peer(by)})
        greet({"tm": last_t, "chan": chan_peer(by)})

    pairs = [
        (series, rows_in.at[pl.ds(halo, steps), columns(own_c)]),
        (spectrum.at[:, 0], spectrum_v),
        *[(weight.at[j], weight_v.at[:, pl.ds((j + 2) % 3 * channels, channels)]) for j in range(3)],
        (proj_bias, proj_bias_v),
        (taps, taps_v),
        (short_bias, short_bias_v),
        (dft, dft_v),
        (twist, twist_v),
        (skip_gain, skip_v),
        (out_weight.at[:, columns(own_c)], out_weight_v),
        (out_bias, out_bias_v),
    ]
    local = [pltpu.make_async_copy(a, b, local_sem.at[i]) for i, (a, b) in enumerate(pairs)]
    local[1].start()

    def remote(src, dst, send, recv, where):
        return pltpu.make_async_remote_copy(
            src_ref=src, dst_ref=dst, send_sem=send, recv_sem=recv, device_id=where, device_id_type=MESH
        )

    residue = 2 * sum((own_t >> i & 1) << digits - 1 - i for i in range(digits))
    down = lax.broadcasted_iota(jnp.int32, (steps, steps), 0)
    across = lax.broadcasted_iota(jnp.int32, (steps, steps), 1)

    def turn_spectrum(parity):
        wanted = jnp.where(residue + parity > tm_count, steps - 1 - down, down)
        order = jnp.where(wanted == across, 1.0 / (slots * steps), 0.0).astype(jnp.bfloat16)
        for part in range(2):
            block = spectrum_v[part, parity].astype(jnp.bfloat16)
            block = jnp.dot(order, block, preferred_element_type=jnp.float32).T
            spec_out[parity, :, part] = block.astype(jnp.bfloat16).reshape(tm_count, share, steps)

    early = own_t < tm_count // 2

    @pl.when(early)
    def _():
        local[1].wait()
        turn_spectrum(0)
        turn_spectrum(1)

    pl.semaphore_wait(barrier, chan_count - 1 + tm_count - 1 + 2 * (chan_count - 1))

    core_c, x_c, far_c = chan_peer(1), chan_peer(2), chan_peer(3)
    part_rows = steps // 2

    def rows_copy(owner, first, count, recv, to):
        block = rows_in.at[pl.ds(halo + first, count), columns(owner)]
        source = series.at[pl.ds(first, count)] if owner is own_c else block
        return remote(source, block, rows_send.at[0], rows_recv.at[recv], {"chan": to})

    def halo_copy(by, owner):
        return remote(
            series.at[pl.ds(steps - halo, halo)],
            rows_in.at[pl.ds(0, halo), columns(owner)],
            halo_send.at[0],
            halo_recv.at[0],
            {"tm": next_t, "chan": chan_peer(by)},
        )

    for i in range(2):
        rows_copy(own_c, i * part_rows, part_rows, i, x_c).start()
    rows_copy(own_c, part_rows, part_rows, 3, far_c).start()
    rows_copy(own_c, 0, steps, 2, core_c).start()

    @pl.when(own_t < tm_count - 1)
    def _():
        for by in range(chan_count):
            halo_copy(by, own_c).start()

    @pl.when(own_t == 0)
    def _():
        rows_in[pl.ds(0, halo), :] = jnp.zeros((halo, rows_in.shape[1]), rows_in.dtype)

    def bytes_of(ref, sem):
        pltpu.make_async_copy(ref, ref, sem).wait()

    def spread(src, dst, send, recv):
        for by in far_first:
            remote(src.at[tm_peer(by)], dst.at[own_t], send, recv, {"tm": tm_peer(by)}).start()
        dst[own_t] = src[own_t]

    def collect(dst, recv):
        bytes_of(dst.at[pl.ds(0, tm_count - 1)], recv)

    for copy in local[:1] + local[2:]:
        copy.start()

    def relay_rows():
        bytes_of(rows_in.at[pl.ds(halo, part_rows), columns(x_c)], rows_recv.at[0])
        rows_copy(x_c, 0, part_rows, 4, core_c).start()

    def spread_spectrum(parity):
        spread(spec_out.at[parity], spec_in.at[parity], spec_send.at[parity], spec_recv.at[parity])

    @pl.when(early)
    def _():
        spread_spectrum(0)
        spread_spectrum(1)
        relay_rows()

    @pl.when(jnp.logical_not(early))
    def _():
        local[1].wait()
        for parity in range(2):
            turn_spectrum(parity)
            spread_spectrum(parity)
        relay_rows()

    local[0].wait()
    for copy in local[2:]:
        copy.wait()
    others = pl.ds(0, (chan_count - 1) * channels)

    @pl.when(own_t > 0)
    def _():
        bytes_of(rows_in.at[pl.ds(0, halo)], halo_recv.at[0])

    bytes_of(rows_in.at[pl.ds(halo, steps), columns(core_c)], rows_recv.at[2])

    def of_chip(chip):
        inputs = pl.ds(pl.multiple_of(chip * 2 * channels, 2 * channels), 2 * channels)
        return jnp.dot(
            rows_in[:, inputs], weight_v[inputs, pl.ds(0, 2 * channels)], preferred_element_type=jnp.float32
        )

    own_chip = lax.div(own_c, 2)
    near_sum = of_chip(own_chip)
    bytes_of(rows_in.at[pl.ds(halo, part_rows), columns(x_c)], rows_recv.at[1])
    for i in range(2):
        bytes_of(rows_in.at[pl.ds(halo, part_rows), columns(far_c)], rows_recv.at[3 + i])
    sums = near_sum + of_chip(1 - own_chip)

    streams = []
    for j in (1, 2, 0):
        if j:
            value = sums[:, (j - 1) * channels : j * channels]
        else:
            value = jnp.dot(
                rows_in[...], weight_v[:, pl.ds(2 * channels, channels)], preferred_element_type=jnp.float32
            )
        value = (value + proj_bias_v[j : j + 1]).astype(jnp.bfloat16).astype(jnp.float32)
        projected[j] = value

        @pl.when(own_t == 0)
        def _():
            projected[j, pl.ds(0, halo)] = jnp.zeros((halo, channels), jnp.float32)

        stream = short_bias_v[j : j + 1] + taps_v[0, j : j + 1] * projected[j, pl.ds(halo, steps)]
        for k in range(1, taps.shape[0]):
            stream = stream + taps_v[k, j : j + 1] * projected[j, pl.ds(halo - k, steps)]
        stream = stream.astype(jnp.bfloat16).astype(jnp.float32)
        if j == 2:
            signal = (streams[0] * stream).astype(jnp.bfloat16).astype(jnp.float32)
            mixed_out[...] = signal.T.astype(jnp.bfloat16).reshape(tm_count, share, steps)
            spread(mixed_out, mixed_in, mix_send.at[0], mix_recv.at[0])
        streams.append(stream)
    gate_t[...] = streams[2].T.reshape(tm_count, share, steps)
    direct_t[...] = (skip_v[...] * signal).T.reshape(tm_count, share, steps)
    near = tm_count // 2
    for half in range(2):
        blocks = [
            out_weight_v[pl.ds(pl.multiple_of(c * channels + tm_peer(half * near + by) * share, share), share)]
            for c in range(chan_count)
            for by in range(near)
        ]
        out_weight_t[half] = jnp.concatenate(blocks, 0).astype(jnp.float32).T.astype(jnp.bfloat16)

    collect(mixed_in, mix_recv.at[0])
    blocks = [mixed_in[b].astype(jnp.float32) for b in range(tm_count)]
    turns = 2.0 * np.pi * np.arange(slots) / slots
    cosine = lambda r, b: math.cos(turns[r * b % slots])
    sine = lambda r, b: math.sin(turns[r * b % slots])
    kept = tm_count + 1

    for r in range(kept):
        real = weighted(blocks, [cosine(r, b) for b in range(tm_count)])
        imag = weighted(blocks, [-sine(r, b) for b in range(tm_count)])
        cos_row, sin_row = twist_v[0, r : r + 1], twist_v[1, r : r + 1]
        if imag is None:
            turned = (real * cos_row, -(real * sin_row))
        else:
            turned = (real * cos_row + imag * sin_row, imag * cos_row - real * sin_row)
        for part in range(2):
            wave[part, r] = turned[part].astype(jnp.bfloat16)

    def within():
        rows = wave[...].reshape(2 * kept * share, steps)
        first = jnp.dot(rows, dft_v[0], preferred_element_type=jnp.float32)
        second = jnp.dot(rows, dft_v[1], preferred_element_type=jnp.float32)
        half = kept * share
        return [a.reshape(kept, share, steps) for a in (first[:half], first[half:], second[:half], second[half:])]

    real_cos, imag_cos, real_sin, imag_sin = within()
    real, imag = real_cos + imag_sin, imag_cos - real_sin
    for parity in range(2):
        collect(spec_in.at[parity], spec_recv.at[parity])

    def filter_of(part, r):
        return spec_in[r % 2, flip(r // 2, digits), part].astype(jnp.float32)

    for r in range(kept):
        filter_real, filter_imag = filter_of(0, r), filter_of(1, r)
        if 0 < r < tm_count:
            filter_real = filter_real + filter_of(0, slots - r)
            filter_imag = filter_imag - filter_of(1, slots - r)
        wave[0, r] = (real[r] * filter_real - imag[r] * filter_imag).astype(jnp.bfloat16)
        wave[1, r] = (real[r] * filter_imag + imag[r] * filter_real).astype(jnp.bfloat16)
    real_cos, imag_cos, real_sin, imag_sin = within()
    real, imag = real_cos - imag_sin, real_sin + imag_cos

    terms = []
    for r in range(kept):
        cos_row, sin_row = twist_v[0, r : r + 1], twist_v[1, r : r + 1]
        terms.append(real[r] * cos_row - imag[r] * sin_row)
    for r in range(kept):
        cos_row, sin_row = twist_v[0, r : r + 1], twist_v[1, r : r + 1]
        terms.append(real[r] * sin_row + imag[r] * cos_row)
    for b in range(tm_count):
        weights = [cosine(r, b) for r in range(kept)] + [-sine(r, b) for r in range(kept)]
        conv_out[b] = weighted(terms, weights).astype(jnp.bfloat16)
    for by in far_first:
        half = by // near
        remote(
            conv_out.at[tm_peer(by)], conv_in.at[by], conv_send.at[0], conv_recv.at[half], {"tm": tm_peer(by)}
        ).start()

    bytes_of(rows_in.at[pl.ds(halo, steps), others], rows_send.at[0])

    @pl.when(own_t < tm_count - 1)
    def _():
        bytes_of(rows_in.at[pl.ds(0, halo)], halo_send.at[0])

    for parity in range(2):
        collect(spec_in.at[parity], spec_send.at[parity])
    bytes_of(mixed_in.at[pl.ds(0, tm_count - 1)], mix_send.at[0])

    def gate_copy(half, owner, recv, to):
        block = gated.at[half, owner]
        return remote(block, block, gate_send.at[half], gate_recv.at[half, recv], {"chan": to})

    for half in range(2):
        if half == 0:
            bytes_of(conv_in.at[pl.ds(0, near - 1)], conv_recv.at[0])
        else:
            bytes_of(conv_in.at[pl.ds(0, near)], conv_recv.at[1])
        for by in range(half * near, (half + 1) * near):
            source = tm_peer(by)
            arrived = conv_in[by] if by else conv_out[source]
            value = (arrived.astype(jnp.float32) + direct_t[source]) * gate_t[source]
            gated[half, own_c, pl.ds(by % near * share, share)] = value.astype(jnp.bfloat16)
        gate_copy(half, own_c, 0, x_c).start()
        if half:
            gate_copy(half, own_c, 2, far_c).start()
        gate_copy(half, own_c, 1, core_c).start()

    bytes_of(gated.at[0, x_c], gate_recv.at[0, 0])
    gate_copy(0, x_c, 2, core_c).start()

    total = None
    for half in range(2):
        bytes_of(gated.at[half, core_c], gate_recv.at[half, 1])
        if half:
            bytes_of(gated.at[half, x_c], gate_recv.at[half, 0])
        bytes_of(gated.at[half, far_c], gate_recv.at[half, 2])
        rows = gated[half].reshape(chan_count * channels // 2, steps)
        term = jnp.dot(out_weight_t[half], rows, preferred_element_type=jnp.float32)
        total = term if total is None else total + term
    out[...] = (total.T + out_bias_v[...]).astype(out.dtype)

    bytes_of(conv_in.at[pl.ds(0, tm_count - 1)], conv_send.at[0])
    for half in range(2):
        bytes_of(gated.at[half, pl.ds(0, chan_count - 1)], gate_send.at[half])


def fused(
    series,
    proj_weight,
    proj_bias,
    short_taps,
    short_bias,
    spectrum,
    skip_gain,
    out_weight,
    out_bias,
):
    steps, channels = series.shape
    width = proj_weight.shape[0]
    tm_count, chan_count = lax.axis_size("tm"), lax.axis_size("chan")
    dft, twist = make_tables(tm_count, steps)
    share, slots, halo = channels // tm_count, 2 * tm_count, 16
    spread_shape = (tm_count, share, steps)
    vmem, dma = pltpu.VMEM, pltpu.SemaphoreType.DMA
    operands = [
        series,
        proj_weight.transpose(1, 0, 2),
        proj_bias,
        short_taps,
        short_bias,
        spectrum,
        skip_gain.reshape(1, channels),
        out_weight,
        out_bias.reshape(1, channels),
        jnp.asarray(dft),
        jnp.asarray(twist),
    ]
    return pl.pallas_call(
        functools.partial(kernel, tm_count, chan_count),
        out_shape=jax.ShapeDtypeStruct((steps, channels), jnp.bfloat16),
        in_specs=[pl.BlockSpec(memory_space=pl.ANY)] * len(operands),
        out_specs=pl.BlockSpec(memory_space=pltpu.VMEM),
        scratch_shapes=[
            vmem((halo + steps, width), jnp.bfloat16),
            vmem((width, 3 * channels), jnp.bfloat16),
            vmem(proj_bias.shape, jnp.float32),
            vmem(short_taps.shape, jnp.float32),
            vmem(short_bias.shape, jnp.float32),
            vmem((2, 2, steps, channels), jnp.float32),
            vmem((1, channels), jnp.float32),
            vmem((width, channels), jnp.bfloat16),
            vmem((2, channels, width // 2), jnp.bfloat16),
            vmem((1, channels), jnp.float32),
            vmem(dft.shape, jnp.bfloat16),
            vmem(twist.shape, jnp.float32),
            vmem((3, halo + steps, channels), jnp.float32),
            vmem((2, tm_count, 2, share, steps), jnp.bfloat16),
            vmem((2, tm_count, 2, share, steps), jnp.bfloat16),
            vmem(spread_shape, jnp.bfloat16),
            vmem(spread_shape, jnp.bfloat16),
            vmem((2, tm_count + 1, share, steps), jnp.bfloat16),
            vmem(spread_shape, jnp.bfloat16),
            vmem(spread_shape, jnp.bfloat16),
            vmem(spread_shape, jnp.float32),
            vmem(spread_shape, jnp.float32),
            vmem((2, chan_count, channels // 2, steps), jnp.bfloat16),
            dma((len(operands) + 2,)),
            dma((1,)),
            dma((5,)),
            *[dma((2,))] * 9,
            dma((2, 3)),
        ],
        compiler_params=pltpu.CompilerParams(
            collective_id=0, has_side_effects=True, vmem_limit_bytes=32 * 1024 * 1024
        ),
    )(*[pltpu.with_memory_space_constraint(operand, pltpu.HBM) for operand in operands])


def solution(mesh):
    sizes = mesh.shape

    def program(*arrays):
        share = arrays[0].shape[1] // sizes["chan"] // sizes["tm"]
        wide = share > 0 and share % 16 == 0 and sizes["tm"] >= 4 and sizes["chan"] == 4
        wide = wide and sizes["tm"] & sizes["tm"] - 1 == 0
        return jax.shard_map(
            fused if wide else shards,
            mesh=mesh,
            in_specs=(
                P("tm", "chan"),
                P(None, None, "chan"),
                P(None, "chan"),
                P(None, None, "chan"),
                P(None, "chan"),
                P(None, "tm", None, None, "chan"),
                P("chan"),
                P(),
                P("chan"),
            ),
            out_specs=P("tm", "chan"),
            check_vma=False,
        )(*arrays)

    return program
```

```python
import functools
import math

import jax
import jax.numpy as jnp
import numpy as np
from jax import lax
from jax.experimental import pallas as pl
from jax.experimental.pallas import tpu as pltpu
from jax.sharding import PartitionSpec as P

MESH = pl.DeviceIdType.MESH


def from_behind(array, axis, by):
    length = lax.axis_size(axis)
    pairs = [(i, i + by) for i in range(length) if 0 <= i + by < length]
    return lax.ppermute(array, axis, pairs)


def partner_2(block, axis, bit):
    count = lax.axis_size(axis)
    route = []
    for low in range(count):
        high = low | 1 << bit
        if high != low and high < count:
            route += [(low, high), (high, low)]
    return lax.ppermute(block, axis, route)


def reverse_bits(values, digits):
    result = jnp.zeros_like(values)
    for bit_level in range(digits):
        result = result | (values >> bit_level & 1) << digits - 1 - bit_level
    return result


def turning(numer, denom):
    angle = numer.astype(jnp.float32) * (-2.0 * math.pi / denom)
    return (jnp.cos(angle), jnp.sin(angle))


def complex_times(stacked, real_part, imag_part):
    return jnp.stack(
        [
            stacked[0] * real_part - stacked[1] * imag_part,
            stacked[0] * imag_part + stacked[1] * real_part,
        ]
    )


def dft_rows(signals, period, inverse):
    indices = jnp.arange(period, dtype=jnp.int32)
    cosine, sine_part = turning(indices[:, None] * indices[None, :] % period, period)
    if inverse:
        sine_part = -sine_part
    stacked = jnp.concatenate([cosine, sine_part], 0)
    result = jnp.einsum("bt,retc->rebc", stacked, signals, precision=lax.Precision.HIGHEST)
    real_out = result[0, :, :period] - result[1, :, period:]
    imag_out = result[1, :, :period] + result[0, :, period:]
    return jnp.stack([real_out, imag_out])


def shards(
    series,
    proj_weight,
    proj_bias,
    short_taps,
    short_bias,
    spectrum,
    skip_gain,
    out_weight,
    out_bias,
):
    steps_dev = series.shape[0]
    model_width = proj_weight.shape[0]
    channels = proj_weight.shape[2]
    flat_weight = proj_weight.reshape(model_width, 3 * channels)
    weight_rows = flat_weight
    projected = jnp.dot(
        lax.all_gather(series, "chan", axis=1, tiled=True),
        weight_rows,
        preferred_element_type=jnp.float32,
    )
    projected = (projected.reshape(steps_dev, 3, channels) + proj_bias).astype(jnp.bfloat16)
    taps_count = short_taps.shape[0]
    earlier = from_behind(projected[steps_dev - taps_count + 1 :], "tm", 1)
    extended = jnp.concatenate([earlier, projected], 0).astype(jnp.float32)
    streams = short_bias + short_taps[0] * extended[taps_count - 1 :]
    for offset in range(1, taps_count):
        streams = (
            streams
            + short_taps[offset]
            * extended[taps_count - 1 - offset : taps_count - 1 - offset + steps_dev]
        )
    streams = lax.optimization_barrier(streams.astype(jnp.bfloat16)).astype(jnp.float32)
    gate_out = streams[:, 0]
    mixed_in = lax.optimization_barrier((streams[:, 1] * streams[:, 2]).astype(jnp.bfloat16))
    signal = mixed_in.astype(jnp.float32)
    tm_count = lax.axis_size("tm")
    digits = tm_count.bit_length() - 1
    own_index = lax.axis_index("tm")
    period = 2 * tm_count * steps_dev
    positions = jnp.arange(steps_dev, dtype=jnp.int32)
    own_rows = 2 * reverse_bits(own_index, digits) + jnp.arange(2, dtype=jnp.int32)
    twist_cos, twist_sin = turning(own_rows[:, None] * positions[None, :] % period, period)
    twist_cos, twist_sin = (twist_cos[:, :, None], twist_sin[:, :, None])
    half_cos, half_sin = turning(own_index, 2 * tm_count)
    zero_field = jnp.zeros_like(signal)
    current = jnp.stack(
        [jnp.stack([signal, signal * half_cos]), jnp.stack([zero_field, signal * half_sin])]
    )
    for bit_level in reversed(range(digits)):
        partner = partner_2(current, "tm", bit_level)
        half_span = 1 << bit_level
        rot_cos, rot_sin = turning(own_index % half_span, 2 * half_span)
        upper_half = own_index >> bit_level & 1 == 1
        current = jnp.where(
            upper_half, complex_times(partner - current, rot_cos, rot_sin), current + partner
        )
    twisted = complex_times(current, twist_cos, twist_sin)
    spectral = dft_rows(twisted, steps_dev, False)
    response = spectrum.reshape(2, 2, steps_dev, channels)
    product = complex_times(spectral, response[0], response[1])
    returned = dft_rows(product, steps_dev, True)
    current = complex_times(returned, twist_cos, -twist_sin)
    for bit_level in range(digits):
        partner = partner_2(current, "tm", bit_level)
        half_span = 1 << bit_level
        rot_cos, rot_sin = turning(own_index % half_span, 2 * half_span)
        rot_sin = -rot_sin
        upper_half = own_index >> bit_level & 1 == 1
        current = jnp.where(
            upper_half,
            partner - complex_times(current, rot_cos, rot_sin),
            current + complex_times(partner, rot_cos, rot_sin),
        )
    convolved = current[0, 0] + half_cos * current[0, 1] + half_sin * current[1, 1]
    convolved = convolved * (1.0 / period)
    gated_rows = ((convolved + skip_gain * signal) * gate_out).astype(jnp.bfloat16)
    column_start = lax.axis_index("chan") * channels
    weight_rows = lax.dynamic_slice_in_dim(out_weight, column_start, channels, 0)
    partial_value = jnp.dot(gated_rows, weight_rows, preferred_element_type=jnp.float32)
    mixed_out = lax.psum_scatter(partial_value, "chan", scatter_dimension=1, tiled=True)
    return (mixed_out + out_bias).astype(jnp.bfloat16)


def make_tables(tm_count, steps):
    count, period = 2 * tm_count, 2 * tm_count * steps
    rows = np.arange(steps)
    angle = 2.0 * np.pi * (rows[:, None] * rows[None, :] % steps) / steps
    dft = np.stack([np.cos(angle), np.sin(angle)]).astype(jnp.bfloat16)
    angle = 2.0 * np.pi * (np.arange(count)[:, None] * rows[None, :] % period) / period
    twist = np.stack([np.cos(angle), np.sin(angle)]).astype(np.float32)
    return dft, twist


def flip(value, digits):
    result = 0
    for bit_level in range(digits):
        result |= (value >> bit_level & 1) << digits - 1 - bit_level
    return result


def across_bits(index, by):
    result, bit = index, 1
    while bit <= by:
        if by & bit:
            result = result + bit * (1 - 2 * lax.rem(lax.div(index, bit), 2))
        bit *= 2
    return result


def weighted(blocks, weights):
    total = None
    for block, weight in zip(blocks, weights):
        if abs(weight) < 1e-12:
            continue
        if abs(weight - 1.0) < 1e-12:
            term = block
        elif abs(weight + 1.0) < 1e-12:
            term = -block
        else:
            term = block * float(weight)
        total = term if total is None else total + term
    return total


def kernel(
    tm_count,
    chan_count,
    series,
    weight,
    proj_bias,
    taps,
    short_bias,
    spectrum,
    skip_gain,
    out_weight,
    out_bias,
    dft,
    twist,
    out,
    rows_in,
    weight_v,
    proj_bias_v,
    taps_v,
    short_bias_v,
    spectrum_v,
    skip_v,
    out_weight_v,
    out_weight_t,
    out_bias_v,
    dft_v,
    twist_v,
    projected,
    spec_out,
    spec_in,
    mixed_out,
    mixed_in,
    wave,
    conv_out,
    conv_in,
    gate_t,
    direct_t,
    gated,
    local_sem,
    rows_send,
    rows_recv,
    halo_send,
    halo_recv,
    spec_send,
    spec_recv,
    mix_send,
    mix_recv,
    conv_send,
    conv_recv,
    gate_send,
    gate_recv,
):
    steps, channels = series.shape
    halo = rows_in.shape[0] - steps
    share = channels // tm_count
    digits = tm_count.bit_length() - 1
    slots = 2 * tm_count
    own_t, own_c = lax.axis_index("tm"), lax.axis_index("chan")
    columns = lambda c: pl.ds(pl.multiple_of(c * channels, channels), channels)
    next_t, last_t = lax.rem(own_t + 1, tm_count), lax.rem(own_t + tm_count - 1, tm_count)
    tm_peer = lambda by: across_bits(own_t, by)
    chan_peer = lambda by: across_bits(own_c, by)
    far_first = list(range(tm_count // 2, tm_count)) + list(range(1, tm_count // 2))

    barrier = pltpu.get_barrier_semaphore()
    greet = lambda where: pl.semaphore_signal(barrier, inc=1, device_id=where, device_id_type=MESH)
    for by in range(1, chan_count):
        greet({"chan": chan_peer(by)})
    for by in range(1, tm_count):
        greet({"tm": tm_peer(by)})
    for by in range(1, chan_count):
        greet({"tm": next_t, "chan": chan_peer(by)})
        greet({"tm": last_t, "chan": chan_peer(by)})

    pairs = [
        (series, rows_in.at[pl.ds(halo, steps), columns(own_c)]),
        (spectrum.at[:, 0], spectrum_v),
        *[(weight.at[j], weight_v.at[:, pl.ds((j + 2) % 3 * channels, channels)]) for j in range(3)],
        (proj_bias, proj_bias_v),
        (taps, taps_v),
        (short_bias, short_bias_v),
        (dft, dft_v),
        (twist, twist_v),
        (skip_gain, skip_v),
        (out_weight.at[:, columns(own_c)], out_weight_v),
        (out_bias, out_bias_v),
    ]
    local = [pltpu.make_async_copy(a, b, local_sem.at[i]) for i, (a, b) in enumerate(pairs)]
    local[1].start()

    def remote(src, dst, send, recv, where):
        return pltpu.make_async_remote_copy(
            src_ref=src, dst_ref=dst, send_sem=send, recv_sem=recv, device_id=where, device_id_type=MESH
        )

    residue = 2 * sum((own_t >> i & 1) << digits - 1 - i for i in range(digits))
    down = lax.broadcasted_iota(jnp.int32, (steps, steps), 0)
    across = lax.broadcasted_iota(jnp.int32, (steps, steps), 1)

    def turn_spectrum(parity):
        wanted = jnp.where(residue + parity > tm_count, steps - 1 - down, down)
        order = jnp.where(wanted == across, 1.0 / (slots * steps), 0.0).astype(jnp.bfloat16)
        for part in range(2):
            block = spectrum_v[part, parity].astype(jnp.bfloat16)
            block = jnp.dot(order, block, preferred_element_type=jnp.float32).T
            spec_out[parity, :, part] = block.astype(jnp.bfloat16).reshape(tm_count, share, steps)

    early = own_t < tm_count // 2

    @pl.when(early)
    def _():
        local[1].wait()
        turn_spectrum(0)
        turn_spectrum(1)

    pl.semaphore_wait(barrier, chan_count - 1 + tm_count - 1 + 2 * (chan_count - 1))

    core_c, x_c, far_c = chan_peer(1), chan_peer(2), chan_peer(3)
    part_rows = steps // 2

    def rows_copy(owner, first, count, recv, to):
        block = rows_in.at[pl.ds(halo + first, count), columns(owner)]
        source = series.at[pl.ds(first, count)] if owner is own_c else block
        return remote(source, block, rows_send.at[0], rows_recv.at[recv], {"chan": to})

    def halo_copy(by, owner):
        return remote(
            series.at[pl.ds(steps - halo, halo)],
            rows_in.at[pl.ds(0, halo), columns(owner)],
            halo_send.at[0],
            halo_recv.at[0],
            {"tm": next_t, "chan": chan_peer(by)},
        )

    for i in range(2):
        rows_copy(own_c, i * part_rows, part_rows, i, x_c).start()
    rows_copy(own_c, part_rows, part_rows, 3, far_c).start()
    rows_copy(own_c, 0, steps, 2, core_c).start()

    @pl.when(own_t < tm_count - 1)
    def _():
        for by in range(chan_count):
            halo_copy(by, own_c).start()

    @pl.when(own_t == 0)
    def _():
        rows_in[pl.ds(0, halo), :] = jnp.zeros((halo, rows_in.shape[1]), rows_in.dtype)

    def bytes_of(ref, sem):
        pltpu.make_async_copy(ref, ref, sem).wait()

    def spread(src, dst, send, recv):
        for by in far_first:
            remote(src.at[tm_peer(by)], dst.at[own_t], send, recv, {"tm": tm_peer(by)}).start()
        dst[own_t] = src[own_t]

    def collect(dst, recv):
        bytes_of(dst.at[pl.ds(0, tm_count - 1)], recv)

    for copy in local[:1] + local[2:]:
        copy.start()

    def relay_rows():
        bytes_of(rows_in.at[pl.ds(halo, part_rows), columns(x_c)], rows_recv.at[0])
        rows_copy(x_c, 0, part_rows, 4, core_c).start()

    def spread_spectrum(parity):
        spread(spec_out.at[parity], spec_in.at[parity], spec_send.at[parity], spec_recv.at[parity])

    @pl.when(early)
    def _():
        spread_spectrum(0)
        spread_spectrum(1)
        relay_rows()

    @pl.when(jnp.logical_not(early))
    def _():
        local[1].wait()
        for parity in range(2):
            turn_spectrum(parity)
            spread_spectrum(parity)
        relay_rows()

    local[0].wait()
    for copy in local[2:]:
        copy.wait()
    others = pl.ds(0, (chan_count - 1) * channels)

    @pl.when(own_t > 0)
    def _():
        bytes_of(rows_in.at[pl.ds(0, halo)], halo_recv.at[0])

    bytes_of(rows_in.at[pl.ds(halo, steps), columns(core_c)], rows_recv.at[2])

    def of_chip(chip):
        inputs = pl.ds(pl.multiple_of(chip * 2 * channels, 2 * channels), 2 * channels)
        return jnp.dot(
            rows_in[:, inputs], weight_v[inputs, pl.ds(0, 2 * channels)], preferred_element_type=jnp.float32
        )

    own_chip = lax.div(own_c, 2)
    near_sum = of_chip(own_chip)
    bytes_of(rows_in.at[pl.ds(halo, part_rows), columns(x_c)], rows_recv.at[1])
    for i in range(2):
        bytes_of(rows_in.at[pl.ds(halo, part_rows), columns(far_c)], rows_recv.at[3 + i])
    sums = near_sum + of_chip(1 - own_chip)

    streams = []
    for j in (1, 2, 0):
        if j:
            value = sums[:, (j - 1) * channels : j * channels]
        else:
            value = jnp.dot(
                rows_in[...], weight_v[:, pl.ds(2 * channels, channels)], preferred_element_type=jnp.float32
            )
        value = (value + proj_bias_v[j : j + 1]).astype(jnp.bfloat16).astype(jnp.float32)
        projected[j] = value

        @pl.when(own_t == 0)
        def _():
            projected[j, pl.ds(0, halo)] = jnp.zeros((halo, channels), jnp.float32)

        stream = short_bias_v[j : j + 1] + taps_v[0, j : j + 1] * projected[j, pl.ds(halo, steps)]
        for k in range(1, taps.shape[0]):
            stream = stream + taps_v[k, j : j + 1] * projected[j, pl.ds(halo - k, steps)]
        stream = stream.astype(jnp.bfloat16).astype(jnp.float32)
        if j == 2:
            signal = (streams[0] * stream).astype(jnp.bfloat16).astype(jnp.float32)
            mixed_out[...] = signal.T.astype(jnp.bfloat16).reshape(tm_count, share, steps)
            spread(mixed_out, mixed_in, mix_send.at[0], mix_recv.at[0])
        streams.append(stream)
    gate_t[...] = streams[2].T.reshape(tm_count, share, steps)
    direct_t[...] = (skip_v[...] * signal).T.reshape(tm_count, share, steps)
    near = tm_count // 2
    for half in range(2):
        blocks = [
            out_weight_v[pl.ds(pl.multiple_of(c * channels + tm_peer(half * near + by) * share, share), share)]
            for c in range(chan_count)
            for by in range(near)
        ]
        out_weight_t[half] = jnp.concatenate(blocks, 0).astype(jnp.float32).T.astype(jnp.bfloat16)

    collect(mixed_in, mix_recv.at[0])
    blocks = [mixed_in[b].astype(jnp.float32) for b in range(tm_count)]
    turns = 2.0 * np.pi * np.arange(slots) / slots
    cosine = lambda r, b: math.cos(turns[r * b % slots])
    sine = lambda r, b: math.sin(turns[r * b % slots])
    kept = tm_count + 1

    for r in range(kept):
        real = weighted(blocks, [cosine(r, b) for b in range(tm_count)])
        imag = weighted(blocks, [-sine(r, b) for b in range(tm_count)])
        cos_row, sin_row = twist_v[0, r : r + 1], twist_v[1, r : r + 1]
        if imag is None:
            turned = (real * cos_row, -(real * sin_row))
        else:
            turned = (real * cos_row + imag * sin_row, imag * cos_row - real * sin_row)
        for part in range(2):
            wave[part, r] = turned[part].astype(jnp.bfloat16)

    def within():
        rows = wave[...].reshape(2 * kept * share, steps)
        first = jnp.dot(rows, dft_v[0], preferred_element_type=jnp.float32)
        second = jnp.dot(rows, dft_v[1], preferred_element_type=jnp.float32)
        half = kept * share
        return [a.reshape(kept, share, steps) for a in (first[:half], first[half:], second[:half], second[half:])]

    real_cos, imag_cos, real_sin, imag_sin = within()
    real, imag = real_cos + imag_sin, imag_cos - real_sin
    for parity in range(2):
        collect(spec_in.at[parity], spec_recv.at[parity])

    def filter_of(part, r):
        return spec_in[r % 2, flip(r // 2, digits), part].astype(jnp.float32)

    for r in range(kept):
        filter_real, filter_imag = filter_of(0, r), filter_of(1, r)
        if 0 < r < tm_count:
            filter_real = filter_real + filter_of(0, slots - r)
            filter_imag = filter_imag - filter_of(1, slots - r)
        wave[0, r] = (real[r] * filter_real - imag[r] * filter_imag).astype(jnp.bfloat16)
        wave[1, r] = (real[r] * filter_imag + imag[r] * filter_real).astype(jnp.bfloat16)
    real_cos, imag_cos, real_sin, imag_sin = within()
    real, imag = real_cos - imag_sin, real_sin + imag_cos

    terms = []
    for r in range(kept):
        cos_row, sin_row = twist_v[0, r : r + 1], twist_v[1, r : r + 1]
        terms.append(real[r] * cos_row - imag[r] * sin_row)
    for r in range(kept):
        cos_row, sin_row = twist_v[0, r : r + 1], twist_v[1, r : r + 1]
        terms.append(real[r] * sin_row + imag[r] * cos_row)
    for b in range(tm_count):
        weights = [cosine(r, b) for r in range(kept)] + [-sine(r, b) for r in range(kept)]
        conv_out[b] = weighted(terms, weights).astype(jnp.bfloat16)
    for by in far_first:
        half = by // near
        remote(
            conv_out.at[tm_peer(by)], conv_in.at[by], conv_send.at[0], conv_recv.at[half], {"tm": tm_peer(by)}
        ).start()

    bytes_of(rows_in.at[pl.ds(halo, steps), others], rows_send.at[0])

    @pl.when(own_t < tm_count - 1)
    def _():
        bytes_of(rows_in.at[pl.ds(0, halo)], halo_send.at[0])

    for parity in range(2):
        collect(spec_in.at[parity], spec_send.at[parity])
    bytes_of(mixed_in.at[pl.ds(0, tm_count - 1)], mix_send.at[0])

    def gate_copy(half, owner, recv, to):
        block = gated.at[half, owner]
        return remote(block, block, gate_send.at[half], gate_recv.at[half, recv], {"chan": to})

    for half in range(2):
        if half == 0:
            bytes_of(conv_in.at[pl.ds(0, near - 1)], conv_recv.at[0])
        else:
            bytes_of(conv_in.at[pl.ds(0, near)], conv_recv.at[1])
        for by in range(half * near, (half + 1) * near):
            source = tm_peer(by)
            arrived = conv_in[by] if by else conv_out[source]
            value = (arrived.astype(jnp.float32) + direct_t[source]) * gate_t[source]
            gated[half, own_c, pl.ds(by % near * share, share)] = value.astype(jnp.bfloat16)
        gate_copy(half, own_c, 0, x_c).start()
        gate_copy(half, own_c, 2, far_c).start()
        gate_copy(half, own_c, 1, core_c).start()


    total = None
    for half in range(2):
        bytes_of(gated.at[half, core_c], gate_recv.at[half, 1])
        bytes_of(gated.at[half, x_c], gate_recv.at[half, 0])
        bytes_of(gated.at[half, far_c], gate_recv.at[half, 2])
        rows = gated[half].reshape(chan_count * channels // 2, steps)
        term = jnp.dot(out_weight_t[half], rows, preferred_element_type=jnp.float32)
        total = term if total is None else total + term
    out[...] = (total.T + out_bias_v[...]).astype(out.dtype)

    bytes_of(conv_in.at[pl.ds(0, tm_count - 1)], conv_send.at[0])
    for half in range(2):
        bytes_of(gated.at[half, pl.ds(0, chan_count - 1)], gate_send.at[half])


def fused(
    series,
    proj_weight,
    proj_bias,
    short_taps,
    short_bias,
    spectrum,
    skip_gain,
    out_weight,
    out_bias,
):
    steps, channels = series.shape
    width = proj_weight.shape[0]
    tm_count, chan_count = lax.axis_size("tm"), lax.axis_size("chan")
    dft, twist = make_tables(tm_count, steps)
    share, slots, halo = channels // tm_count, 2 * tm_count, 16
    spread_shape = (tm_count, share, steps)
    vmem, dma = pltpu.VMEM, pltpu.SemaphoreType.DMA
    operands = [
        series,
        proj_weight.transpose(1, 0, 2),
        proj_bias,
        short_taps,
        short_bias,
        spectrum,
        skip_gain.reshape(1, channels),
        out_weight,
        out_bias.reshape(1, channels),
        jnp.asarray(dft),
        jnp.asarray(twist),
    ]
    return pl.pallas_call(
        functools.partial(kernel, tm_count, chan_count),
        out_shape=jax.ShapeDtypeStruct((steps, channels), jnp.bfloat16),
        in_specs=[pl.BlockSpec(memory_space=pl.ANY)] * len(operands),
        out_specs=pl.BlockSpec(memory_space=pltpu.VMEM),
        scratch_shapes=[
            vmem((halo + steps, width), jnp.bfloat16),
            vmem((width, 3 * channels), jnp.bfloat16),
            vmem(proj_bias.shape, jnp.float32),
            vmem(short_taps.shape, jnp.float32),
            vmem(short_bias.shape, jnp.float32),
            vmem((2, 2, steps, channels), jnp.float32),
            vmem((1, channels), jnp.float32),
            vmem((width, channels), jnp.bfloat16),
            vmem((2, channels, width // 2), jnp.bfloat16),
            vmem((1, channels), jnp.float32),
            vmem(dft.shape, jnp.bfloat16),
            vmem(twist.shape, jnp.float32),
            vmem((3, halo + steps, channels), jnp.float32),
            vmem((2, tm_count, 2, share, steps), jnp.bfloat16),
            vmem((2, tm_count, 2, share, steps), jnp.bfloat16),
            vmem(spread_shape, jnp.bfloat16),
            vmem(spread_shape, jnp.bfloat16),
            vmem((2, tm_count + 1, share, steps), jnp.bfloat16),
            vmem(spread_shape, jnp.bfloat16),
            vmem(spread_shape, jnp.bfloat16),
            vmem(spread_shape, jnp.float32),
            vmem(spread_shape, jnp.float32),
            vmem((2, chan_count, channels // 2, steps), jnp.bfloat16),
            dma((len(operands) + 2,)),
            dma((1,)),
            dma((5,)),
            *[dma((2,))] * 9,
            dma((2, 3)),
        ],
        compiler_params=pltpu.CompilerParams(
            collective_id=0, has_side_effects=True, vmem_limit_bytes=32 * 1024 * 1024
        ),
    )(*[pltpu.with_memory_space_constraint(operand, pltpu.HBM) for operand in operands])


def solution(mesh):
    sizes = mesh.shape

    def program(*arrays):
        share = arrays[0].shape[1] // sizes["chan"] // sizes["tm"]
        wide = share > 0 and share % 16 == 0 and sizes["tm"] >= 4 and sizes["chan"] == 4
        wide = wide and sizes["tm"] & sizes["tm"] - 1 == 0
        return jax.shard_map(
            fused if wide else shards,
            mesh=mesh,
            in_specs=(
                P("tm", "chan"),
                P(None, None, "chan"),
                P(None, "chan"),
                P(None, None, "chan"),
                P(None, "chan"),
                P(None, "tm", None, None, "chan"),
                P("chan"),
                P(),
                P("chan"),
            ),
            out_specs=P("tm", "chan"),
            check_vma=False,
        )(*arrays)

    return program
```
